256 devices in a mesh: member: 8 (over y, z_hi), space: 32 (over z_lo, x, core).
Axes of the slice: x: 4, y: 4, z: 8 (z_hi: 2, z_lo: 4; z = z_hi * 4 + z_lo), core: 2. Of those that a mesh axis runs over, the one named last changes fastest.
Arguments:
- hidden_state: bfloat16 [8, 128, 512, 1024], P('member', 'space'), may hold values from -6 to 6
- proj_weight: bfloat16 [100, 1024], replicated, may hold values from -0.1875 to 0.1875
- output_offset_vector: float32 [100], replicated, may hold values from -3 to 3
- verifying_reanalysis: float32 [100, 128, 512], P(None, 'space'), may hold values from -6 to 6
- counts: int32 [128], P('space'), may hold values from 128 to 512, as said below
- var_weight: float32 [100], replicated, may hold values from 0.25 to 4
Outputs:
- latent_grad: bfloat16 [8, 128, 512, 1024], P('member', 'space')
- weight_grad: float32 [100, 1024], replicated
- bias_grad: float32 [100], replicated
- loss: float32 [], replicated
The draws below stay inside these ranges and needn't reach their ends.
Inputs may be any that keep to these rules, and one draw needn't show every extreme that they name: `counts`: row 0 has all 512 slots live; lengths decrease on average with the row index, with random variation from row to row.
All inputs are finite; a program needn't handle non-finite values.
Results may differ from the reference program's by a relative error of at most 0.0049.
Values sent between devices are 32-bit elements; how exact they have to be, the bound alone decides.
A program may use at most 64 MiB of HBM per device.

```python
import math
import jax
import jax.numpy as jnp
from jax import lax

D = 1024
V = 100
CAP = 512
NROWS = 128
MEMBERS = 8


def draw_counts(key, part):
    key = jax.random.fold_in(key, 1)
    row_index = jnp.arange(NROWS, dtype=jnp.int32)
    jitter = jax.random.randint(key, (NROWS,), 0, CAP // 8, dtype=jnp.int32)
    lengths = CAP - row_index * (CAP // 2) // NROWS - jitter
    return jnp.where(row_index == 0, CAP, lengths).astype(jnp.int32)


def level_of(stream_key, dims, shards, low, top_value):
    def one(dim, parts):
        draws = jax.random.uniform(jax.random.fold_in(jax.random.fold_in(stream_key, 6), dim), (parts,), jnp.float32, low / len(shards), top_value / len(shards))
        return jnp.repeat(jnp.exp(draws), dims[dim] // parts).reshape((-1,) + (1,) * (len(dims) - dim - 1))

    gain = one(*shards[0])
    for cut in shards[1:]:
        gain = gain * one(*cut)
    return gain


def bell_draw(stream_key, extent, deviation, reach, split=(), kind=jnp.bfloat16):
    entries = deviation * jax.random.normal(stream_key, extent, jnp.float32)
    if split:
        entries = entries * level_of(stream_key, extent, split, -0.22, 0.18)
    return jnp.clip(entries, -reach, reach).astype(kind)


def setup_inputs(seed: int = 0) -> dict:
    arg_keys = jax.random.split(jax.random.key(seed), 7)
    return {
        "hidden_state": bell_draw(arg_keys[0], (MEMBERS, NROWS, CAP, D), 1.0, 6.0, ((0, 8), (1, 32))),
        "proj_weight": bell_draw(arg_keys[1], (V, D), D ** -0.5, 0.1875),
        "output_offset_vector": bell_draw(arg_keys[2], (V,), 0.5, 3.0, (), jnp.float32),
        "verifying_reanalysis": bell_draw(arg_keys[3], (V, NROWS, CAP), 1.0, 6.0, ((1, 32),), jnp.float32),
        "counts": draw_counts(jax.random.fold_in(arg_keys[6], 71), 0),
        "var_weight": jnp.clip(jnp.exp(jax.random.uniform(arg_keys[5], (V,), jnp.float32, math.log(0.25), math.log(4.0))), 0.25, 4.0),
    }


SMOOTHING = 0.05
FAIRNESS = 0.95
GRAD_SCALE = 16.0
LATITUDE_SPAN = 80.0

def smooth_abs(values):
    return jnp.sqrt(values * values + SMOOTHING * SMOOTHING) - SMOOTHING

def smooth_sign(values):
    return values / jnp.sqrt(values * values + SMOOTHING * SMOOTHING)

def reference(hidden_state, proj_weight, output_offset_vector, verifying_reanalysis, counts, var_weight):
    ensemble_members = MEMBERS
    row_index = jnp.arange(NROWS).astype(jnp.float32)
    latitude = (row_index + 0.5) * (LATITUDE_SPAN / NROWS) * (math.pi / 180.0)
    area_weight = jnp.cos(latitude)
    live_mask = (jnp.arange(CAP, dtype=jnp.int32)[None, :] < counts[:, None]).astype(jnp.float32)
    gridpoint_weight = area_weight[:, None] * live_mask

    def compute_outputs(member_latent):
        flat_latent = member_latent.reshape(NROWS * CAP, D)
        out = lax.dot_general(proj_weight, flat_latent, (((1,), (1,)), ((), ())), preferred_element_type=jnp.float32)
        return out.reshape(V, NROWS, CAP) + output_offset_vector[:, None, None]
    predicted_maps = lax.map(compute_outputs, hidden_state)

    def couple_contributions(own):

        def loop_iteration(carry, other):
            realization_gaps = own - other
            return ((carry[0] + smooth_sign(realization_gaps), carry[1] + smooth_abs(realization_gaps)), None)
        empty_tile = jnp.zeros(own.shape, jnp.float32)
        (polarity_totals, modulus_totals), discarded_carry = lax.scan(loop_iteration, (empty_tile, empty_tile), predicted_maps)
        return (polarity_totals, modulus_totals)
    polarity_totals, modulus_totals = lax.map(couple_contributions, predicted_maps)
    coeff = FAIRNESS / (ensemble_members * (ensemble_members - 1)) + (1.0 - FAIRNESS) / (ensemble_members * ensemble_members)
    variable_scale = var_weight[:, None, None]
    observation_misfit = predicted_maps - verifying_reanalysis[None]
    total = jnp.sum(gridpoint_weight * variable_scale * (smooth_abs(observation_misfit) / ensemble_members - 0.5 * coeff * modulus_totals))
    normalizer = V * jnp.sum(area_weight * counts.astype(jnp.float32))
    loss = total / normalizer
    field_grad = gridpoint_weight * variable_scale * (smooth_sign(observation_misfit) / ensemble_members - coeff * polarity_totals)
    grad_bf = field_grad.astype(jnp.bfloat16)
    factor = GRAD_SCALE / math.sqrt(ensemble_members * NROWS * CAP)

    def backward(pair):
        member_grad, member_latent = pair
        flat_grad = member_grad.reshape(V, NROWS * CAP)
        flat_latent = member_latent.reshape(NROWS * CAP, D)
        back = lax.dot_general(flat_grad, proj_weight, (((0,), (0,)), ((), ())), preferred_element_type=jnp.float32)
        back = (GRAD_SCALE * back).astype(jnp.bfloat16).reshape(NROWS, CAP, D)
        wpart = jnp.dot(flat_grad, flat_latent, preferred_element_type=jnp.float32)
        return (back, wpart)
    latent_grad, wparts = lax.map(backward, (grad_bf, hidden_state))
    weight_grad = lax.optimization_barrier(jnp.sum(wparts, axis=0)) * factor
    bias_grad = lax.optimization_barrier(jnp.sum(field_grad, axis=(0, 2, 3))) * factor
    return (latent_grad, weight_grad, bias_grad, loss)
```

```python
import math

import numpy as np

import jax
import jax.numpy as jnp
from jax import lax
from jax.experimental import pallas as pl
from jax.experimental.pallas import tpu as pltpu
from jax.sharding import PartitionSpec as P

SMOOTHING = 0.05
FAIRNESS = 0.95
GRAD_SCALE = 16.0
LATITUDE_SPAN = 80.0

V = 100
VP = 104
D = 1024
ROWS = 4
CAP = 512
POINTS = ROWS * CAP
BLOCK = 256
NB = 8
TILES = VP // 8
GP = 112
CHUNKS = ((0, 32), (32, 32), (64, 40))
SENT = (32, 32, 40)
GROUPS = ((0, 64), (64, 40))
NC = len(CHUNKS)
MESH = pl.DeviceIdType.MESH
F32 = jnp.float32
EPS2 = SMOOTHING * SMOOTHING
COEFF = FAIRNESS / (NB * (NB - 1)) + (1.0 - FAIRNESS) / (NB * NB)


def column(row):
    n = row.shape[1]
    here = lax.broadcasted_iota(jnp.int32, (VP, n), 0) == lax.broadcasted_iota(
        jnp.int32, (VP, n), 1
    )
    return jnp.sum(jnp.where(here, jnp.broadcast_to(row, (VP, n)), 0.0), axis=1, keepdims=True)


def exchange_kernel(
    counts_ref,
    area_ref,
    offset_ref,
    scale_ref,
    weight_hbm,
    hidden_hbm,
    truth_hbm,
    latent_ref,
    sums_ref,
    weight,
    hbuf,
    truth,
    field,
    met,
    signs,
    back,
    obs,
    grad,
    loss_acc,
    bias_acc,
    offset_col,
    scale_col,
    part,
    part_in,
    plane,
    y_in,
    z_out,
    z_in,
    own_all,
    out_in,
    load_sem,
    side_sem,
    fwd_send,
    fwd_recv,
    ret_send,
    ret_recv,
    part_send,
    part_recv,
    y_send,
    y_recv,
    z_send,
    z_recv,
    row_send,
    row_recv,
    out_send,
    out_recv,
):
    member = lax.axis_index("member")
    space = lax.axis_index("space")
    y, z_hi = lax.div(member, 2), lax.rem(member, 2)
    z_lo, q = lax.div(space, 8), lax.rem(space, 8)
    z = z_hi * 4 + z_lo

    def at(yy, zz):
        return (yy * 2 + lax.div(zz, 4), lax.rem(zz, 4) * 8 + q)

    def beside(j):
        return (member, z_lo * 8 + j)

    def load(t):
        b = lax.rem(member + t, NB)
        rows = pl.ds(pl.multiple_of(b * BLOCK, BLOCK), BLOCK)
        return pltpu.make_async_copy(hidden_hbm.at[rows], hbuf.at[rows], load_sem.at[t])

    load_weight = pltpu.make_async_copy(weight_hbm, weight, side_sem.at[0])
    load_weight.start()
    for t in range(NB):
        load(t).start()
    load_truth = pltpu.make_async_copy(truth_hbm, truth.at[pl.ds(0, V)], side_sem.at[1])
    load_truth.start()

    met[:, V:VP, :] = jnp.zeros((NB, VP - V, BLOCK), F32)
    back[:, V:VP, :] = jnp.zeros((NB, VP - V, BLOCK), F32)

    barrier = pltpu.get_barrier_semaphore()

    def greet(device):
        pl.semaphore_signal(barrier, inc=1, device_id=device, device_id_type=MESH)

    @pl.loop(1, 8)
    def _(t):
        greet(beside(lax.rem(q + t, 8)))
        greet(at(y, lax.rem(z + t, 8)))

    @pl.loop(1, ROWS)
    def _(t):
        for step in (0, 2, 6):
            greet(at(lax.rem(y + t, ROWS), lax.rem(z + step, 8)))

    offset_col[...] = jnp.broadcast_to(column(offset_ref[...]), (VP, 128))
    scale_col[...] = jnp.broadcast_to(column(scale_ref[...]), (VP, 128))
    loss_acc[...] = jnp.zeros_like(loss_acc)
    bias_acc[...] = jnp.zeros_like(bias_acc)
    field[:, V:VP, :] = jnp.zeros((NB, VP - V, BLOCK), F32)
    truth[V:VP] = jnp.zeros((VP - V, ROWS, CAP), F32)

    lanes = lax.broadcasted_iota(jnp.int32, (1, BLOCK), 1)

    def live(b):
        return lanes + lax.rem(b, 2) * BLOCK < counts_ref[lax.div(b, 2)]

    def send_forecast(c, b):
        v0, n = CHUNKS[c][0], SENT[c]
        zz = lax.rem(z_lo + 2 + 4 * lax.rem(b, 2), 8)
        return pltpu.make_async_remote_copy(
            src_ref=field.at[b, pl.ds(v0, n)],
            dst_ref=met.at[member, pl.ds(v0, n)],
            send_sem=fwd_send.at[c, b],
            recv_sem=fwd_recv.at[c],
            device_id=at(lax.div(b, 2), zz),
            device_id_type=MESH,
        )

    def send_forecasts(c):
        @pl.loop(0, NB)
        def _(t):
            send_forecast(c, lax.rem(member + t, NB)).start()

    @pl.loop(0, NB)
    def _(t):
        load(t).wait()

        @pl.when(t == 0)
        def _():
            load_weight.wait()

        b = lax.rem(member + t, NB)
        rows = pl.ds(pl.multiple_of(b * BLOCK, BLOCK), BLOCK)
        product = lax.dot_general(
            weight[...], hbuf[rows, :], (((1,), (1,)), ((), ())), preferred_element_type=F32
        )
        forecast = product + offset_col[0:V, 0:1]
        field[b, 0:V, :] = jnp.where(live(b), forecast, 0.0)

        @pl.when(t == 0)
        def _():
            pl.semaphore_wait(barrier, 23)

        send_forecast(0, b).start()

    for c in range(1, NC):
        send_forecasts(c)

    load_truth.wait()

    @pl.loop(0, TILES)
    def _(i):
        at_v = pl.ds(pl.multiple_of(i * 8, 8), 8)
        for b in range(NB):
            r, half = b // 2, b % 2
            point_weight = jnp.where(live(b), area_ref[space * ROWS + r], 0.0) * (1.0 / NB)
            factor = point_weight * scale_col[at_v, 0:1]
            gap = field[b, at_v, :] - truth[at_v, r, half * BLOCK : (half + 1) * BLOCK]
            square = gap * gap + EPS2
            inverse = lax.rsqrt(square)
            obs[b, at_v, :] = factor * (gap * inverse)
            misfit = factor * (square * inverse - SMOOTHING)
            loss_acc[at_v, :] += misfit[:, 0:128] + misfit[:, 128:256]

    z_from = lax.rem(z + 2, 4)
    block_here = y * 2 + lax.div(lax.rem(z - z_from - 2 + 16, 8), 4)
    space_from = z_from * 8 + q
    area_here = area_ref[space_from * ROWS + y]

    def send_sign(c, m):
        v0, n = CHUNKS[c][0], SENT[c]
        return pltpu.make_async_remote_copy(
            src_ref=signs.at[m, pl.ds(v0, n)],
            dst_ref=back.at[block_here, pl.ds(v0, n)],
            send_sem=ret_send.at[c, m],
            recv_sem=ret_recv.at[c],
            device_id=(m, space_from),
            device_id_type=MESH,
        )

    def pairs(c):
        v0, n = CHUNKS[c]
        arrived = met.at[:, pl.ds(v0, SENT[c])]
        pltpu.make_async_copy(arrived, arrived, fwd_recv.at[c]).wait()

        @pl.loop(0, n // 8)
        def _(i):
            at_v = pl.ds(pl.multiple_of(v0 + i * 8, 8), 8)
            values = [met[m, at_v, :] for m in range(NB)]
            sums = [None] * NB
            roots = None
            for m in range(NB):
                for k in range(m + 1, NB):
                    gap = values[m] - values[k]
                    square = gap * gap + EPS2
                    inverse = lax.rsqrt(square)
                    sign = gap * inverse
                    root = square * inverse
                    roots = root if roots is None else roots + root
                    sums[m] = sign if sums[m] is None else sums[m] + sign
                    sums[k] = -sign if sums[k] is None else sums[k] - sign
            for m in range(NB):
                signs[m, at_v, :] = sums[m]
            spread = roots - (NB * (NB - 1) // 2) * SMOOTHING
            spread = (-COEFF * area_here) * scale_col[at_v, 0:1] * spread
            loss_acc[at_v, :] += spread[:, 0:128] + spread[:, 128:256]

        @pl.loop(0, NB)
        def _(t):
            send_sign(c, lax.rem(member + t, NB)).start()

    lane = lax.broadcasted_iota(jnp.int32, (1, 128), 1)
    sub = lax.broadcasted_iota(jnp.int32, (8, 128), 0)

    def extras():
        bias = jnp.sum(bias_acc[...], axis=1, keepdims=True)
        eye = lax.broadcasted_iota(jnp.int32, (VP, 128), 0) == lax.broadcasted_iota(
            jnp.int32, (VP, 128), 1
        )
        extra = jnp.sum(jnp.where(eye, bias, 0.0), axis=0, keepdims=True)
        loss_here = jnp.sum(jnp.sum(loss_acc[...], axis=0, keepdims=True), axis=1, keepdims=True)
        points_here = jnp.float32(0.0)
        for r in range(ROWS):
            points_here += area_ref[space * ROWS + r] * counts_ref[r].astype(F32)
        extra = jnp.where(lane < V, extra, 0.0)
        extra = jnp.where(lane == V, loss_here, extra)
        extra = jnp.where(lane == V + 1, points_here, extra)
        part[0, 96:VP, :] = jnp.where(sub == V - 96, extra, part[0, 96:VP, :])

    def gradient(c):
        v0, n = CHUNKS[c]
        arrived = back.at[:, pl.ds(v0, SENT[c])]
        pltpu.make_async_copy(arrived, arrived, ret_recv.at[c]).wait()
        padded = (n + 15) // 16 * 16

        @pl.loop(0, NB)
        def _(b):
            points = pl.ds(pl.multiple_of(b * BLOCK, BLOCK), BLOCK)
            area = area_ref[space * ROWS + lax.div(b, 2)]
            point_weight = jnp.where(live(b), area * COEFF, 0.0)
            factor = point_weight * scale_col[v0 : v0 + n, 0:1]
            value = obs[b, v0 : v0 + n, :] - factor * back[b, v0 : v0 + n, :]
            bias_acc[v0 : v0 + n, :] += value[:, 0:128] + value[:, 128:256]
            if padded > n:
                value = jnp.concatenate([value, jnp.zeros((padded - n, BLOCK), F32)], axis=0)
            grad[v0 : v0 + padded, points] = value.astype(jnp.bfloat16)

        @pl.loop(0, 4)
        def _(j):
            piece = jnp.dot(
                grad[v0 : v0 + padded, :],
                hbuf[:, pl.ds(pl.multiple_of(j * 256, 256), 256)],
                preferred_element_type=F32,
            )
            part[2 * j, v0 : v0 + n, :] = piece[0:n, 0:128]
            part[2 * j + 1, v0 : v0 + n, :] = piece[0:n, 128:256]

    def tiles(g):
        first, n = GROUPS[g]
        return first // 8, (first + n) // 8

    def send_part(g, t):
        first, n = GROUPS[g]
        j = lax.rem(q + t, 8)
        return pltpu.make_async_remote_copy(
            src_ref=part.at[j, pl.ds(first, n)],
            dst_ref=part_in.at[t - 1, pl.ds(first, n)],
            send_sem=part_send.at[g, t - 1],
            recv_sem=part_recv.at[g],
            device_id=beside(j),
            device_id_type=MESH,
        )

    def send_plane(g, t):
        yy = lax.rem(y + t, ROWS)
        return pltpu.make_async_remote_copy(
            src_ref=plane.at[g, yy],
            dst_ref=y_in.at[g, y],
            send_sem=y_send.at[g, t - 1],
            recv_sem=y_recv.at[g],
            device_id=at(yy, z),
            device_id_type=MESH,
        )

    def send_across(g, t):
        return pltpu.make_async_remote_copy(
            src_ref=z_out.at[g],
            dst_ref=z_in.at[g, z],
            send_sem=z_send.at[g, t - 1],
            recv_sem=z_recv.at[g],
            device_id=at(y, lax.rem(z + t, 8)),
            device_id_type=MESH,
        )

    def send_row(g, t):
        block = own_all.at[pl.ds(2 * y, 2) if g == 0 else pl.ds(8 + y, 1)]
        return pltpu.make_async_remote_copy(
            src_ref=block,
            dst_ref=block,
            send_sem=row_send.at[g, t - 1],
            recv_sem=row_recv.at[g],
            device_id=at(lax.rem(y + t, ROWS), z),
            device_id_type=MESH,
        )

    def send_out(g, t):
        first, end = tiles(g)
        block = pl.ds(first, end - first)
        return pltpu.make_async_remote_copy(
            src_ref=own_all.at[block],
            dst_ref=out_in.at[t, block],
            send_sem=out_send.at[g, t - 1],
            recv_sem=out_recv.at[g],
            device_id=beside(lax.rem(q + t, 8)),
            device_id_type=MESH,
        )

    def send_all(send, g, number):
        @pl.loop(1, number)
        def _(t):
            send(g, t).start()

    def arrive(ref, sem):
        pltpu.make_async_copy(ref, ref, sem).wait()

    def sum_beside(g):
        first, n = GROUPS[g]
        arrive(part_in.at[:, pl.ds(first, n)], part_recv.at[g])

        def column_sum(o):
            at_v = pl.ds(pl.multiple_of(o * 8, 8), 8)
            value = part[q, at_v, :]
            for t in range(7):
                value += part_in[t, at_v, :]
            return value

        if g == 0:

            @pl.loop(0, ROWS)
            def _(yy):
                for i in range(2):
                    plane[g, yy, i] = column_sum(2 * yy + i)
        else:
            last = column_sum(TILES - 1)

            @pl.loop(0, ROWS)
            def _(yy):
                plane[g, yy, 0] = column_sum(8 + yy)
                plane[g, yy, 1] = last

        send_all(send_plane, g, ROWS)
        y_in[g, y] = plane[g, y]

    def sum_plane(g):
        arrive(y_in.at[g, pl.ds(0, 3)], y_recv.at[g])
        value = y_in[g, 0]
        for yy in range(1, ROWS):
            value += y_in[g, yy]
        z_out[g] = value
        send_all(send_across, g, 8)
        z_in[g, z] = value

    def sum_across(g):
        arrive(z_in.at[g, pl.ds(0, 7)], z_recv.at[g])
        value = z_in[g, 0]
        for zz in range(1, 8):
            value += z_in[g, zz]
        if g == 0:
            own_all[pl.ds(2 * y, 2)] = value
        else:
            own_all[8 + y] = value[0]
            own_all[TILES - 1] = value[1]
        send_all(send_row, g, ROWS)

    def spread_out(g):
        first, end = tiles(g)
        arrive(own_all.at[pl.ds(0, 6 if g == 0 else 3)], row_recv.at[g])
        send_all(send_out, g, 8)
        out_in[0, first:end] = own_all[first:end]

    def collect(g):
        first, end = tiles(g)
        arrive(out_in.at[pl.ds(1, 7), pl.ds(first, end - first)], out_recv.at[g])

        @pl.loop(0, 8)
        def _(t):
            cols = pl.ds(pl.multiple_of(lax.rem(q - t + 8, 8) * 128, 128), 128)
            for o in range(first, end):
                sums_ref[o * 8 : (o + 1) * 8, cols] = out_in[t, o]

    def latent(first, end):
        @pl.loop(first, end)
        def _(b):
            points = pl.ds(pl.multiple_of(b * BLOCK, BLOCK), BLOCK)
            value = lax.dot_general(
                grad[0:V, points], weight[...], (((0,), (0,)), ((), ())), preferred_element_type=F32
            )
            latent_ref[points, :] = (GRAD_SCALE * value).astype(jnp.bfloat16)

    for c in range(NC):
        pairs(c)
    gradient(0)
    gradient(1)
    send_all(send_part, 0, 8)
    sum_beside(0)
    sum_plane(0)
    gradient(2)
    extras()
    send_all(send_part, 1, 8)
    sum_across(0)
    latent(0, 2)
    sum_beside(1)
    spread_out(0)
    latent(2, 4)
    sum_plane(1)
    latent(4, 6)
    sum_across(1)
    collect(0)
    latent(6, 8)
    spread_out(1)
    collect(1)

    for c in range(NC):

        @pl.loop(0, NB)
        def _(b):
            send_forecast(c, b).wait_send()
            send_sign(c, b).wait_send()

    for g in range(len(GROUPS)):

        @pl.loop(1, 8)
        def _(t):
            send_part(g, t).wait_send()
            send_across(g, t).wait_send()
            send_out(g, t).wait_send()

        @pl.loop(1, ROWS)
        def _(t):
            send_plane(g, t).wait_send()
            send_row(g, t).wait_send()


def finish_kernel(factor, latent, sums, latent_hbm, wgrad_hbm, bias_ref, loss_ref, wgrad, sem):
    store_latent = pltpu.make_async_copy(latent, latent_hbm, sem.at[0])
    store_latent.start()
    wgrad[...] = sums[0:V, :] * factor
    store_wgrad = pltpu.make_async_copy(wgrad, wgrad_hbm, sem.at[1])
    store_wgrad.start()
    extra = sums[V : V + 1, 0:128]
    lane = lax.broadcasted_iota(jnp.int32, (1, 128), 1)
    total = jnp.sum(jnp.where(lane == V, extra, 0.0), axis=1, keepdims=True)
    points = jnp.sum(jnp.where(lane == V + 1, extra, 0.0), axis=1, keepdims=True)
    bias_ref[...] = extra[:, 0:V] * factor
    loss_ref[...] = total / (V * (points * (1.0 / NB)))
    store_wgrad.wait()
    store_latent.wait()


def per_device(hidden_state, proj_weight, offset, truth, counts, var_weight, total_rows):
    latitude = (np.arange(total_rows) + 0.5) * (LATITUDE_SPAN / total_rows) * (math.pi / 180.0)
    area = jnp.asarray(np.cos(latitude), dtype=F32)
    vmem = pl.BlockSpec(memory_space=pltpu.VMEM)
    smem = pl.BlockSpec(memory_space=pltpu.SMEM)
    hbm = pl.BlockSpec(memory_space=pltpu.HBM)
    dma = pltpu.SemaphoreType.DMA
    bf16 = jnp.bfloat16
    blocks = pltpu.VMEM((NB, VP, BLOCK), F32)
    ng = len(GROUPS)
    latent, sums = pl.pallas_call(
        exchange_kernel,
        out_shape=(
            pltpu.VMEM((POINTS, D), bf16),
            pltpu.VMEM((VP, D), F32),
        ),
        in_specs=[smem, smem, vmem, vmem, hbm, hbm, hbm],
        out_specs=(vmem, vmem),
        scratch_shapes=[
            pltpu.VMEM((V, D), bf16),
            pltpu.VMEM((POINTS, D), bf16),
            pltpu.VMEM((VP, ROWS, CAP), F32),
            blocks,
            blocks,
            blocks,
            blocks,
            blocks,
            pltpu.VMEM((GP, POINTS), bf16),
            pltpu.VMEM((VP, 128), F32),
            pltpu.VMEM((VP, 128), F32),
            pltpu.VMEM((VP, 128), F32),
            pltpu.VMEM((VP, 128), F32),
            pltpu.VMEM((8, VP, 128), F32),
            pltpu.VMEM((7, VP, 128), F32),
            pltpu.VMEM((ng, ROWS, 2, 8, 128), F32),
            pltpu.VMEM((ng, ROWS, 2, 8, 128), F32),
            pltpu.VMEM((ng, 2, 8, 128), F32),
            pltpu.VMEM((ng, 8, 2, 8, 128), F32),
            pltpu.VMEM((TILES, 8, 128), F32),
            pltpu.VMEM((8, TILES, 8, 128), F32),
            dma((NB,)),
            dma((2,)),
            dma((NC, NB)),
            dma((NC,)),
            dma((NC, NB)),
            dma((NC,)),
            dma((ng, 7)),
            dma((ng,)),
            dma((ng, 3)),
            dma((ng,)),
            dma((ng, 7)),
            dma((ng,)),
            dma((ng, 3)),
            dma((ng,)),
            dma((ng, 7)),
            dma((ng,)),
        ],
        compiler_params=pltpu.CompilerParams(
            collective_id=0, has_side_effects=True, vmem_limit_bytes=59 * 1024 * 1024
        ),
        cost_estimate=pl.CostEstimate(
            flops=4 * V * POINTS * D, bytes_accessed=5_000_000, transcendentals=8_000_000
        ),
    )(
        counts,
        area,
        offset.reshape(1, V),
        var_weight.reshape(1, V),
        proj_weight,
        hidden_state.reshape(POINTS, D),
        truth,
    )
    factor = GRAD_SCALE / math.sqrt(NB * total_rows * CAP)
    latent, wgrad, bias, loss = pl.pallas_call(
        lambda *refs: finish_kernel(factor, *refs),
        out_shape=(
            jax.ShapeDtypeStruct((POINTS, D), bf16),
            jax.ShapeDtypeStruct((V, D), F32),
            jax.ShapeDtypeStruct((1, V), F32),
            jax.ShapeDtypeStruct((1, 1), F32),
        ),
        in_specs=[vmem, vmem],
        out_specs=(hbm, hbm, vmem, vmem),
        scratch_shapes=[pltpu.VMEM((V, D), F32), dma((2,))],
        compiler_params=pltpu.CompilerParams(vmem_limit_bytes=16 * 1024 * 1024),
        cost_estimate=pl.CostEstimate(flops=V * D, bytes_accessed=5_000_000, transcendentals=0),
    )(latent, sums)
    return latent.reshape(hidden_state.shape), wgrad, bias.reshape(V), loss.reshape(())


def solution(mesh):
    total_rows = ROWS * mesh.shape["space"]

    def step(*args):
        return per_device(*args, total_rows)

    return jax.shard_map(
        step,
        mesh=mesh,
        in_specs=(
            P("member", "space", None, None),
            P(),
            P(),
            P(None, "space", None),
            P("space"),
            P(),
        ),
        out_specs=(P("member", "space", None, None), P(), P(), P()),
        check_vma=False,
    )
```

```python
import math

import numpy as np

import jax
import jax.numpy as jnp
from jax import lax
from jax.experimental import pallas as pl
from jax.experimental.pallas import tpu as pltpu
from jax.sharding import PartitionSpec as P

SMOOTHING = 0.05
FAIRNESS = 0.95
GRAD_SCALE = 16.0
LATITUDE_SPAN = 80.0

V = 100
VP = 104
D = 1024
ROWS = 4
CAP = 512
POINTS = ROWS * CAP
BLOCK = 256
NB = 8
TILES = VP // 8
GP = 112
CHUNKS = ((0, 16), (16, 32), (48, 32), (80, 16), (96, 8))
SENT = (16, 32, 32, 16, 4)
NC = len(CHUNKS)
MESH = pl.DeviceIdType.MESH
F32 = jnp.float32
EPS2 = SMOOTHING * SMOOTHING
COEFF = FAIRNESS / (NB * (NB - 1)) + (1.0 - FAIRNESS) / (NB * NB)


def column(row):
    n = row.shape[1]
    here = lax.broadcasted_iota(jnp.int32, (VP, n), 0) == lax.broadcasted_iota(
        jnp.int32, (VP, n), 1
    )
    return jnp.sum(jnp.where(here, jnp.broadcast_to(row, (VP, n)), 0.0), axis=1, keepdims=True)


def exchange_kernel(
    counts_ref,
    area_ref,
    offset_ref,
    scale_ref,
    weight_hbm,
    hidden_hbm,
    truth_hbm,
    latent_ref,
    sums_ref,
    weight,
    hbuf,
    truth,
    field,
    met,
    signs,
    back,
    obs,
    grad,
    loss_acc,
    bias_acc,
    offset_col,
    scale_col,
    part,
    part_in,
    plane,
    plane_in,
    own_all,
    out_in,
    load_sem,
    side_sem,
    fwd_send,
    fwd_recv,
    ret_send,
    ret_recv,
    rs1_send,
    rs1_recv,
    rs2_send,
    rs2_recv,
    ag2_send,
    ag2_recv,
    ag1_send,
    ag1_recv,
):
    member = lax.axis_index("member")
    space = lax.axis_index("space")
    y, z_hi = lax.div(member, 2), lax.rem(member, 2)
    z_lo, q = lax.div(space, 8), lax.rem(space, 8)
    core = lax.rem(q, 2)
    z = z_hi * 4 + z_lo
    rank = y * 8 + z

    def at(yy, zz):
        return (yy * 2 + lax.div(zz, 4), lax.rem(zz, 4) * 8 + q)

    def at_rank(p):
        return at(lax.div(p, 8), lax.rem(p, 8))

    def beside(j):
        return (member, z_lo * 8 + j)

    def load(t):
        b = lax.rem(member + t, NB)
        rows = pl.ds(pl.multiple_of(b * BLOCK, BLOCK), BLOCK)
        return pltpu.make_async_copy(hidden_hbm.at[rows], hbuf.at[rows], load_sem.at[t - 1])

    load_weight = pltpu.make_async_copy(weight_hbm, weight, side_sem.at[0])
    load_weight.start()
    for t in range(1, NB + 1):
        load(t).start()
    load_truth = pltpu.make_async_copy(truth_hbm, truth, side_sem.at[1])
    load_truth.start()

    met[:, V:VP, :] = jnp.zeros((NB, VP - V, BLOCK), F32)
    back[:, V:VP, :] = jnp.zeros((NB, VP - V, BLOCK), F32)

    barrier = pltpu.get_barrier_semaphore()

    @pl.loop(1, 8)
    def _(t):
        pl.semaphore_signal(
            barrier, inc=1, device_id=beside(lax.rem(q + t, 8)), device_id_type=MESH
        )

    @pl.loop(1, 32)
    def _(t):
        pl.semaphore_signal(
            barrier, inc=1, device_id=at_rank(lax.rem(rank + t, 32)), device_id_type=MESH
        )

    offset_col[...] = jnp.broadcast_to(column(offset_ref[...]), (VP, 128))
    scale_col[...] = jnp.broadcast_to(column(scale_ref[...]), (VP, 128))
    loss_acc[...] = jnp.zeros_like(loss_acc)
    bias_acc[...] = jnp.zeros_like(bias_acc)
    obs[:, 96:VP, :] = jnp.zeros((NB, VP - 96, BLOCK), F32)

    lanes = lax.broadcasted_iota(jnp.int32, (1, BLOCK), 1)

    def live(b):
        return lanes + lax.rem(b, 2) * BLOCK < counts_ref[lax.div(b, 2)]

    def send_forecast(c, b):
        v0, n = CHUNKS[c][0], SENT[c]
        return pltpu.make_async_remote_copy(
            src_ref=field.at[b, pl.ds(v0, n)],
            dst_ref=met.at[member, pl.ds(v0, n)],
            send_sem=fwd_send.at[c, b],
            recv_sem=fwd_recv.at[c],
            device_id=(b, space),
            device_id_type=MESH,
        )

    def keep_forecast(c):
        v0, n = CHUNKS[c][0], SENT[c]
        return pltpu.make_async_copy(
            field.at[member, pl.ds(v0, n)], met.at[member, pl.ds(v0, n)], fwd_recv.at[c]
        )

    def send_forecasts(c):
        @pl.loop(1, NB)
        def _(t):
            send_forecast(c, lax.rem(member + t, NB)).start()

        keep_forecast(c).start()

    for t in range(1, NB + 1):
        load(t).wait()
        if t == 1:
            load_weight.wait()
        b = lax.rem(member + t, NB)
        rows = pl.ds(pl.multiple_of(b * BLOCK, BLOCK), BLOCK)
        product = lax.dot_general(
            weight[...], hbuf[rows, :], (((1,), (1,)), ((), ())), preferred_element_type=F32
        )
        forecast = product + offset_col[0:V, 0:1]
        field[b, 0:V, :] = jnp.where(live(b), forecast, 0.0)
        if t == 1:
            pl.semaphore_wait(barrier, 38)
        for c in range(2):
            if t < NB:
                send_forecast(c, b).start()
            else:
                keep_forecast(c).start()

    load_truth.wait()
    for b in range(NB):
        r, half = b // 2, b % 2
        point_weight = jnp.where(live(b), area_ref[space * ROWS + r], 0.0) * (1.0 / NB)
        factor = point_weight * scale_col[0:V, 0:1]
        gap = field[b, 0:V, :] - truth[:, r, half * BLOCK : (half + 1) * BLOCK]
        square = gap * gap + EPS2
        inverse = lax.rsqrt(square)
        obs[b, 0:V, :] = factor * (gap * inverse)
        misfit = factor * (square * inverse - SMOOTHING)
        loss_acc[0:V, :] += misfit[:, 0:128] + misfit[:, 128:256]

    area_here = area_ref[space * ROWS + y]

    def send_sign(c, m):
        v0, n = CHUNKS[c][0], SENT[c]
        return pltpu.make_async_remote_copy(
            src_ref=signs.at[m, pl.ds(v0, n)],
            dst_ref=back.at[member, pl.ds(v0, n)],
            send_sem=ret_send.at[c, m],
            recv_sem=ret_recv.at[c],
            device_id=(m, space),
            device_id_type=MESH,
        )

    def keep_sign(c):
        v0, n = CHUNKS[c][0], SENT[c]
        return pltpu.make_async_copy(
            signs.at[member, pl.ds(v0, n)], back.at[member, pl.ds(v0, n)], ret_recv.at[c]
        )

    def pairs(c):
        v0, n = CHUNKS[c]
        arrived = met.at[:, pl.ds(v0, SENT[c])]
        pltpu.make_async_copy(arrived, arrived, fwd_recv.at[c]).wait()

        @pl.loop(0, n // 8)
        def _(i):
            at_v = pl.ds(pl.multiple_of(v0 + i * 8, 8), 8)
            values = [met[m, at_v, :] for m in range(NB)]
            sums = [None] * NB
            roots = None
            for m in range(NB):
                for k in range(m + 1, NB):
                    gap = values[m] - values[k]
                    square = gap * gap + EPS2
                    inverse = lax.rsqrt(square)
                    sign = gap * inverse
                    root = square * inverse
                    roots = root if roots is None else roots + root
                    sums[m] = sign if sums[m] is None else sums[m] + sign
                    sums[k] = -sign if sums[k] is None else sums[k] - sign
            for m in range(NB):
                signs[m, at_v, :] = sums[m]
            spread = roots - (NB * (NB - 1) // 2) * SMOOTHING
            spread = (-COEFF * area_here) * scale_col[at_v, 0:1] * spread
            loss_acc[at_v, :] += spread[:, 0:128] + spread[:, 128:256]

        @pl.loop(1, NB)
        def _(t):
            send_sign(c, lax.rem(member + t, NB)).start()

        keep_sign(c).start()

    def send_part(c, t):
        v0, n = CHUNKS[c]
        j = lax.rem(q + t, 8)
        return pltpu.make_async_remote_copy(
            src_ref=part.at[j, pl.ds(v0, n)],
            dst_ref=part_in.at[t - 1, pl.ds(v0, n)],
            send_sem=rs1_send.at[c, t - 1],
            recv_sem=rs1_recv.at[c],
            device_id=beside(j),
            device_id_type=MESH,
        )

    lane = lax.broadcasted_iota(jnp.int32, (1, 128), 1)
    sub = lax.broadcasted_iota(jnp.int32, (8, 128), 0)

    def extras():
        bias = jnp.sum(bias_acc[...], axis=1, keepdims=True)
        eye = lax.broadcasted_iota(jnp.int32, (VP, 128), 0) == lax.broadcasted_iota(
            jnp.int32, (VP, 128), 1
        )
        extra = jnp.sum(jnp.where(eye, bias, 0.0), axis=0, keepdims=True)
        loss_here = jnp.sum(jnp.sum(loss_acc[...], axis=0, keepdims=True), axis=1, keepdims=True)
        points_here = jnp.float32(0.0)
        for r in range(ROWS):
            points_here += area_ref[space * ROWS + r] * counts_ref[r].astype(F32)
        extra = jnp.where(lane < V, extra, 0.0)
        extra = jnp.where(lane == V, loss_here, extra)
        extra = jnp.where(lane == V + 1, points_here, extra)
        part[0, 96:VP, :] = jnp.where(sub == V - 96, extra, part[0, 96:VP, :])

    def gradient(c):
        v0, n = CHUNKS[c]
        arrived = back.at[:, pl.ds(v0, SENT[c])]
        pltpu.make_async_copy(arrived, arrived, ret_recv.at[c]).wait()
        padded = max(n, 16)
        for b in range(NB):
            point_weight = jnp.where(live(b), area_ref[space * ROWS + b // 2] * COEFF, 0.0)
            factor = point_weight * scale_col[v0 : v0 + n, 0:1]
            value = obs[b, v0 : v0 + n, :] - factor * back[b, v0 : v0 + n, :]
            bias_acc[v0 : v0 + n, :] += value[:, 0:128] + value[:, 128:256]
            if padded > n:
                value = jnp.concatenate([value, jnp.zeros((padded - n, BLOCK), F32)], axis=0)
            grad[v0 : v0 + padded, b * BLOCK : (b + 1) * BLOCK] = value.astype(jnp.bfloat16)
        for j in range(0, 8, 2):
            piece = jnp.dot(
                grad[v0 : v0 + padded, :],
                hbuf[:, j * 128 : (j + 2) * 128],
                preferred_element_type=F32,
            )
            part[j, v0 : v0 + n, :] = piece[0:n, 0:128]
            part[j + 1, v0 : v0 + n, :] = piece[0:n, 128:256]
        if c == NC - 1:
            extras()

        @pl.loop(1, 8)
        def _(t):
            send_part(c, t).start()

    def owner(o):
        return 2 * o + core

    mine = lax.div(rank, 2)
    owns = lax.rem(rank, 2) == core

    def tiles(c):
        v0, n = CHUNKS[c]
        return v0 // 8, (v0 + n) // 8

    def send_plane(o):
        p = owner(o)
        return pltpu.make_async_remote_copy(
            src_ref=plane.at[o],
            dst_ref=plane_in.at[lax.rem(rank - p + 31, 32)],
            send_sem=rs2_send.at[o],
            recv_sem=rs2_recv,
            device_id=at_rank(p),
            device_id_type=MESH,
        )

    def sum_beside(c):
        v0, n = CHUNKS[c]
        arrived = part_in.at[:, pl.ds(v0, n)]
        pltpu.make_async_copy(arrived, arrived, rs1_recv.at[c]).wait()

        @pl.loop(*tiles(c))
        def _(o):
            at_v = pl.ds(pl.multiple_of(o * 8, 8), 8)
            value = part[q, at_v, :]
            for t in range(7):
                value += part_in[t, at_v, :]
            plane[o] = value

            @pl.when(owner(o) != rank)
            def _():
                send_plane(o).start()

    def send_own(t):
        return pltpu.make_async_remote_copy(
            src_ref=own_all.at[mine],
            dst_ref=own_all.at[mine],
            send_sem=ag2_send.at[t - 1],
            recv_sem=ag2_recv.at[mine],
            device_id=at_rank(lax.rem(rank + t, 32)),
            device_id_type=MESH,
        )

    def owns_in(c):
        first, end = tiles(c)
        return jnp.logical_and(owns, jnp.logical_and(mine >= first, mine < end))

    def sum_across(c):
        @pl.when(owns_in(c))
        def _():
            pltpu.make_async_copy(plane_in, plane_in, rs2_recv).wait()
            value = plane[mine]
            for t in range(31):
                value += plane_in[t]
            own_all[mine] = value

            @pl.loop(1, 32)
            def _(t):
                send_own(t).start()

    def send_out(c, t):
        first, end = tiles(c)
        block = pl.ds(first, end - first)
        return pltpu.make_async_remote_copy(
            src_ref=own_all.at[block],
            dst_ref=out_in.at[t, block],
            send_sem=ag1_send.at[c, t - 1],
            recv_sem=ag1_recv.at[c],
            device_id=beside(lax.rem(q + t, 8)),
            device_id_type=MESH,
        )

    def spread_out(c):
        first, end = tiles(c)

        @pl.loop(first, end)
        def _(o):
            @pl.when(owner(o) != rank)
            def _():
                pltpu.make_async_copy(own_all.at[o], own_all.at[o], ag2_recv.at[o]).wait()

        @pl.loop(1, 8)
        def _(t):
            send_out(c, t).start()

        out_in[0, first:end] = own_all[first:end]

    def collect(c):
        first, end = tiles(c)
        arrived = out_in.at[pl.ds(1, 7), pl.ds(first, end - first)]
        pltpu.make_async_copy(arrived, arrived, ag1_recv.at[c]).wait()

        @pl.loop(0, 8)
        def _(t):
            cols = pl.ds(pl.multiple_of(lax.rem(q - t + 8, 8) * 128, 128), 128)
            for o in range(first, end):
                sums_ref[o * 8 : (o + 1) * 8, cols] = out_in[t, o]

    def latent(first, end):
        for b in range(first, end):
            rows = slice(b * BLOCK, (b + 1) * BLOCK)
            value = lax.dot_general(
                grad[0:V, rows], weight[...], (((0,), (0,)), ((), ())), preferred_element_type=F32
            )
            latent_ref[rows, :] = (GRAD_SCALE * value).astype(jnp.bfloat16)

    stages = (pairs, gradient, sum_beside, sum_across, spread_out, collect)
    for step in range(NC + len(stages) - 1):
        for i, stage in enumerate(stages):
            c = step - i
            if 0 <= c < NC:
                stage(c)
                if stage is pairs and c + 2 < NC:
                    send_forecasts(c + 2)
                if c == NC - 1 and 1 <= i <= 4:
                    latent(2 * (i - 1), 2 * i)

    for c in range(NC):

        @pl.loop(1, NB)
        def _(t):
            b = lax.rem(member + t, NB)
            send_forecast(c, b).wait_send()
            send_sign(c, b).wait_send()

        @pl.loop(1, 8)
        def _(t):
            send_part(c, t).wait_send()
            send_out(c, t).wait_send()

    @pl.loop(0, TILES)
    def _(o):
        @pl.when(owner(o) != rank)
        def _():
            send_plane(o).wait_send()

    @pl.when(jnp.logical_and(owns, mine < TILES))
    def _():
        @pl.loop(1, 32)
        def _(t):
            send_own(t).wait_send()


def finish_kernel(factor, latent, sums, latent_hbm, wgrad_hbm, bias_ref, loss_ref, wgrad, sem):
    store_latent = pltpu.make_async_copy(latent, latent_hbm, sem.at[0])
    store_latent.start()
    wgrad[...] = sums[0:V, :] * factor
    store_wgrad = pltpu.make_async_copy(wgrad, wgrad_hbm, sem.at[1])
    store_wgrad.start()
    extra = sums[V : V + 1, 0:128]
    lane = lax.broadcasted_iota(jnp.int32, (1, 128), 1)
    total = jnp.sum(jnp.where(lane == V, extra, 0.0), axis=1, keepdims=True)
    points = jnp.sum(jnp.where(lane == V + 1, extra, 0.0), axis=1, keepdims=True)
    bias_ref[...] = extra[:, 0:V] * factor
    loss_ref[...] = total / (V * (points * (1.0 / NB)))
    store_wgrad.wait()
    store_latent.wait()


def per_device(hidden_state, proj_weight, offset, truth, counts, var_weight, total_rows):
    latitude = (np.arange(total_rows) + 0.5) * (LATITUDE_SPAN / total_rows) * (math.pi / 180.0)
    area = jnp.asarray(np.cos(latitude), dtype=F32)
    vmem = pl.BlockSpec(memory_space=pltpu.VMEM)
    smem = pl.BlockSpec(memory_space=pltpu.SMEM)
    hbm = pl.BlockSpec(memory_space=pltpu.HBM)
    dma = pltpu.SemaphoreType.DMA
    bf16 = jnp.bfloat16
    blocks = pltpu.VMEM((NB, VP, BLOCK), F32)
    latent, sums = pl.pallas_call(
        exchange_kernel,
        out_shape=(
            pltpu.VMEM((POINTS, D), bf16),
            pltpu.VMEM((VP, D), F32),
        ),
        in_specs=[smem, smem, vmem, vmem, hbm, hbm, hbm],
        out_specs=(vmem, vmem),
        scratch_shapes=[
            pltpu.VMEM((V, D), bf16),
            pltpu.VMEM((POINTS, D), bf16),
            pltpu.VMEM((V, ROWS, CAP), F32),
            blocks,
            blocks,
            blocks,
            blocks,
            blocks,
            pltpu.VMEM((GP, POINTS), bf16),
            pltpu.VMEM((VP, 128), F32),
            pltpu.VMEM((VP, 128), F32),
            pltpu.VMEM((VP, 128), F32),
            pltpu.VMEM((VP, 128), F32),
            pltpu.VMEM((8, VP, 128), F32),
            pltpu.VMEM((7, VP, 128), F32),
            pltpu.VMEM((TILES, 8, 128), F32),
            pltpu.VMEM((31, 8, 128), F32),
            pltpu.VMEM((TILES, 8, 128), F32),
            pltpu.VMEM((8, TILES, 8, 128), F32),
            dma((NB,)),
            dma((2,)),
            dma((NC, NB)),
            dma((NC,)),
            dma((NC, NB)),
            dma((NC,)),
            dma((NC, 7)),
            dma((NC,)),
            dma((TILES,)),
            dma,
            dma((31,)),
            dma((TILES,)),
            dma((NC, 7)),
            dma((NC,)),
        ],
        compiler_params=pltpu.CompilerParams(
            collective_id=0, has_side_effects=True, vmem_limit_bytes=59 * 1024 * 1024
        ),
        cost_estimate=pl.CostEstimate(
            flops=4 * V * POINTS * D, bytes_accessed=5_000_000, transcendentals=8_000_000
        ),
    )(
        counts,
        area,
        offset.reshape(1, V),
        var_weight.reshape(1, V),
        proj_weight,
        hidden_state.reshape(POINTS, D),
        truth,
    )
    factor = GRAD_SCALE / math.sqrt(NB * total_rows * CAP)
    latent, wgrad, bias, loss = pl.pallas_call(
        lambda *refs: finish_kernel(factor, *refs),
        out_shape=(
            jax.ShapeDtypeStruct((POINTS, D), bf16),
            jax.ShapeDtypeStruct((V, D), F32),
            jax.ShapeDtypeStruct((1, V), F32),
            jax.ShapeDtypeStruct((1, 1), F32),
        ),
        in_specs=[vmem, vmem],
        out_specs=(hbm, hbm, vmem, vmem),
        scratch_shapes=[pltpu.VMEM((V, D), F32), dma((2,))],
        compiler_params=pltpu.CompilerParams(vmem_limit_bytes=16 * 1024 * 1024),
        cost_estimate=pl.CostEstimate(flops=V * D, bytes_accessed=5_000_000, transcendentals=0),
    )(latent, sums)
    return latent.reshape(hidden_state.shape), wgrad, bias.reshape(V), loss.reshape(())


def solution(mesh):
    total_rows = ROWS * mesh.shape["space"]

    def step(*args):
        return per_device(*args, total_rows)

    return jax.shard_map(
        step,
        mesh=mesh,
        in_specs=(
            P("member", "space", None, None),
            P(),
            P(),
            P(None, "space", None),
            P("space"),
            P(),
        ),
        out_specs=(P("member", "space", None, None), P(), P(), P()),
        check_vma=False,
    )
```

```python
import math

import numpy as np

import jax
import jax.numpy as jnp
from jax import lax
from jax.experimental import pallas as pl
from jax.experimental.pallas import tpu as pltpu
from jax.sharding import PartitionSpec as P

SMOOTHING = 0.05
FAIRNESS = 0.95
GRAD_SCALE = 16.0
LATITUDE_SPAN = 80.0

V = 100
VP = 104
GP = 112
D = 1024
ROWS = 4
CAP = 512
POINTS = ROWS * CAP
BLOCK = 256
NB = 8
NT = 25
CHUNKS = ((0, 8), (8, 8), (16, 4), (20, 5))
NC = len(CHUNKS)
GROUPS = ((0, 64), (64, 16))
LAST = 80
MESH = pl.DeviceIdType.MESH
F32 = jnp.float32
EPS2 = SMOOTHING * SMOOTHING
COEFF = FAIRNESS / (NB * (NB - 1)) + (1.0 - FAIRNESS) / (NB * NB)


def column(row):
    n = row.shape[1]
    here = lax.broadcasted_iota(jnp.int32, (VP, n), 0) == lax.broadcasted_iota(
        jnp.int32, (VP, n), 1
    )
    return jnp.sum(jnp.where(here, jnp.broadcast_to(row, (VP, n)), 0.0), axis=1, keepdims=True)


def exchange_kernel(
    counts_ref,
    area_ref,
    offset_ref,
    scale_ref,
    weight_hbm,
    hidden_hbm,
    truth_hbm,
    latent_ref,
    sums_ref,
    weight,
    hbuf,
    truth,
    field,
    met,
    signs,
    back,
    obs,
    grad,
    loss_acc,
    bias_acc,
    scale,
    part,
    part_in,
    plane,
    pair,
    y_in,
    z_out,
    z_in,
    own_all,
    out_in,
    last,
    last_in,
    last_mid,
    last_z,
    last_own,
    last_out,
    load_sem,
    side_sem,
    fwd_send,
    fwd_recv,
    ret_send,
    ret_recv,
    part_send,
    part_recv,
    y_send,
    y_recv,
    z_send,
    z_recv,
    row_send,
    row_recv,
    out_send,
    out_recv,
    last_send,
    last_recv,
):
    member = lax.axis_index("member")
    space = lax.axis_index("space")
    y, z_hi = lax.div(member, 2), lax.rem(member, 2)
    z_lo, q = lax.div(space, 8), lax.rem(space, 8)
    x, core = lax.div(q, 2), lax.rem(q, 2)
    z = z_hi * 4 + z_lo
    in_plane = x * 4 + y
    in_stack = z * 2 + core

    def at(xx, yy, zz, cc):
        return (yy * 2 + lax.div(zz, 4), lax.rem(zz, 4) * 8 + xx * 2 + cc)

    def beside(j):
        return at(lax.div(j, 2), y, z, lax.rem(j, 2))

    def plane_device(w):
        return at(lax.div(w, 4), lax.rem(w, 4), z, core)

    def stack_device(u):
        return at(x, y, lax.div(u, 2), lax.rem(u, 2))

    def block_points(b):
        return pl.ds(pl.multiple_of(b * BLOCK, BLOCK), BLOCK)

    def load(t):
        rows = block_points(lax.rem(member + t, NB))
        return pltpu.make_async_copy(hidden_hbm.at[rows], hbuf.at[rows], load_sem.at[t - 1])

    load_weight = pltpu.make_async_copy(weight_hbm, weight, side_sem.at[0])
    load_weight.start()
    for t in range(1, NB + 1):
        load(t).start()
    load_truth = pltpu.make_async_copy(truth_hbm, truth, side_sem.at[1])
    load_truth.start()

    barrier = pltpu.get_barrier_semaphore()

    def greet(device):
        pl.semaphore_signal(barrier, inc=1, device_id=device, device_id_type=MESH)

    @pl.loop(1, 16)
    def _(t):
        greet(plane_device(lax.rem(in_plane + t, 16)))
        greet(stack_device(lax.rem(in_stack + t, 16)))

    @pl.loop(1, 4)
    def _(t):
        greet(at(x, lax.rem(y + t, 4), lax.rem(z + 4, 8), core))
        greet(at(lax.rem(x + t, 4), y, z, 1 - core))

    offsets = column(offset_ref[...])[0:V]
    scales = jnp.broadcast_to(column(scale_ref[...]), (VP, 128))
    for i in range(NT // 2):
        scale[2 * i] = scales[8 * i : 8 * i + 8]
        scale[2 * i + 1] = scales[8 * i : 8 * i + 8]
    scale[NT - 1] = jnp.concatenate([scales[96:V], scales[96:V]], axis=0)
    loss_acc[...] = jnp.zeros_like(loss_acc)
    bias_acc[...] = jnp.zeros_like(bias_acc)

    lane = lax.broadcasted_iota(jnp.int32, (1, 128), 1)
    sub = lax.broadcasted_iota(jnp.int32, (8, 128), 0)

    def live(b, h):
        return lane + (lax.rem(b, 2) * 2 + h) * 128 < counts_ref[lax.div(b, 2)]

    def point_weights(b, factor):
        area = area_ref[space * ROWS + lax.div(b, 2)] * factor
        halves = [jnp.where(live(b, h), area, 0.0) for h in range(2)]
        return halves, jnp.where(sub < 4, halves[0], halves[1])

    def send_forecast(c, b):
        block = pl.ds(*CHUNKS[c])
        return pltpu.make_async_remote_copy(
            src_ref=field.at[b, block],
            dst_ref=met.at[member, block],
            send_sem=fwd_send.at[c, b],
            recv_sem=fwd_recv.at[c],
            device_id=(b, space),
            device_id_type=MESH,
        )

    def keep_forecast(c):
        block = pl.ds(*CHUNKS[c])
        return pltpu.make_async_copy(
            field.at[member, block], met.at[member, block], fwd_recv.at[c]
        )

    for t in range(1, NB + 1):
        load(t).wait()
        if t == 1:
            load_weight.wait()
        b = lax.rem(member + t, NB)
        product = lax.dot_general(
            weight[...],
            hbuf[block_points(b), :],
            (((1,), (1,)), ((), ())),
            preferred_element_type=F32,
        )
        forecast = product + offsets
        halves = [
            jnp.where(live(b, h), forecast[:, h * 128 : (h + 1) * 128], 0.0) for h in range(2)
        ]
        for i in range(NT // 2):
            for h in range(2):
                field[b, 2 * i + h] = halves[h][8 * i : 8 * i + 8]
        field[b, NT - 1] = jnp.concatenate([halves[0][96:V], halves[1][96:V]], axis=0)
        if t == 1:
            pl.semaphore_wait(barrier, 36)
        for c in range(2):
            if t < NB:
                send_forecast(c, b).start()
            else:
                keep_forecast(c).start()
    for c in range(2, NC):

        @pl.loop(1, NB)
        def _(t):
            send_forecast(c, lax.rem(member + t, NB)).start()

        keep_forecast(c).start()

    load_truth.wait()

    def misfit(b, tile, target, weight_here):
        gap = field[b, tile] - target
        square = gap * gap + EPS2
        inverse = lax.rsqrt(square)
        factor = weight_here * scale[tile]
        obs[b, tile] = factor * (gap * inverse)
        return factor * (square * inverse - SMOOTHING)

    def target(b, v, h):
        first = (b % 2) * BLOCK + h * 128
        return truth[v, b // 2, first : first + 128]

    @pl.loop(0, NT // 2)
    def _(i):
        at_v = pl.ds(pl.multiple_of(i * 8, 8), 8)
        total = jnp.zeros((8, 128), F32)
        for b in range(NB):
            halves, _ = point_weights(b, 1.0 / NB)
            for h in range(2):
                total += misfit(b, 2 * i + h, target(b, at_v, h), halves[h])
        loss_acc[...] += total

    total = jnp.zeros((8, 128), F32)
    for b in range(NB):
        _, both = point_weights(b, 1.0 / NB)
        tail = pl.ds(96, 4)
        goal = jnp.concatenate([target(b, tail, 0), target(b, tail, 1)], axis=0)
        total += misfit(b, NT - 1, goal, both)
    loss_acc[...] += total

    area_here = area_ref[space * ROWS + y]

    def send_sign(c, m):
        block = pl.ds(*CHUNKS[c])
        return pltpu.make_async_remote_copy(
            src_ref=signs.at[m, block],
            dst_ref=back.at[member, block],
            send_sem=ret_send.at[c, m],
            recv_sem=ret_recv.at[c],
            device_id=(m, space),
            device_id_type=MESH,
        )

    def keep_sign(c):
        block = pl.ds(*CHUNKS[c])
        return pltpu.make_async_copy(
            signs.at[member, block], back.at[member, block], ret_recv.at[c]
        )

    def arrive(ref, sem):
        pltpu.make_async_copy(ref, ref, sem).wait()

    def meet(block):
        values = [met[m, block] for m in range(NB)]
        sums = [None] * NB
        roots = None
        for m in range(NB):
            for k in range(m + 1, NB):
                gap = values[m] - values[k]
                square = gap * gap + EPS2
                inverse = lax.rsqrt(square)
                sign = gap * inverse
                root = square * inverse
                roots = root if roots is None else roots + root
                sums[m] = sign if sums[m] is None else sums[m] + sign
                sums[k] = -sign if sums[k] is None else sums[k] - sign
        for m in range(NB):
            signs[m, block] = sums[m]
        spread = (roots - (NB * (NB - 1) // 2) * SMOOTHING) * scale[block]
        loss_acc[...] += (-COEFF * area_here) * jnp.sum(spread, axis=0)

    def pairs(c):
        first, n = CHUNKS[c]
        arrive(met.at[:, pl.ds(first, n)], fwd_recv.at[c])

        @pl.loop(0, n // 2)
        def _(i):
            meet(pl.ds(first + 2 * i, 2))

        if n % 2:
            meet(pl.ds(first + n - 1, 1))

        @pl.loop(1, NB)
        def _(t):
            send_sign(c, lax.rem(member + t, NB)).start()

        keep_sign(c).start()

    def gradient(c):
        first, n = CHUNKS[c]
        v0 = 4 * first
        arrive(back.at[:, pl.ds(first, n)], ret_recv.at[c])

        @pl.loop(0, NB)
        def _(b):
            halves, both = point_weights(b, COEFF)

            def value(tile, weight_here):
                result = obs[b, tile] - (weight_here * scale[tile]) * back[b, tile]
                bias_acc[tile] += result
                return result

            pieces = [
                [value(first + 2 * i + h, halves[h]) for i in range(n // 2)] for h in range(2)
            ]
            if n % 2:
                tail = value(NT - 1, both)
                for h in range(2):
                    pieces[h] += [tail[4 * h : 4 * h + 4], jnp.zeros((GP - V, 128), F32)]
            for h in range(2):
                stacked = jnp.concatenate(pieces[h], axis=0)
                points = pl.ds(pl.multiple_of(b * BLOCK + h * 128, 128), 128)
                grad[v0 : v0 + stacked.shape[0], points] = stacked.astype(jnp.bfloat16)

        @pl.loop(0, 4)
        def _(j):
            rows = GP - v0 if n % 2 else 4 * n
            piece = jnp.dot(
                grad[v0 : v0 + rows, :],
                hbuf[:, pl.ds(pl.multiple_of(j * 256, 256), 256)],
                preferred_element_type=F32,
            )
            for k in range(2):
                block = piece[:, k * 128 : (k + 1) * 128]
                if n % 2:
                    for i in range(6):
                        last[4 * j + 2 * k + i // 3, i % 3] = block[4 * i : 4 * i + 4]
                else:
                    part[2 * j + k, v0 : v0 + rows, :] = block

    def extras():
        rows = []
        for i in range(NT // 2):
            rows.append(bias_acc[2 * i] + bias_acc[2 * i + 1])
        tail = bias_acc[NT - 1]
        rows += [tail[0:4] + tail[4:8], jnp.zeros((VP - V, 128), F32)]
        bias = jnp.sum(jnp.concatenate(rows, axis=0), axis=1, keepdims=True)
        eye = lax.broadcasted_iota(jnp.int32, (VP, 128), 0) == lax.broadcasted_iota(
            jnp.int32, (VP, 128), 1
        )
        extra = jnp.sum(jnp.where(eye, bias, 0.0), axis=0, keepdims=True)
        loss_here = jnp.sum(jnp.sum(loss_acc[...], axis=0, keepdims=True), axis=1, keepdims=True)
        points_here = jnp.float32(0.0)
        for r in range(ROWS):
            points_here += area_ref[space * ROWS + r] * counts_ref[r].astype(F32)
        extra = jnp.where(lane == V, loss_here, extra)
        extra = jnp.where(lane == V + 1, points_here, extra)
        last[1, 2, 0:1, :] = extra

    def tiles(g):
        first, n = GROUPS[g]
        return first // 8, (first + n) // 8

    def send_part(g, t):
        rows = pl.ds(*GROUPS[g])
        j = lax.rem(q + t, 8)
        return pltpu.make_async_remote_copy(
            src_ref=part.at[j, rows],
            dst_ref=part_in.at[t - 1, rows],
            send_sem=part_send.at[g, t - 1],
            recv_sem=part_recv.at[g],
            device_id=beside(j),
            device_id_type=MESH,
        )

    def send_plane(g, t):
        yy = lax.rem(y + t, 4)
        return pltpu.make_async_remote_copy(
            src_ref=plane.at[yy] if g == 0 else pair,
            dst_ref=y_in.at[g, y],
            send_sem=y_send.at[g, t - 1],
            recv_sem=y_recv.at[g],
            device_id=at(x, yy, z, core),
            device_id_type=MESH,
        )

    def send_across(g, t):
        return pltpu.make_async_remote_copy(
            src_ref=z_out.at[g],
            dst_ref=z_in.at[g, z],
            send_sem=z_send.at[g, t - 1],
            recv_sem=z_recv.at[g],
            device_id=at(x, y, lax.rem(z + t, 8), core),
            device_id_type=MESH,
        )

    def send_row(t):
        block = own_all.at[pl.ds(2 * y, 2)]
        return pltpu.make_async_remote_copy(
            src_ref=block,
            dst_ref=block,
            send_sem=row_send.at[t - 1],
            recv_sem=row_recv,
            device_id=at(x, lax.rem(y + t, 4), z, core),
            device_id_type=MESH,
        )

    def send_out(g, t):
        first, end = tiles(g)
        block = pl.ds(first, end - first)
        return pltpu.make_async_remote_copy(
            src_ref=own_all.at[block],
            dst_ref=out_in.at[t, block],
            send_sem=out_send.at[g, t - 1],
            recv_sem=out_recv.at[g],
            device_id=beside(lax.rem(q + t, 8)),
            device_id_type=MESH,
        )

    def send_all(send, number):
        @pl.loop(1, number)
        def _(t):
            send(t).start()

    def send_parts(g):
        send_all(lambda t: send_part(g, t), 8)

    def sum_beside(g):
        arrive(part_in.at[:, pl.ds(*GROUPS[g])], part_recv.at[g])

        def column_sum(o):
            at_v = pl.ds(pl.multiple_of(o * 8, 8), 8)
            value = part[q, at_v, :]
            for t in range(7):
                value += part_in[t, at_v, :]
            return value

        if g == 0:

            @pl.loop(0, 4)
            def _(yy):
                for i in range(2):
                    plane[yy, i] = column_sum(2 * yy + i)

            y_in[g, y] = plane[y]
        else:
            for i in range(2):
                pair[i] = column_sum(8 + i)
            y_in[g, y] = pair[...]
        send_all(lambda t: send_plane(g, t), 4)

    def sum_plane(g):
        arrive(y_in.at[g, pl.ds(0, 3)], y_recv.at[g])
        value = y_in[g, 0]
        for yy in range(1, 4):
            value += y_in[g, yy]
        z_out[g] = value
        z_in[g, z] = value
        send_all(lambda t: send_across(g, t), 8)

    def spread_out(g):
        first, end = tiles(g)
        send_all(lambda t: send_out(g, t), 8)
        out_in[0, first:end] = own_all[first:end]

    def sum_across(g):
        arrive(z_in.at[g, pl.ds(0, 7)], z_recv.at[g])
        value = z_in[g, 0]
        for zz in range(1, 8):
            value += z_in[g, zz]
        if g == 0:
            own_all[pl.ds(2 * y, 2)] = value
            send_all(send_row, 4)
        else:
            own_all[8:10] = value
            spread_out(1)

    def collect_rows():
        arrive(own_all.at[pl.ds(0, 6)], row_recv)
        spread_out(0)

    def collect(g):
        first, end = tiles(g)
        arrive(out_in.at[pl.ds(1, 7), pl.ds(first, end - first)], out_recv.at[g])

        @pl.loop(0, 8)
        def _(t):
            cols = pl.ds(pl.multiple_of(lax.rem(q - t + 8, 8) * 128, 128), 128)
            for o in range(first, end):
                sums_ref[o * 8 : (o + 1) * 8, cols] = out_in[t, o]

    def last_copy(phase, t):
        if phase == 1:
            to = lax.rem(in_stack + t, 16)
            src, dst, device = last_mid, last_z.at[in_stack], stack_device(to)
        else:
            to = lax.rem(in_plane + t, 16)
            src = last.at[to] if phase == 0 else last_own
            dst = (last_in if phase == 0 else last_out).at[in_plane]
            device = plane_device(to)
        return pltpu.make_async_remote_copy(
            src_ref=src,
            dst_ref=dst,
            send_sem=last_send.at[phase, t - 1],
            recv_sem=last_recv.at[phase],
            device_id=device,
            device_id_type=MESH,
        )

    def last_start(phase):
        send_all(lambda t: last_copy(phase, t), 16)

    def last_sum(phase, source):
        arrive(source.at[pl.ds(0, 15)], last_recv.at[phase])
        value = source[0]
        for t in range(1, 16):
            value += source[t]
        return value

    def last_scatter():
        last_start(0)
        last_in[in_plane] = last[in_plane]

    def last_across():
        value = last_sum(0, last_in)
        last_mid[...] = value
        last_start(1)
        last_z[in_stack] = value

    def last_gather():
        value = last_sum(1, last_z)
        last_own[...] = value
        last_start(2)
        last_out[in_plane] = value

    def last_collect():
        arrive(last_out.at[pl.ds(0, 15)], last_recv.at[2])

        @pl.loop(0, 8)
        def _(j):
            cols = pl.ds(pl.multiple_of(j * 128, 128), 128)
            for i in range(6):
                rows = slice(LAST + 4 * i, LAST + 4 * i + 4)
                sums_ref[rows, cols] = last_out[2 * j + i // 3, i % 3]

    def latent(first, end):
        @pl.loop(first, end)
        def _(b):
            points = block_points(b)
            value = lax.dot_general(
                grad[0:V, points], weight[...], (((0,), (0,)), ((), ())), preferred_element_type=F32
            )
            latent_ref[points, :] = (GRAD_SCALE * value).astype(jnp.bfloat16)

    for c in range(NC):
        pairs(c)
    gradient(0)
    gradient(1)
    send_parts(0)
    gradient(2)
    send_parts(1)
    sum_beside(0)
    gradient(3)
    extras()
    last_scatter()
    sum_plane(0)
    sum_beside(1)
    latent(0, 2)
    last_across()
    sum_across(0)
    sum_plane(1)
    latent(2, 4)
    last_gather()
    collect_rows()
    sum_across(1)
    latent(4, 8)
    last_collect()
    collect(0)
    collect(1)

    @pl.loop(1, NB)
    def _(t):
        b = lax.rem(member + t, NB)
        for c in range(NC):
            send_forecast(c, b).wait_send()
            send_sign(c, b).wait_send()
        for g in range(len(GROUPS)):
            send_part(g, t).wait_send()
            send_across(g, t).wait_send()
            send_out(g, t).wait_send()

    @pl.loop(1, 4)
    def _(t):
        for g in range(len(GROUPS)):
            send_plane(g, t).wait_send()
        send_row(t).wait_send()

    @pl.loop(1, 16)
    def _(t):
        for phase in range(3):
            last_copy(phase, t).wait_send()


def finish_kernel(factor, latent, sums, latent_hbm, wgrad_hbm, bias_ref, loss_ref, wgrad, sem):
    stores = []
    for b in range(4):
        rows = pl.ds(b * CAP, CAP)
        stores.append(pltpu.make_async_copy(latent.at[rows], latent_hbm.at[rows], sem.at[b]))
        stores[-1].start()
    wgrad[...] = sums[0:V, :] * factor
    stores.append(pltpu.make_async_copy(wgrad, wgrad_hbm, sem.at[4]))
    stores[-1].start()
    extra = sums[V : V + 1, 0:128]
    lane = lax.broadcasted_iota(jnp.int32, (1, 128), 1)
    total = jnp.sum(jnp.where(lane == V, extra, 0.0), axis=1, keepdims=True)
    points = jnp.sum(jnp.where(lane == V + 1, extra, 0.0), axis=1, keepdims=True)
    bias_ref[...] = extra[:, 0:V] * factor
    loss_ref[...] = total / (V * (points * (1.0 / NB)))
    for store in stores:
        store.wait()


def per_device(hidden_state, proj_weight, offset, truth, counts, var_weight, total_rows):
    latitude = (np.arange(total_rows) + 0.5) * (LATITUDE_SPAN / total_rows) * (math.pi / 180.0)
    area = jnp.asarray(np.cos(latitude), dtype=F32)
    vmem = pl.BlockSpec(memory_space=pltpu.VMEM)
    smem = pl.BlockSpec(memory_space=pltpu.SMEM)
    hbm = pl.BlockSpec(memory_space=pltpu.HBM)
    dma = pltpu.SemaphoreType.DMA
    bf16 = jnp.bfloat16
    blocks = pltpu.VMEM((NB, NT, 8, 128), F32)
    half_tiles = (3, 4, 128)
    latent, sums = pl.pallas_call(
        exchange_kernel,
        out_shape=(
            pltpu.VMEM((POINTS, D), bf16),
            pltpu.VMEM((VP, D), F32),
        ),
        in_specs=[smem, smem, vmem, vmem, hbm, hbm, hbm],
        out_specs=(vmem, vmem),
        scratch_shapes=[
            pltpu.VMEM((V, D), bf16),
            pltpu.VMEM((POINTS, D), bf16),
            pltpu.VMEM((V, ROWS, CAP), F32),
            blocks,
            blocks,
            blocks,
            blocks,
            blocks,
            pltpu.VMEM((GP, POINTS), bf16),
            pltpu.VMEM((8, 128), F32),
            pltpu.VMEM((NT, 8, 128), F32),
            pltpu.VMEM((NT, 8, 128), F32),
            pltpu.VMEM((8, LAST, 128), F32),
            pltpu.VMEM((7, LAST, 128), F32),
            pltpu.VMEM((4, 2, 8, 128), F32),
            pltpu.VMEM((2, 8, 128), F32),
            pltpu.VMEM((2, 4, 2, 8, 128), F32),
            pltpu.VMEM((2, 2, 8, 128), F32),
            pltpu.VMEM((2, 8, 2, 8, 128), F32),
            pltpu.VMEM((LAST // 8, 8, 128), F32),
            pltpu.VMEM((8, LAST // 8, 8, 128), F32),
            pltpu.VMEM((16, *half_tiles), F32),
            pltpu.VMEM((16, *half_tiles), F32),
            pltpu.VMEM(half_tiles, F32),
            pltpu.VMEM((16, *half_tiles), F32),
            pltpu.VMEM(half_tiles, F32),
            pltpu.VMEM((16, *half_tiles), F32),
            dma((NB,)),
            dma((2,)),
            dma((NC, NB)),
            dma((NC,)),
            dma((NC, NB)),
            dma((NC,)),
            dma((2, 7)),
            dma((2,)),
            dma((2, 3)),
            dma((2,)),
            dma((2, 7)),
            dma((2,)),
            dma((3,)),
            dma,
            dma((2, 7)),
            dma((2,)),
            dma((3, 15)),
            dma((3,)),
        ],
        compiler_params=pltpu.CompilerParams(
            collective_id=0, has_side_effects=True, vmem_limit_bytes=59 * 1024 * 1024
        ),
        cost_estimate=pl.CostEstimate(
            flops=6 * V * POINTS * D, bytes_accessed=5_000_000, transcendentals=8_000_000
        ),
    )(
        counts,
        area,
        offset.reshape(1, V),
        var_weight.reshape(1, V),
        proj_weight,
        hidden_state.reshape(POINTS, D),
        truth,
    )
    factor = GRAD_SCALE / math.sqrt(NB * total_rows * CAP)
    latent, wgrad, bias, loss = pl.pallas_call(
        lambda *refs: finish_kernel(factor, *refs),
        out_shape=(
            jax.ShapeDtypeStruct((POINTS, D), bf16),
            jax.ShapeDtypeStruct((V, D), F32),
            jax.ShapeDtypeStruct((1, V), F32),
            jax.ShapeDtypeStruct((1, 1), F32),
        ),
        in_specs=[vmem, vmem],
        out_specs=(hbm, hbm, vmem, vmem),
        scratch_shapes=[pltpu.VMEM((V, D), F32), dma((5,))],
        compiler_params=pltpu.CompilerParams(vmem_limit_bytes=16 * 1024 * 1024),
        cost_estimate=pl.CostEstimate(flops=V * D, bytes_accessed=5_000_000, transcendentals=0),
    )(latent, sums)
    return latent.reshape(hidden_state.shape), wgrad, bias.reshape(V), loss.reshape(())


def solution(mesh):
    total_rows = ROWS * mesh.shape["space"]

    def step(*args):
        return per_device(*args, total_rows)

    return jax.shard_map(
        step,
        mesh=mesh,
        in_specs=(
            P("member", "space", None, None),
            P(),
            P(),
            P(None, "space", None),
            P("space"),
            P(),
        ),
        out_specs=(P("member", "space", None, None), P(), P(), P()),
        check_vma=False,
    )
```

```python
import math

import numpy as np

import jax
import jax.numpy as jnp
from jax import lax
from jax.experimental import pallas as pl
from jax.experimental.pallas import tpu as pltpu
from jax.sharding import PartitionSpec as P

SMOOTHING = 0.05
FAIRNESS = 0.95
GRAD_SCALE = 16.0
LATITUDE_SPAN = 80.0

V = 100
VP = 104
GP = 112
D = 1024
ROWS = 4
CAP = 512
POINTS = ROWS * CAP
BLOCK = 256
NB = 8
NT = 25
CHUNKS = ((0, 8), (8, 8), (16, 4), (20, 5))
NC = len(CHUNKS)
GROUPS = ((0, 64), (64, 16))
LAST = 80
MESH = pl.DeviceIdType.MESH
F32 = jnp.float32
EPS2 = SMOOTHING * SMOOTHING
COEFF = FAIRNESS / (NB * (NB - 1)) + (1.0 - FAIRNESS) / (NB * NB)


def column(row):
    n = row.shape[1]
    here = lax.broadcasted_iota(jnp.int32, (VP, n), 0) == lax.broadcasted_iota(
        jnp.int32, (VP, n), 1
    )
    return jnp.sum(jnp.where(here, jnp.broadcast_to(row, (VP, n)), 0.0), axis=1, keepdims=True)


def exchange_kernel(
    counts_ref,
    area_ref,
    offset_ref,
    scale_ref,
    weight_hbm,
    hidden_hbm,
    truth_hbm,
    latent_ref,
    sums_ref,
    weight,
    hbuf,
    truth,
    field,
    met,
    signs,
    back,
    obs,
    grad,
    loss_acc,
    bias_acc,
    scale,
    part,
    part_in,
    plane,
    pair,
    y_in,
    z_out,
    z_in,
    own_all,
    out_in,
    last,
    last_in,
    last_mid,
    last_z,
    last_own,
    last_out,
    load_sem,
    side_sem,
    fwd_send,
    fwd_recv,
    ret_send,
    ret_recv,
    part_send,
    part_recv,
    y_send,
    y_recv,
    z_send,
    z_recv,
    row_send,
    row_recv,
    out_send,
    out_recv,
    last_send,
    last_recv,
):
    member = lax.axis_index("member")
    space = lax.axis_index("space")
    y, z_hi = lax.div(member, 2), lax.rem(member, 2)
    z_lo, q = lax.div(space, 8), lax.rem(space, 8)
    x, core = lax.div(q, 2), lax.rem(q, 2)
    z = z_hi * 4 + z_lo
    in_plane = x * 4 + y
    in_stack = z * 2 + core

    def at(xx, yy, zz, cc):
        return (yy * 2 + lax.div(zz, 4), lax.rem(zz, 4) * 8 + xx * 2 + cc)

    def beside(j):
        return at(lax.div(j, 2), y, z, lax.rem(j, 2))

    def plane_device(w):
        return at(lax.div(w, 4), lax.rem(w, 4), z, core)

    def stack_device(u):
        return at(x, y, lax.div(u, 2), lax.rem(u, 2))

    def block_points(b):
        return pl.ds(pl.multiple_of(b * BLOCK, BLOCK), BLOCK)

    def load(t):
        rows = block_points(lax.rem(member + t, NB))
        return pltpu.make_async_copy(hidden_hbm.at[rows], hbuf.at[rows], load_sem.at[t - 1])

    load_weight = pltpu.make_async_copy(weight_hbm, weight, side_sem.at[0])
    load_weight.start()
    for t in range(1, NB + 1):
        load(t).start()
    load_truth = pltpu.make_async_copy(truth_hbm, truth, side_sem.at[1])
    load_truth.start()

    barrier = pltpu.get_barrier_semaphore()

    def greet(device):
        pl.semaphore_signal(barrier, inc=1, device_id=device, device_id_type=MESH)

    for t in range(1, 16):
        greet(plane_device(lax.rem(in_plane + t, 16)))
        greet(stack_device(lax.rem(in_stack + t, 16)))
    for t in range(1, 4):
        greet(at(x, lax.rem(y + t, 4), lax.rem(z + 2, 8), core))
        greet(at(x, lax.rem(y + t, 4), lax.rem(z + 6, 8), core))
        greet(at(lax.rem(x + t, 4), y, z, 1 - core))

    offsets = column(offset_ref[...])[0:V]
    scales = jnp.broadcast_to(column(scale_ref[...]), (VP, 128))
    for i in range(NT // 2):
        scale[2 * i] = scales[8 * i : 8 * i + 8]
        scale[2 * i + 1] = scales[8 * i : 8 * i + 8]
    scale[NT - 1] = jnp.concatenate([scales[96:V], scales[96:V]], axis=0)
    loss_acc[...] = jnp.zeros_like(loss_acc)
    bias_acc[...] = jnp.zeros_like(bias_acc)

    lane = lax.broadcasted_iota(jnp.int32, (1, 128), 1)
    sub = lax.broadcasted_iota(jnp.int32, (8, 128), 0)

    def live(b, h):
        return lane + (lax.rem(b, 2) * 2 + h) * 128 < counts_ref[lax.div(b, 2)]

    def point_weights(b, factor):
        area = area_ref[space * ROWS + lax.div(b, 2)] * factor
        halves = [jnp.where(live(b, h), area, 0.0) for h in range(2)]
        return halves, jnp.where(sub < 4, halves[0], halves[1])

    def send_forecast(c, b):
        block = pl.ds(*CHUNKS[c])
        return pltpu.make_async_remote_copy(
            src_ref=field.at[b, block],
            dst_ref=met.at[member, block],
            send_sem=fwd_send,
            recv_sem=fwd_recv.at[c],
            device_id=at(x, lax.div(b, 2), lax.rem(z_lo + 2 + 4 * lax.rem(b, 2), 8), core),
            device_id_type=MESH,
        )

    for t in range(1, NB + 1):
        load(t).wait()
        if t == 1:
            load_weight.wait()
        b = lax.rem(member + t, NB)
        product = lax.dot_general(
            weight[...],
            hbuf[block_points(b), :],
            (((1,), (1,)), ((), ())),
            preferred_element_type=F32,
        )
        forecast = product + offsets
        halves = [
            jnp.where(live(b, h), forecast[:, h * 128 : (h + 1) * 128], 0.0) for h in range(2)
        ]
        for i in range(NT // 2):
            for h in range(2):
                field[b, 2 * i + h] = halves[h][8 * i : 8 * i + 8]
        field[b, NT - 1] = jnp.concatenate([halves[0][96:V], halves[1][96:V]], axis=0)
        if t == 1:
            pl.semaphore_wait(barrier, 39)
        for c in range(2):
            send_forecast(c, b).start()
    for c in range(2, NC):
        for t in range(1, NB + 1):
            send_forecast(c, lax.rem(member + t, NB)).start()

    load_truth.wait()

    def misfit(b, tile, target, weight_here):
        gap = field[b, tile] - target
        square = gap * gap + EPS2
        inverse = lax.rsqrt(square)
        factor = weight_here * scale[tile]
        obs[b, tile] = factor * (gap * inverse)
        return factor * (square * inverse - SMOOTHING)

    def target(b, v, h):
        first = (b % 2) * BLOCK + h * 128
        return truth[v, b // 2, first : first + 128]

    @pl.loop(0, NT // 2)
    def _(i):
        at_v = pl.ds(pl.multiple_of(i * 8, 8), 8)
        total = jnp.zeros((8, 128), F32)
        for b in range(NB):
            halves, _ = point_weights(b, 1.0 / NB)
            for h in range(2):
                total += misfit(b, 2 * i + h, target(b, at_v, h), halves[h])
        loss_acc[...] += total

    total = jnp.zeros((8, 128), F32)
    for b in range(NB):
        _, both = point_weights(b, 1.0 / NB)
        tail = pl.ds(96, 4)
        goal = jnp.concatenate([target(b, tail, 0), target(b, tail, 1)], axis=0)
        total += misfit(b, NT - 1, goal, both)
    loss_acc[...] += total

    z_from = lax.rem(z + 2, 4)
    block_here = y * 2 + lax.div(lax.rem(z - z_from - 2 + 16, 8), 4)
    space_from = z_from * 8 + q
    area_here = area_ref[space_from * ROWS + y]

    def send_sign(c, m):
        block = pl.ds(*CHUNKS[c])
        return pltpu.make_async_remote_copy(
            src_ref=signs.at[m, block],
            dst_ref=back.at[block_here, block],
            send_sem=ret_send,
            recv_sem=ret_recv.at[c],
            device_id=(m, space_from),
            device_id_type=MESH,
        )

    def arrive(ref, sem):
        pltpu.make_async_copy(ref, ref, sem).wait()

    def meet(block):
        values = [met[m, block] for m in range(NB)]
        sums = [None] * NB
        roots = None
        for m in range(NB):
            for k in range(m + 1, NB):
                gap = values[m] - values[k]
                square = gap * gap + EPS2
                inverse = lax.rsqrt(square)
                sign = gap * inverse
                root = square * inverse
                roots = root if roots is None else roots + root
                sums[m] = sign if sums[m] is None else sums[m] + sign
                sums[k] = -sign if sums[k] is None else sums[k] - sign
        for m in range(NB):
            signs[m, block] = sums[m]
        spread = (roots - (NB * (NB - 1) // 2) * SMOOTHING) * scale[block]
        loss_acc[...] += (-COEFF * area_here) * jnp.sum(spread, axis=0)

    def pairs(c):
        first, n = CHUNKS[c]
        arrive(met.at[:, pl.ds(first, n)], fwd_recv.at[c])

        @pl.loop(0, n // 2)
        def _(i):
            meet(pl.ds(first + 2 * i, 2))

        if n % 2:
            meet(pl.ds(first + n - 1, 1))

        for t in range(1, NB + 1):
            send_sign(c, lax.rem(member + t, NB)).start()

    def gradient(c):
        first, n = CHUNKS[c]
        v0 = 4 * first
        arrive(back.at[:, pl.ds(first, n)], ret_recv.at[c])

        @pl.loop(0, NB)
        def _(b):
            halves, both = point_weights(b, COEFF)

            def value(tile, weight_here):
                result = obs[b, tile] - (weight_here * scale[tile]) * back[b, tile]
                bias_acc[tile] += result
                return result

            pieces = [
                [value(first + 2 * i + h, halves[h]) for i in range(n // 2)] for h in range(2)
            ]
            if n % 2:
                tail = value(NT - 1, both)
                for h in range(2):
                    pieces[h] += [tail[4 * h : 4 * h + 4], jnp.zeros((GP - V, 128), F32)]
            for h in range(2):
                stacked = jnp.concatenate(pieces[h], axis=0)
                points = pl.ds(pl.multiple_of(b * BLOCK + h * 128, 128), 128)
                grad[v0 : v0 + stacked.shape[0], points] = stacked.astype(jnp.bfloat16)

        @pl.loop(0, 4)
        def _(j):
            rows = GP - v0 if n % 2 else 4 * n
            piece = jnp.dot(
                grad[v0 : v0 + rows, :],
                hbuf[:, pl.ds(pl.multiple_of(j * 256, 256), 256)],
                preferred_element_type=F32,
            )
            for k in range(2):
                block = piece[:, k * 128 : (k + 1) * 128]
                if n % 2:
                    for i in range(6):
                        last[4 * j + 2 * k + i // 3, i % 3] = block[4 * i : 4 * i + 4]
                else:
                    part[2 * j + k, v0 : v0 + rows, :] = block

    def extras():
        rows = []
        for i in range(NT // 2):
            rows.append(bias_acc[2 * i] + bias_acc[2 * i + 1])
        tail = bias_acc[NT - 1]
        rows += [tail[0:4] + tail[4:8], jnp.zeros((VP - V, 128), F32)]
        bias = jnp.sum(jnp.concatenate(rows, axis=0), axis=1, keepdims=True)
        eye = lax.broadcasted_iota(jnp.int32, (VP, 128), 0) == lax.broadcasted_iota(
            jnp.int32, (VP, 128), 1
        )
        extra = jnp.sum(jnp.where(eye, bias, 0.0), axis=0, keepdims=True)
        loss_here = jnp.sum(jnp.sum(loss_acc[...], axis=0, keepdims=True), axis=1, keepdims=True)
        points_here = jnp.float32(0.0)
        for r in range(ROWS):
            points_here += area_ref[space * ROWS + r] * counts_ref[r].astype(F32)
        extra = jnp.where(lane == V, loss_here, extra)
        extra = jnp.where(lane == V + 1, points_here, extra)
        last[1, 2, 0:1, :] = extra

    def tiles(g):
        first, n = GROUPS[g]
        return first // 8, (first + n) // 8

    def send_part(g, t):
        rows = pl.ds(*GROUPS[g])
        j = lax.rem(q + t, 8)
        return pltpu.make_async_remote_copy(
            src_ref=part.at[j, rows],
            dst_ref=part_in.at[t - 1, rows],
            send_sem=part_send,
            recv_sem=part_recv.at[g],
            device_id=beside(j),
            device_id_type=MESH,
        )

    def send_plane(g, t):
        yy = lax.rem(y + t, 4)
        return pltpu.make_async_remote_copy(
            src_ref=plane.at[yy] if g == 0 else pair,
            dst_ref=y_in.at[g, y],
            send_sem=y_send.at[g],
            recv_sem=y_recv.at[g],
            device_id=at(x, yy, z, core),
            device_id_type=MESH,
        )

    def send_across(g, t):
        return pltpu.make_async_remote_copy(
            src_ref=z_out.at[g],
            dst_ref=z_in.at[g, z],
            send_sem=z_send.at[g],
            recv_sem=z_recv.at[g],
            device_id=at(x, y, lax.rem(z + t, 8), core),
            device_id_type=MESH,
        )

    def send_row(t):
        block = own_all.at[pl.ds(2 * y, 2)]
        return pltpu.make_async_remote_copy(
            src_ref=block,
            dst_ref=block,
            send_sem=row_send,
            recv_sem=row_recv,
            device_id=at(x, lax.rem(y + t, 4), z, core),
            device_id_type=MESH,
        )

    def send_out(g, t):
        first, end = tiles(g)
        block = pl.ds(first, end - first)
        return pltpu.make_async_remote_copy(
            src_ref=own_all.at[block],
            dst_ref=out_in.at[t, block],
            send_sem=out_send,
            recv_sem=out_recv.at[g],
            device_id=beside(lax.rem(q + t, 8)),
            device_id_type=MESH,
        )

    def send_all(send, number):
        for t in range(1, number):
            send(t).start()

    def send_parts(g):
        send_all(lambda t: send_part(g, t), 8)

    def sum_beside(g):
        arrive(part_in.at[:, pl.ds(*GROUPS[g])], part_recv.at[g])

        def column_sum(o):
            at_v = pl.ds(pl.multiple_of(o * 8, 8), 8)
            value = part[q, at_v, :]
            for t in range(7):
                value += part_in[t, at_v, :]
            return value

        if g == 0:

            @pl.loop(0, 4)
            def _(yy):
                for i in range(2):
                    plane[yy, i] = column_sum(2 * yy + i)

            y_in[g, y] = plane[y]
        else:
            for i in range(2):
                pair[i] = column_sum(8 + i)
            y_in[g, y] = pair[...]
        send_all(lambda t: send_plane(g, t), 4)

    def sum_plane(g):
        arrive(y_in.at[g, pl.ds(0, 3)], y_recv.at[g])
        value = y_in[g, 0]
        for yy in range(1, 4):
            value += y_in[g, yy]
        z_out[g] = value
        z_in[g, z] = value
        send_all(lambda t: send_across(g, t), 8)

    def spread_out(g):
        first, end = tiles(g)
        send_all(lambda t: send_out(g, t), 8)
        out_in[0, first:end] = own_all[first:end]

    def sum_across(g):
        arrive(z_in.at[g, pl.ds(0, 7)], z_recv.at[g])
        value = z_in[g, 0]
        for zz in range(1, 8):
            value += z_in[g, zz]
        if g == 0:
            own_all[pl.ds(2 * y, 2)] = value
            send_all(send_row, 4)
        else:
            own_all[8:10] = value
            spread_out(1)

    def collect_rows():
        arrive(own_all.at[pl.ds(0, 6)], row_recv)
        spread_out(0)

    def collect(g):
        first, end = tiles(g)
        arrive(out_in.at[pl.ds(1, 7), pl.ds(first, end - first)], out_recv.at[g])

        @pl.loop(0, 8)
        def _(t):
            cols = pl.ds(pl.multiple_of(lax.rem(q - t + 8, 8) * 128, 128), 128)
            for o in range(first, end):
                sums_ref[o * 8 : (o + 1) * 8, cols] = out_in[t, o]

    def last_copy(phase, t):
        if phase == 1:
            to = lax.rem(in_stack + t, 16)
            src, dst, device = last_mid, last_z.at[in_stack], stack_device(to)
        else:
            to = lax.rem(in_plane + t, 16)
            src = last.at[to] if phase == 0 else last_own
            dst = (last_in if phase == 0 else last_out).at[in_plane]
            device = plane_device(to)
        return pltpu.make_async_remote_copy(
            src_ref=src,
            dst_ref=dst,
            send_sem=last_send.at[phase],
            recv_sem=last_recv.at[phase],
            device_id=device,
            device_id_type=MESH,
        )

    def last_start(phase):
        send_all(lambda t: last_copy(phase, t), 16)

    def last_sum(phase, source):
        arrive(source.at[pl.ds(0, 15)], last_recv.at[phase])
        value = source[0]
        for t in range(1, 16):
            value += source[t]
        return value

    def last_scatter():
        last_start(0)
        last_in[in_plane] = last[in_plane]

    def last_across():
        value = last_sum(0, last_in)
        last_mid[...] = value
        last_start(1)
        last_z[in_stack] = value

    def last_gather():
        value = last_sum(1, last_z)
        last_own[...] = value
        last_start(2)
        last_out[in_plane] = value

    def last_collect():
        arrive(last_out.at[pl.ds(0, 15)], last_recv.at[2])

        @pl.loop(0, 8)
        def _(j):
            cols = pl.ds(pl.multiple_of(j * 128, 128), 128)
            for i in range(6):
                rows = slice(LAST + 4 * i, LAST + 4 * i + 4)
                sums_ref[rows, cols] = last_out[2 * j + i // 3, i % 3]

    def latent(first, end):
        @pl.loop(first, end)
        def _(b):
            points = block_points(b)
            value = lax.dot_general(
                grad[0:V, points], weight[...], (((0,), (0,)), ((), ())), preferred_element_type=F32
            )
            latent_ref[points, :] = (GRAD_SCALE * value).astype(jnp.bfloat16)

    for c in range(NC):
        pairs(c)
    gradient(0)
    gradient(1)
    send_parts(0)
    gradient(2)
    send_parts(1)
    sum_beside(0)
    gradient(3)
    extras()
    last_scatter()
    sum_plane(0)
    sum_beside(1)
    latent(0, 2)
    last_across()
    sum_across(0)
    sum_plane(1)
    latent(2, 4)
    last_gather()
    collect_rows()
    sum_across(1)
    latent(4, 8)
    last_collect()
    collect(0)
    collect(1)

    arrive(field, fwd_send)
    arrive(signs, ret_send)
    arrive(part.at[pl.ds(0, 7)], part_send)
    arrive(plane.at[pl.ds(0, 3)], y_send.at[0])
    arrive(plane.at[pl.ds(0, 3)], y_send.at[1])
    for g in range(len(GROUPS)):
        arrive(z_in.at[g, pl.ds(0, 7)], z_send.at[g])
    arrive(own_all.at[pl.ds(0, 6)], row_send)
    arrive(out_in.at[pl.ds(0, 7)], out_send)
    for phase in range(3):
        arrive(last.at[pl.ds(0, 15)], last_send.at[phase])


def finish_kernel(factor, latent, sums, latent_hbm, wgrad_hbm, bias_ref, loss_ref, wgrad, sem):
    stores = []
    for b in range(4):
        rows = pl.ds(b * CAP, CAP)
        stores.append(pltpu.make_async_copy(latent.at[rows], latent_hbm.at[rows], sem.at[b]))
        stores[-1].start()
    wgrad[...] = sums[0:V, :] * factor
    stores.append(pltpu.make_async_copy(wgrad, wgrad_hbm, sem.at[4]))
    stores[-1].start()
    extra = sums[V : V + 1, 0:128]
    lane = lax.broadcasted_iota(jnp.int32, (1, 128), 1)
    total = jnp.sum(jnp.where(lane == V, extra, 0.0), axis=1, keepdims=True)
    points = jnp.sum(jnp.where(lane == V + 1, extra, 0.0), axis=1, keepdims=True)
    bias_ref[...] = extra[:, 0:V] * factor
    loss_ref[...] = total / (V * (points * (1.0 / NB)))
    for store in stores:
        store.wait()


def per_device(hidden_state, proj_weight, offset, truth, counts, var_weight, total_rows):
    latitude = (np.arange(total_rows) + 0.5) * (LATITUDE_SPAN / total_rows) * (math.pi / 180.0)
    area = jnp.asarray(np.cos(latitude), dtype=F32)
    vmem = pl.BlockSpec(memory_space=pltpu.VMEM)
    smem = pl.BlockSpec(memory_space=pltpu.SMEM)
    hbm = pl.BlockSpec(memory_space=pltpu.HBM)
    dma = pltpu.SemaphoreType.DMA
    bf16 = jnp.bfloat16
    blocks = pltpu.VMEM((NB, NT, 8, 128), F32)
    half_tiles = (3, 4, 128)
    latent, sums = pl.pallas_call(
        exchange_kernel,
        out_shape=(
            pltpu.VMEM((POINTS, D), bf16),
            pltpu.VMEM((VP, D), F32),
        ),
        in_specs=[smem, smem, vmem, vmem, hbm, hbm, hbm],
        out_specs=(vmem, vmem),
        scratch_shapes=[
            pltpu.VMEM((V, D), bf16),
            pltpu.VMEM((POINTS, D), bf16),
            pltpu.VMEM((V, ROWS, CAP), F32),
            blocks,
            blocks,
            blocks,
            blocks,
            blocks,
            pltpu.VMEM((GP, POINTS), bf16),
            pltpu.VMEM((8, 128), F32),
            pltpu.VMEM((NT, 8, 128), F32),
            pltpu.VMEM((NT, 8, 128), F32),
            pltpu.VMEM((8, LAST, 128), F32),
            pltpu.VMEM((7, LAST, 128), F32),
            pltpu.VMEM((4, 2, 8, 128), F32),
            pltpu.VMEM((2, 8, 128), F32),
            pltpu.VMEM((2, 4, 2, 8, 128), F32),
            pltpu.VMEM((2, 2, 8, 128), F32),
            pltpu.VMEM((2, 8, 2, 8, 128), F32),
            pltpu.VMEM((LAST // 8, 8, 128), F32),
            pltpu.VMEM((8, LAST // 8, 8, 128), F32),
            pltpu.VMEM((16, *half_tiles), F32),
            pltpu.VMEM((16, *half_tiles), F32),
            pltpu.VMEM(half_tiles, F32),
            pltpu.VMEM((16, *half_tiles), F32),
            pltpu.VMEM(half_tiles, F32),
            pltpu.VMEM((16, *half_tiles), F32),
            dma((NB,)),
            dma((2,)),
            dma,
            dma((NC,)),
            dma,
            dma((NC,)),
            dma,
            dma((2,)),
            dma((2,)),
            dma((2,)),
            dma((2,)),
            dma((2,)),
            dma,
            dma,
            dma,
            dma((2,)),
            dma((3,)),
            dma((3,)),
        ],
        compiler_params=pltpu.CompilerParams(
            collective_id=0, has_side_effects=True, vmem_limit_bytes=59 * 1024 * 1024
        ),
        cost_estimate=pl.CostEstimate(
            flops=6 * V * POINTS * D, bytes_accessed=5_000_000, transcendentals=8_000_000
        ),
    )(
        counts,
        area,
        offset.reshape(1, V),
        var_weight.reshape(1, V),
        proj_weight,
        hidden_state.reshape(POINTS, D),
        truth,
    )
    factor = GRAD_SCALE / math.sqrt(NB * total_rows * CAP)
    latent, wgrad, bias, loss = pl.pallas_call(
        lambda *refs: finish_kernel(factor, *refs),
        out_shape=(
            jax.ShapeDtypeStruct((POINTS, D), bf16),
            jax.ShapeDtypeStruct((V, D), F32),
            jax.ShapeDtypeStruct((1, V), F32),
            jax.ShapeDtypeStruct((1, 1), F32),
        ),
        in_specs=[vmem, vmem],
        out_specs=(hbm, hbm, vmem, vmem),
        scratch_shapes=[pltpu.VMEM((V, D), F32), dma((5,))],
        compiler_params=pltpu.CompilerParams(vmem_limit_bytes=16 * 1024 * 1024),
        cost_estimate=pl.CostEstimate(flops=V * D, bytes_accessed=5_000_000, transcendentals=0),
    )(latent, sums)
    return latent.reshape(hidden_state.shape), wgrad, bias.reshape(V), loss.reshape(())


def solution(mesh):
    total_rows = ROWS * mesh.shape["space"]

    def step(*args):
        return per_device(*args, total_rows)

    return jax.shard_map(
        step,
        mesh=mesh,
        in_specs=(
            P("member", "space", None, None),
            P(),
            P(),
            P(None, "space", None),
            P("space"),
            P(),
        ),
        out_specs=(P("member", "space", None, None), P(), P(), P()),
        check_vma=False,
    )
```

```python
import math

import numpy as np

import jax
import jax.numpy as jnp
from jax import lax
from jax.experimental import pallas as pl
from jax.experimental.pallas import tpu as pltpu
from jax.sharding import PartitionSpec as P

SMOOTHING = 0.05
FAIRNESS = 0.95
GRAD_SCALE = 16.0
LATITUDE_SPAN = 80.0

V = 100
VP = 104
GP = 112
D = 1024
ROWS = 4
CAP = 512
POINTS = ROWS * CAP
BLOCK = 256
NB = 8
NT = 25
CHUNKS = ((0, 8), (8, 8), (16, 4), (20, 5))
NC = len(CHUNKS)
GROUPS = ((0, 64), (64, 16))
LAST = 80
MESH = pl.DeviceIdType.MESH
F32 = jnp.float32
EPS2 = SMOOTHING * SMOOTHING
COEFF = FAIRNESS / (NB * (NB - 1)) + (1.0 - FAIRNESS) / (NB * NB)


def column(row):
    n = row.shape[1]
    here = lax.broadcasted_iota(jnp.int32, (VP, n), 0) == lax.broadcasted_iota(
        jnp.int32, (VP, n), 1
    )
    return jnp.sum(jnp.where(here, jnp.broadcast_to(row, (VP, n)), 0.0), axis=1, keepdims=True)


def exchange_kernel(
    counts_ref,
    area_ref,
    offset_ref,
    scale_ref,
    weight_hbm,
    hidden_hbm,
    truth_hbm,
    latent_ref,
    sums_ref,
    weight,
    hbuf,
    truth,
    field,
    met,
    signs,
    back,
    obs,
    grad,
    loss_acc,
    bias_acc,
    scale,
    part,
    part_in,
    plane,
    pair,
    y_in,
    z_out,
    z_in,
    own_all,
    out_in,
    last,
    last_in,
    last_mid,
    last_z,
    last_own,
    last_out,
    load_sem,
    side_sem,
    fwd_send,
    fwd_recv,
    ret_send,
    ret_recv,
    part_send,
    part_recv,
    y_send,
    y_recv,
    z_send,
    z_recv,
    row_send,
    row_recv,
    out_send,
    out_recv,
    last_send,
    last_recv,
):
    member = lax.axis_index("member")
    space = lax.axis_index("space")
    y, z_hi = lax.div(member, 2), lax.rem(member, 2)
    z_lo, q = lax.div(space, 8), lax.rem(space, 8)
    x, core = lax.div(q, 2), lax.rem(q, 2)
    z = z_hi * 4 + z_lo
    in_plane = x * 4 + y
    in_stack = z * 2 + core

    def at(xx, yy, zz, cc):
        return (yy * 2 + lax.div(zz, 4), lax.rem(zz, 4) * 8 + xx * 2 + cc)

    def beside(j):
        return at(lax.div(j, 2), y, z, lax.rem(j, 2))

    def plane_device(w):
        return at(lax.div(w, 4), lax.rem(w, 4), z, core)

    def stack_device(u):
        return at(x, y, lax.div(u, 2), lax.rem(u, 2))

    def block_points(b):
        return pl.ds(pl.multiple_of(b * BLOCK, BLOCK), BLOCK)

    def load(t):
        rows = block_points(lax.rem(member + t, NB))
        return pltpu.make_async_copy(hidden_hbm.at[rows], hbuf.at[rows], load_sem.at[t - 1])

    load_weight = pltpu.make_async_copy(weight_hbm, weight, side_sem.at[0])
    load_weight.start()
    for t in range(1, NB + 1):
        load(t).start()
    load_truth = pltpu.make_async_copy(truth_hbm, truth, side_sem.at[1])
    load_truth.start()

    barrier = pltpu.get_barrier_semaphore()

    def greet(device):
        pl.semaphore_signal(barrier, inc=1, device_id=device, device_id_type=MESH)

    for t in range(1, 16):
        greet(plane_device(lax.rem(in_plane + t, 16)))
        greet(stack_device(lax.rem(in_stack + t, 16)))
    for t in range(1, 4):
        greet(at(x, lax.rem(y + t, 4), lax.rem(z + 2, 8), core))
        greet(at(x, lax.rem(y + t, 4), lax.rem(z + 6, 8), core))
        greet(at(lax.rem(x + t, 4), y, z, 1 - core))

    offsets = column(offset_ref[...])[0:V]
    scales = jnp.broadcast_to(column(scale_ref[...]), (VP, 128))
    for i in range(NT // 2):
        scale[2 * i] = scales[8 * i : 8 * i + 8]
        scale[2 * i + 1] = scales[8 * i : 8 * i + 8]
    scale[NT - 1] = jnp.concatenate([scales[96:V], scales[96:V]], axis=0)
    loss_acc[...] = jnp.zeros_like(loss_acc)
    bias_acc[...] = jnp.zeros_like(bias_acc)

    lane = lax.broadcasted_iota(jnp.int32, (1, 128), 1)
    sub = lax.broadcasted_iota(jnp.int32, (8, 128), 0)

    def live(b, h):
        return lane + (lax.rem(b, 2) * 2 + h) * 128 < counts_ref[lax.div(b, 2)]

    def point_weights(b, factor):
        area = area_ref[space * ROWS + lax.div(b, 2)] * factor
        halves = [jnp.where(live(b, h), area, 0.0) for h in range(2)]
        return halves, jnp.where(sub < 4, halves[0], halves[1])

    def send_forecast(c, b):
        block = pl.ds(*CHUNKS[c])
        return pltpu.make_async_remote_copy(
            src_ref=field.at[b, block],
            dst_ref=met.at[member, block],
            send_sem=fwd_send,
            recv_sem=fwd_recv.at[c],
            device_id=at(x, lax.div(b, 2), lax.rem(z_lo + 2 + 4 * lax.rem(b, 2), 8), core),
            device_id_type=MESH,
        )

    for t in range(1, NB + 1):
        load(t).wait()
        if t == 1:
            load_weight.wait()
        b = lax.rem(member + t, NB)
        product = lax.dot_general(
            weight[...],
            hbuf[block_points(b), :],
            (((1,), (1,)), ((), ())),
            preferred_element_type=F32,
        )
        forecast = product + offsets
        halves = [
            jnp.where(live(b, h), forecast[:, h * 128 : (h + 1) * 128], 0.0) for h in range(2)
        ]
        for i in range(NT // 2):
            for h in range(2):
                field[b, 2 * i + h] = halves[h][8 * i : 8 * i + 8]
        field[b, NT - 1] = jnp.concatenate([halves[0][96:V], halves[1][96:V]], axis=0)
        if t == 1:
            pl.semaphore_wait(barrier, 39)
        for c in range(2):
            send_forecast(c, b).start()
    for c in range(2, NC):
        for t in range(1, NB + 1):
            send_forecast(c, lax.rem(member + t, NB)).start()

    def misfit(b, tile, target, weight_here):
        gap = field[b, tile] - target
        square = gap * gap + EPS2
        inverse = lax.rsqrt(square)
        factor = weight_here * scale[tile]
        obs[b, tile] = factor * (gap * inverse)
        return factor * (square * inverse - SMOOTHING)

    def target(b, v, h):
        first = (b % 2) * BLOCK + h * 128
        return truth[v, b // 2, first : first + 128]

    def misfits():
        load_truth.wait()

        @pl.loop(0, NT // 2)
        def _(i):
            at_v = pl.ds(pl.multiple_of(i * 8, 8), 8)
            total = jnp.zeros((8, 128), F32)
            for b in range(NB):
                halves, _ = point_weights(b, 1.0 / NB)
                for h in range(2):
                    total += misfit(b, 2 * i + h, target(b, at_v, h), halves[h])
            loss_acc[...] += total

        total = jnp.zeros((8, 128), F32)
        for b in range(NB):
            _, both = point_weights(b, 1.0 / NB)
            tail = pl.ds(96, 4)
            goal = jnp.concatenate([target(b, tail, 0), target(b, tail, 1)], axis=0)
            total += misfit(b, NT - 1, goal, both)
        loss_acc[...] += total

    z_from = lax.rem(z + 2, 4)
    block_here = y * 2 + lax.div(lax.rem(z - z_from - 2 + 16, 8), 4)
    space_from = z_from * 8 + q
    area_here = area_ref[space_from * ROWS + y]

    def send_sign(c, m):
        block = pl.ds(*CHUNKS[c])
        return pltpu.make_async_remote_copy(
            src_ref=signs.at[m, block],
            dst_ref=back.at[block_here, block],
            send_sem=ret_send,
            recv_sem=ret_recv.at[c],
            device_id=(m, space_from),
            device_id_type=MESH,
        )

    def arrive(ref, sem):
        pltpu.make_async_copy(ref, ref, sem).wait()

    def meet(block):
        values = [met[m, block] for m in range(NB)]
        sums = [None] * NB
        roots = None
        for m in range(NB):
            for k in range(m + 1, NB):
                gap = values[m] - values[k]
                square = gap * gap + EPS2
                inverse = lax.rsqrt(square)
                sign = gap * inverse
                root = square * inverse
                roots = root if roots is None else roots + root
                sums[m] = sign if sums[m] is None else sums[m] + sign
                sums[k] = -sign if sums[k] is None else sums[k] - sign
        for m in range(NB):
            signs[m, block] = sums[m]
        spread = (roots - (NB * (NB - 1) // 2) * SMOOTHING) * scale[block]
        loss_acc[...] += (-COEFF * area_here) * jnp.sum(spread, axis=0)

    def pairs(c):
        first, n = CHUNKS[c]
        arrive(met.at[:, pl.ds(first, n)], fwd_recv.at[c])

        @pl.loop(0, n // 2)
        def _(i):
            meet(pl.ds(first + 2 * i, 2))

        if n % 2:
            meet(pl.ds(first + n - 1, 1))

        for t in range(1, NB + 1):
            send_sign(c, lax.rem(member + t, NB)).start()

    def gradient(c):
        first, n = CHUNKS[c]
        v0 = 4 * first
        arrive(back.at[:, pl.ds(first, n)], ret_recv.at[c])

        @pl.loop(0, NB)
        def _(b):
            halves, both = point_weights(b, COEFF)

            def value(tile, weight_here):
                result = obs[b, tile] - (weight_here * scale[tile]) * back[b, tile]
                bias_acc[tile] += result
                return result

            pieces = [
                [value(first + 2 * i + h, halves[h]) for i in range(n // 2)] for h in range(2)
            ]
            if n % 2:
                tail = value(NT - 1, both)
                for h in range(2):
                    pieces[h] += [tail[4 * h : 4 * h + 4], jnp.zeros((GP - V, 128), F32)]
            for h in range(2):
                stacked = jnp.concatenate(pieces[h], axis=0)
                points = pl.ds(pl.multiple_of(b * BLOCK + h * 128, 128), 128)
                grad[v0 : v0 + stacked.shape[0], points] = stacked.astype(jnp.bfloat16)

        @pl.loop(0, 4)
        def _(j):
            rows = GP - v0 if n % 2 else 4 * n
            piece = jnp.dot(
                grad[v0 : v0 + rows, :],
                hbuf[:, pl.ds(pl.multiple_of(j * 256, 256), 256)],
                preferred_element_type=F32,
            )
            for k in range(2):
                block = piece[:, k * 128 : (k + 1) * 128]
                if n % 2:
                    for i in range(6):
                        last[4 * j + 2 * k + i // 3, i % 3] = block[4 * i : 4 * i + 4]
                else:
                    part[2 * j + k, v0 : v0 + rows, :] = block

    def extras():
        rows = []
        for i in range(NT // 2):
            rows.append(bias_acc[2 * i] + bias_acc[2 * i + 1])
        tail = bias_acc[NT - 1]
        rows += [tail[0:4] + tail[4:8], jnp.zeros((VP - V, 128), F32)]
        bias = jnp.sum(jnp.concatenate(rows, axis=0), axis=1, keepdims=True)
        eye = lax.broadcasted_iota(jnp.int32, (VP, 128), 0) == lax.broadcasted_iota(
            jnp.int32, (VP, 128), 1
        )
        extra = jnp.sum(jnp.where(eye, bias, 0.0), axis=0, keepdims=True)
        loss_here = jnp.sum(jnp.sum(loss_acc[...], axis=0, keepdims=True), axis=1, keepdims=True)
        points_here = jnp.float32(0.0)
        for r in range(ROWS):
            points_here += area_ref[space * ROWS + r] * counts_ref[r].astype(F32)
        extra = jnp.where(lane == V, loss_here, extra)
        extra = jnp.where(lane == V + 1, points_here, extra)
        last[1, 2, 0:1, :] = extra

    def tiles(g):
        first, n = GROUPS[g]
        return first // 8, (first + n) // 8

    def send_part(g, t):
        rows = pl.ds(*GROUPS[g])
        j = lax.rem(q + t, 8)
        return pltpu.make_async_remote_copy(
            src_ref=part.at[j, rows],
            dst_ref=part_in.at[t - 1, rows],
            send_sem=part_send,
            recv_sem=part_recv.at[g],
            device_id=beside(j),
            device_id_type=MESH,
        )

    def send_plane(g, t):
        yy = lax.rem(y + t, 4)
        return pltpu.make_async_remote_copy(
            src_ref=plane.at[yy] if g == 0 else pair,
            dst_ref=y_in.at[g, y],
            send_sem=y_send.at[g],
            recv_sem=y_recv.at[g],
            device_id=at(x, yy, z, core),
            device_id_type=MESH,
        )

    def send_across(g, t):
        return pltpu.make_async_remote_copy(
            src_ref=z_out.at[g],
            dst_ref=z_in.at[g, z],
            send_sem=z_send.at[g],
            recv_sem=z_recv.at[g],
            device_id=at(x, y, lax.rem(z + t, 8), core),
            device_id_type=MESH,
        )

    def send_row(t):
        block = own_all.at[pl.ds(2 * y, 2)]
        return pltpu.make_async_remote_copy(
            src_ref=block,
            dst_ref=block,
            send_sem=row_send,
            recv_sem=row_recv,
            device_id=at(x, lax.rem(y + t, 4), z, core),
            device_id_type=MESH,
        )

    def send_out(g, t):
        first, end = tiles(g)
        block = pl.ds(first, end - first)
        return pltpu.make_async_remote_copy(
            src_ref=own_all.at[block],
            dst_ref=out_in.at[t, block],
            send_sem=out_send,
            recv_sem=out_recv.at[g],
            device_id=beside(lax.rem(q + t, 8)),
            device_id_type=MESH,
        )

    def send_all(send, number):
        for t in range(1, number):
            send(t).start()

    def send_parts(g):
        send_all(lambda t: send_part(g, t), 8)

    def sum_beside(g):
        arrive(part_in.at[:, pl.ds(*GROUPS[g])], part_recv.at[g])

        def column_sum(o):
            at_v = pl.ds(pl.multiple_of(o * 8, 8), 8)
            value = part[q, at_v, :]
            for t in range(7):
                value += part_in[t, at_v, :]
            return value

        if g == 0:

            @pl.loop(0, 4)
            def _(yy):
                for i in range(2):
                    plane[yy, i] = column_sum(2 * yy + i)

            y_in[g, y] = plane[y]
        else:
            for i in range(2):
                pair[i] = column_sum(8 + i)
            y_in[g, y] = pair[...]
        send_all(lambda t: send_plane(g, t), 4)

    def sum_plane(g):
        arrive(y_in.at[g, pl.ds(0, 3)], y_recv.at[g])
        value = y_in[g, 0]
        for yy in range(1, 4):
            value += y_in[g, yy]
        z_out[g] = value
        z_in[g, z] = value
        send_all(lambda t: send_across(g, t), 8)

    def spread_out(g):
        first, end = tiles(g)
        send_all(lambda t: send_out(g, t), 8)
        out_in[0, first:end] = own_all[first:end]

    def sum_across(g):
        arrive(z_in.at[g, pl.ds(0, 7)], z_recv.at[g])
        value = z_in[g, 0]
        for zz in range(1, 8):
            value += z_in[g, zz]
        if g == 0:
            own_all[pl.ds(2 * y, 2)] = value
            send_all(send_row, 4)
        else:
            own_all[8:10] = value
            spread_out(1)

    def collect_rows():
        arrive(own_all.at[pl.ds(0, 6)], row_recv)
        spread_out(0)

    def collect(g):
        first, end = tiles(g)
        arrive(out_in.at[pl.ds(1, 7), pl.ds(first, end - first)], out_recv.at[g])

        @pl.loop(0, 8)
        def _(t):
            cols = pl.ds(pl.multiple_of(lax.rem(q - t + 8, 8) * 128, 128), 128)
            for o in range(first, end):
                sums_ref[o * 8 : (o + 1) * 8, cols] = out_in[t, o]

    def last_copy(phase, t):
        if phase == 1:
            to = lax.rem(in_stack + t, 16)
            src, dst, device = last_mid, last_z.at[in_stack], stack_device(to)
        else:
            to = lax.rem(in_plane + t, 16)
            src = last.at[to] if phase == 0 else last_own
            dst = (last_in if phase == 0 else last_out).at[in_plane]
            device = plane_device(to)
        return pltpu.make_async_remote_copy(
            src_ref=src,
            dst_ref=dst,
            send_sem=last_send.at[phase],
            recv_sem=last_recv.at[phase],
            device_id=device,
            device_id_type=MESH,
        )

    def last_start(phase):
        send_all(lambda t: last_copy(phase, t), 16)

    def last_sum(phase, source):
        arrive(source.at[pl.ds(0, 15)], last_recv.at[phase])
        value = source[0]
        for t in range(1, 16):
            value += source[t]
        return value

    def last_scatter():
        last_start(0)
        last_in[in_plane] = last[in_plane]

    def last_across():
        value = last_sum(0, last_in)
        last_mid[...] = value
        last_start(1)
        last_z[in_stack] = value

    def last_gather():
        value = last_sum(1, last_z)
        last_own[...] = value
        last_start(2)
        last_out[in_plane] = value

    def last_collect():
        arrive(last_out.at[pl.ds(0, 15)], last_recv.at[2])

        @pl.loop(0, 8)
        def _(j):
            cols = pl.ds(pl.multiple_of(j * 128, 128), 128)
            for i in range(6):
                rows = slice(LAST + 4 * i, LAST + 4 * i + 4)
                sums_ref[rows, cols] = last_out[2 * j + i // 3, i % 3]

    def latent(first, end):
        @pl.loop(first, end)
        def _(b):
            points = block_points(b)
            value = lax.dot_general(
                grad[0:V, points], weight[...], (((0,), (0,)), ((), ())), preferred_element_type=F32
            )
            latent_ref[points, :] = (GRAD_SCALE * value).astype(jnp.bfloat16)

    pairs(0)
    pairs(1)
    misfits()
    pairs(2)
    pairs(3)
    gradient(0)
    gradient(1)
    send_parts(0)
    gradient(2)
    send_parts(1)
    sum_beside(0)
    gradient(3)
    extras()
    last_scatter()
    sum_plane(0)
    sum_beside(1)
    latent(0, 2)
    last_across()
    sum_across(0)
    sum_plane(1)
    latent(2, 4)
    last_gather()
    collect_rows()
    sum_across(1)
    latent(4, 8)
    last_collect()
    collect(0)
    collect(1)

    arrive(field, fwd_send)
    arrive(signs, ret_send)
    arrive(part.at[pl.ds(0, 7)], part_send)
    arrive(plane.at[pl.ds(0, 3)], y_send.at[0])
    arrive(plane.at[pl.ds(0, 3)], y_send.at[1])
    for g in range(len(GROUPS)):
        arrive(z_in.at[g, pl.ds(0, 7)], z_send.at[g])
    arrive(own_all.at[pl.ds(0, 6)], row_send)
    arrive(out_in.at[pl.ds(0, 7)], out_send)
    for phase in range(3):
        arrive(last.at[pl.ds(0, 15)], last_send.at[phase])


def finish_kernel(factor, latent, sums, latent_hbm, wgrad_hbm, bias_ref, loss_ref, wgrad, sem):
    stores = []
    for b in range(4):
        rows = pl.ds(b * CAP, CAP)
        stores.append(pltpu.make_async_copy(latent.at[rows], latent_hbm.at[rows], sem.at[b]))
        stores[-1].start()
    wgrad[...] = sums[0:V, :] * factor
    stores.append(pltpu.make_async_copy(wgrad, wgrad_hbm, sem.at[4]))
    stores[-1].start()
    extra = sums[V : V + 1, 0:128]
    lane = lax.broadcasted_iota(jnp.int32, (1, 128), 1)
    total = jnp.sum(jnp.where(lane == V, extra, 0.0), axis=1, keepdims=True)
    points = jnp.sum(jnp.where(lane == V + 1, extra, 0.0), axis=1, keepdims=True)
    bias_ref[...] = extra[:, 0:V] * factor
    loss_ref[...] = total / (V * (points * (1.0 / NB)))
    for store in stores:
        store.wait()


def per_device(hidden_state, proj_weight, offset, truth, counts, var_weight, total_rows):
    latitude = (np.arange(total_rows) + 0.5) * (LATITUDE_SPAN / total_rows) * (math.pi / 180.0)
    area = jnp.asarray(np.cos(latitude), dtype=F32)
    vmem = pl.BlockSpec(memory_space=pltpu.VMEM)
    smem = pl.BlockSpec(memory_space=pltpu.SMEM)
    hbm = pl.BlockSpec(memory_space=pltpu.HBM)
    dma = pltpu.SemaphoreType.DMA
    bf16 = jnp.bfloat16
    blocks = pltpu.VMEM((NB, NT, 8, 128), F32)
    half_tiles = (3, 4, 128)
    latent, sums = pl.pallas_call(
        exchange_kernel,
        out_shape=(
            pltpu.VMEM((POINTS, D), bf16),
            pltpu.VMEM((VP, D), F32),
        ),
        in_specs=[smem, smem, vmem, vmem, hbm, hbm, hbm],
        out_specs=(vmem, vmem),
        scratch_shapes=[
            pltpu.VMEM((V, D), bf16),
            pltpu.VMEM((POINTS, D), bf16),
            pltpu.VMEM((V, ROWS, CAP), F32),
            blocks,
            blocks,
            blocks,
            blocks,
            blocks,
            pltpu.VMEM((GP, POINTS), bf16),
            pltpu.VMEM((8, 128), F32),
            pltpu.VMEM((NT, 8, 128), F32),
            pltpu.VMEM((NT, 8, 128), F32),
            pltpu.VMEM((8, LAST, 128), F32),
            pltpu.VMEM((7, LAST, 128), F32),
            pltpu.VMEM((4, 2, 8, 128), F32),
            pltpu.VMEM((2, 8, 128), F32),
            pltpu.VMEM((2, 4, 2, 8, 128), F32),
            pltpu.VMEM((2, 2, 8, 128), F32),
            pltpu.VMEM((2, 8, 2, 8, 128), F32),
            pltpu.VMEM((LAST // 8, 8, 128), F32),
            pltpu.VMEM((8, LAST // 8, 8, 128), F32),
            pltpu.VMEM((16, *half_tiles), F32),
            pltpu.VMEM((16, *half_tiles), F32),
            pltpu.VMEM(half_tiles, F32),
            pltpu.VMEM((16, *half_tiles), F32),
            pltpu.VMEM(half_tiles, F32),
            pltpu.VMEM((16, *half_tiles), F32),
            dma((NB,)),
            dma((2,)),
            dma,
            dma((NC,)),
            dma,
            dma((NC,)),
            dma,
            dma((2,)),
            dma((2,)),
            dma((2,)),
            dma((2,)),
            dma((2,)),
            dma,
            dma,
            dma,
            dma((2,)),
            dma((3,)),
            dma((3,)),
        ],
        compiler_params=pltpu.CompilerParams(
            collective_id=0, has_side_effects=True, vmem_limit_bytes=59 * 1024 * 1024
        ),
        cost_estimate=pl.CostEstimate(
            flops=6 * V * POINTS * D, bytes_accessed=5_000_000, transcendentals=8_000_000
        ),
    )(
        counts,
        area,
        offset.reshape(1, V),
        var_weight.reshape(1, V),
        proj_weight,
        hidden_state.reshape(POINTS, D),
        truth,
    )
    factor = GRAD_SCALE / math.sqrt(NB * total_rows * CAP)
    latent, wgrad, bias, loss = pl.pallas_call(
        lambda *refs: finish_kernel(factor, *refs),
        out_shape=(
            jax.ShapeDtypeStruct((POINTS, D), bf16),
            jax.ShapeDtypeStruct((V, D), F32),
            jax.ShapeDtypeStruct((1, V), F32),
            jax.ShapeDtypeStruct((1, 1), F32),
        ),
        in_specs=[vmem, vmem],
        out_specs=(hbm, hbm, vmem, vmem),
        scratch_shapes=[pltpu.VMEM((V, D), F32), dma((5,))],
        compiler_params=pltpu.CompilerParams(vmem_limit_bytes=16 * 1024 * 1024),
        cost_estimate=pl.CostEstimate(flops=V * D, bytes_accessed=5_000_000, transcendentals=0),
    )(latent, sums)
    return latent.reshape(hidden_state.shape), wgrad, bias.reshape(V), loss.reshape(())


def solution(mesh):
    total_rows = ROWS * mesh.shape["space"]

    def step(*args):
        return per_device(*args, total_rows)

    return jax.shard_map(
        step,
        mesh=mesh,
        in_specs=(
            P("member", "space", None, None),
            P(),
            P(),
            P(None, "space", None),
            P("space"),
            P(),
        ),
        out_specs=(P("member", "space", None, None), P(), P(), P()),
        check_vma=False,
    )
```

```python
import math

import numpy as np

import jax
import jax.numpy as jnp
from jax import lax
from jax.experimental import pallas as pl
from jax.experimental.pallas import tpu as pltpu
from jax.sharding import PartitionSpec as P

SMOOTHING = 0.05
FAIRNESS = 0.95
GRAD_SCALE = 16.0
LATITUDE_SPAN = 80.0

V = 100
VP = 104
GP = 112
D = 1024
ROWS = 4
CAP = 512
POINTS = ROWS * CAP
BLOCK = 256
NB = 8
NT = 25
CHUNKS = ((0, 16), (16, 4), (20, 5))
NC = len(CHUNKS)
GROUPS = ((0, 64), (64, 16))
LAST = 80
MESH = pl.DeviceIdType.MESH
F32 = jnp.float32
EPS2 = SMOOTHING * SMOOTHING
COEFF = FAIRNESS / (NB * (NB - 1)) + (1.0 - FAIRNESS) / (NB * NB)


def column(row):
    n = row.shape[1]
    here = lax.broadcasted_iota(jnp.int32, (VP, n), 0) == lax.broadcasted_iota(
        jnp.int32, (VP, n), 1
    )
    return jnp.sum(jnp.where(here, jnp.broadcast_to(row, (VP, n)), 0.0), axis=1, keepdims=True)


def exchange_kernel(
    counts_ref,
    area_ref,
    offset_ref,
    scale_ref,
    weight_hbm,
    hidden_hbm,
    truth_hbm,
    latent_ref,
    sums_ref,
    weight,
    hbuf,
    truth,
    field,
    met,
    signs,
    back,
    obs,
    grad,
    loss_acc,
    bias_acc,
    scale,
    part,
    part_in,
    plane,
    pair,
    y_in,
    z_out,
    z_in,
    own_all,
    out_in,
    last,
    last_in,
    last_mid,
    last_z,
    last_own,
    last_out,
    load_sem,
    side_sem,
    fwd_send,
    fwd_recv,
    ret_send,
    ret_recv,
    part_send,
    part_recv,
    y_send,
    y_recv,
    z_send,
    z_recv,
    row_send,
    row_recv,
    out_send,
    out_recv,
    last_send,
    last_recv,
):
    member = lax.axis_index("member")
    space = lax.axis_index("space")
    y, z_hi = lax.div(member, 2), lax.rem(member, 2)
    z_lo, q = lax.div(space, 8), lax.rem(space, 8)
    x, core = lax.div(q, 2), lax.rem(q, 2)
    z = z_hi * 4 + z_lo
    in_plane = x * 4 + y
    in_stack = z * 2 + core

    def at(xx, yy, zz, cc):
        return (yy * 2 + lax.div(zz, 4), lax.rem(zz, 4) * 8 + xx * 2 + cc)

    def beside(j):
        return at(lax.div(j, 2), y, z, lax.rem(j, 2))

    def plane_device(w):
        return at(lax.div(w, 4), lax.rem(w, 4), z, core)

    def stack_device(u):
        return at(x, y, lax.div(u, 2), lax.rem(u, 2))

    def block_points(b):
        return pl.ds(pl.multiple_of(b * BLOCK, BLOCK), BLOCK)

    def load(t):
        rows = block_points(lax.rem(member + t, NB))
        return pltpu.make_async_copy(hidden_hbm.at[rows], hbuf.at[rows], load_sem.at[t - 1])

    load_weight = pltpu.make_async_copy(weight_hbm, weight, side_sem.at[0])
    load_weight.start()
    for t in range(1, NB + 1):
        load(t).start()
    load_truth = pltpu.make_async_copy(truth_hbm, truth, side_sem.at[1])
    load_truth.start()

    barrier = pltpu.get_barrier_semaphore()

    def greet(device):
        pl.semaphore_signal(barrier, inc=1, device_id=device, device_id_type=MESH)

    for t in range(1, 16):
        greet(plane_device(lax.rem(in_plane + t, 16)))
        greet(stack_device(lax.rem(in_stack + t, 16)))
    for t in range(1, 4):
        greet(at(x, lax.rem(y + t, 4), lax.rem(z + 2, 8), core))
        greet(at(x, lax.rem(y + t, 4), lax.rem(z + 6, 8), core))
        greet(at(lax.rem(x + t, 4), y, z, 1 - core))

    offsets = column(offset_ref[...])[0:V]
    scales = jnp.broadcast_to(column(scale_ref[...]), (VP, 128))
    for i in range(NT // 2):
        scale[2 * i] = scales[8 * i : 8 * i + 8]
        scale[2 * i + 1] = scales[8 * i : 8 * i + 8]
    scale[NT - 1] = jnp.concatenate([scales[96:V], scales[96:V]], axis=0)
    loss_acc[...] = jnp.zeros_like(loss_acc)
    bias_acc[...] = jnp.zeros_like(bias_acc)

    lane = lax.broadcasted_iota(jnp.int32, (1, 128), 1)
    sub = lax.broadcasted_iota(jnp.int32, (8, 128), 0)

    def live(b, h):
        return lane + (lax.rem(b, 2) * 2 + h) * 128 < counts_ref[lax.div(b, 2)]

    def point_weights(b, factor):
        area = area_ref[space * ROWS + lax.div(b, 2)] * factor
        halves = [jnp.where(live(b, h), area, 0.0) for h in range(2)]
        return halves, jnp.where(sub < 4, halves[0], halves[1])

    def send_forecast(c, b):
        block = pl.ds(*CHUNKS[c])
        return pltpu.make_async_remote_copy(
            src_ref=field.at[b, block],
            dst_ref=met.at[member, block],
            send_sem=fwd_send,
            recv_sem=fwd_recv.at[c],
            device_id=at(x, lax.div(b, 2), lax.rem(z_lo + 2 + 4 * lax.rem(b, 2), 8), core),
            device_id_type=MESH,
        )

    for t in range(1, NB + 1):
        load(t).wait()
        if t == 1:
            load_weight.wait()
        b = lax.rem(member + t, NB)
        product = lax.dot_general(
            weight[...],
            hbuf[block_points(b), :],
            (((1,), (1,)), ((), ())),
            preferred_element_type=F32,
        )
        forecast = product + offsets
        halves = [
            jnp.where(live(b, h), forecast[:, h * 128 : (h + 1) * 128], 0.0) for h in range(2)
        ]
        for i in range(NT // 2):
            for h in range(2):
                field[b, 2 * i + h] = halves[h][8 * i : 8 * i + 8]
        field[b, NT - 1] = jnp.concatenate([halves[0][96:V], halves[1][96:V]], axis=0)
        if t == 1:
            pl.semaphore_wait(barrier, 39)
        send_forecast(0, b).start()
    for c in range(1, NC):
        for t in range(1, NB + 1):
            send_forecast(c, lax.rem(member + t, NB)).start()

    def misfit(b, tile, target, weight_here):
        gap = field[b, tile] - target
        square = gap * gap + EPS2
        inverse = lax.rsqrt(square)
        factor = weight_here * scale[tile]
        obs[b, tile] = factor * (gap * inverse)
        return factor * (square * inverse - SMOOTHING)

    def target(b, v, h):
        first = (b % 2) * BLOCK + h * 128
        return truth[v, b // 2, first : first + 128]

    def misfits():
        load_truth.wait()

        @pl.loop(0, NT // 2)
        def _(i):
            at_v = pl.ds(pl.multiple_of(i * 8, 8), 8)
            total = jnp.zeros((8, 128), F32)
            for b in range(NB):
                halves, _ = point_weights(b, 1.0 / NB)
                for h in range(2):
                    total += misfit(b, 2 * i + h, target(b, at_v, h), halves[h])
            loss_acc[...] += total

        total = jnp.zeros((8, 128), F32)
        for b in range(NB):
            _, both = point_weights(b, 1.0 / NB)
            tail = pl.ds(96, 4)
            goal = jnp.concatenate([target(b, tail, 0), target(b, tail, 1)], axis=0)
            total += misfit(b, NT - 1, goal, both)
        loss_acc[...] += total

    z_from = lax.rem(z + 2, 4)
    block_here = y * 2 + lax.div(lax.rem(z - z_from - 2 + 16, 8), 4)
    space_from = z_from * 8 + q
    area_here = area_ref[space_from * ROWS + y]

    def send_sign(c, m):
        block = pl.ds(*CHUNKS[c])
        return pltpu.make_async_remote_copy(
            src_ref=signs.at[m, block],
            dst_ref=back.at[block_here, block],
            send_sem=ret_send,
            recv_sem=ret_recv.at[c],
            device_id=(m, space_from),
            device_id_type=MESH,
        )

    def arrive(ref, sem):
        pltpu.make_async_copy(ref, ref, sem).wait()

    def meet(block):
        values = [met[m, block] for m in range(NB)]
        sums = [None] * NB
        roots = None
        for m in range(NB):
            for k in range(m + 1, NB):
                gap = values[m] - values[k]
                square = gap * gap + EPS2
                inverse = lax.rsqrt(square)
                sign = gap * inverse
                root = square * inverse
                roots = root if roots is None else roots + root
                sums[m] = sign if sums[m] is None else sums[m] + sign
                sums[k] = -sign if sums[k] is None else sums[k] - sign
        for m in range(NB):
            signs[m, block] = sums[m]
        spread = (roots - (NB * (NB - 1) // 2) * SMOOTHING) * scale[block]
        loss_acc[...] += (-COEFF * area_here) * jnp.sum(spread, axis=0)

    def pairs(c):
        first, n = CHUNKS[c]
        arrive(met.at[:, pl.ds(first, n)], fwd_recv.at[c])

        @pl.loop(0, n // 2)
        def _(i):
            meet(pl.ds(first + 2 * i, 2))

        if n % 2:
            meet(pl.ds(first + n - 1, 1))

        for t in range(1, NB + 1):
            send_sign(c, lax.rem(member + t, NB)).start()

    def gradient(c):
        first, n = CHUNKS[c]
        v0 = 4 * first
        arrive(back.at[:, pl.ds(first, n)], ret_recv.at[c])

        @pl.loop(0, NB)
        def _(b):
            halves, both = point_weights(b, COEFF)

            def value(tile, weight_here):
                result = obs[b, tile] - (weight_here * scale[tile]) * back[b, tile]
                bias_acc[tile] += result
                return result

            pieces = [
                [value(first + 2 * i + h, halves[h]) for i in range(n // 2)] for h in range(2)
            ]
            if n % 2:
                tail = value(NT - 1, both)
                for h in range(2):
                    pieces[h] += [tail[4 * h : 4 * h + 4], jnp.zeros((GP - V, 128), F32)]
            for h in range(2):
                stacked = jnp.concatenate(pieces[h], axis=0)
                points = pl.ds(pl.multiple_of(b * BLOCK + h * 128, 128), 128)
                grad[v0 : v0 + stacked.shape[0], points] = stacked.astype(jnp.bfloat16)

        @pl.loop(0, 4)
        def _(j):
            rows = GP - v0 if n % 2 else 4 * n
            piece = jnp.dot(
                grad[v0 : v0 + rows, :],
                hbuf[:, pl.ds(pl.multiple_of(j * 256, 256), 256)],
                preferred_element_type=F32,
            )
            for k in range(2):
                block = piece[:, k * 128 : (k + 1) * 128]
                if n % 2:
                    for i in range(6):
                        last[4 * j + 2 * k + i // 3, i % 3] = block[4 * i : 4 * i + 4]
                else:
                    part[2 * j + k, v0 : v0 + rows, :] = block

    def extras():
        rows = []
        for i in range(NT // 2):
            rows.append(bias_acc[2 * i] + bias_acc[2 * i + 1])
        tail = bias_acc[NT - 1]
        rows += [tail[0:4] + tail[4:8], jnp.zeros((VP - V, 128), F32)]
        bias = jnp.sum(jnp.concatenate(rows, axis=0), axis=1, keepdims=True)
        eye = lax.broadcasted_iota(jnp.int32, (VP, 128), 0) == lax.broadcasted_iota(
            jnp.int32, (VP, 128), 1
        )
        extra = jnp.sum(jnp.where(eye, bias, 0.0), axis=0, keepdims=True)
        loss_here = jnp.sum(jnp.sum(loss_acc[...], axis=0, keepdims=True), axis=1, keepdims=True)
        points_here = jnp.float32(0.0)
        for r in range(ROWS):
            points_here += area_ref[space * ROWS + r] * counts_ref[r].astype(F32)
        extra = jnp.where(lane == V, loss_here, extra)
        extra = jnp.where(lane == V + 1, points_here, extra)
        last[1, 2, 0:1, :] = extra

    def tiles(g):
        first, n = GROUPS[g]
        return first // 8, (first + n) // 8

    def send_part(g, t):
        rows = pl.ds(*GROUPS[g])
        j = lax.rem(q + t, 8)
        return pltpu.make_async_remote_copy(
            src_ref=part.at[j, rows],
            dst_ref=part_in.at[t - 1, rows],
            send_sem=part_send,
            recv_sem=part_recv.at[g],
            device_id=beside(j),
            device_id_type=MESH,
        )

    def send_plane(g, t):
        yy = lax.rem(y + t, 4)
        return pltpu.make_async_remote_copy(
            src_ref=plane.at[yy] if g == 0 else pair,
            dst_ref=y_in.at[g, y],
            send_sem=y_send.at[g],
            recv_sem=y_recv.at[g],
            device_id=at(x, yy, z, core),
            device_id_type=MESH,
        )

    def send_across(g, t):
        return pltpu.make_async_remote_copy(
            src_ref=z_out.at[g],
            dst_ref=z_in.at[g, z],
            send_sem=z_send.at[g],
            recv_sem=z_recv.at[g],
            device_id=at(x, y, lax.rem(z + t, 8), core),
            device_id_type=MESH,
        )

    def send_row(t):
        block = own_all.at[pl.ds(2 * y, 2)]
        return pltpu.make_async_remote_copy(
            src_ref=block,
            dst_ref=block,
            send_sem=row_send,
            recv_sem=row_recv,
            device_id=at(x, lax.rem(y + t, 4), z, core),
            device_id_type=MESH,
        )

    def send_out(g, t):
        first, end = tiles(g)
        block = pl.ds(first, end - first)
        return pltpu.make_async_remote_copy(
            src_ref=own_all.at[block],
            dst_ref=out_in.at[t, block],
            send_sem=out_send,
            recv_sem=out_recv.at[g],
            device_id=beside(lax.rem(q + t, 8)),
            device_id_type=MESH,
        )

    def send_all(send, number):
        for t in range(1, number):
            send(t).start()

    def send_parts(g):
        send_all(lambda t: send_part(g, t), 8)

    def sum_beside(g):
        arrive(part_in.at[:, pl.ds(*GROUPS[g])], part_recv.at[g])

        def column_sum(o):
            at_v = pl.ds(pl.multiple_of(o * 8, 8), 8)
            value = part[q, at_v, :]
            for t in range(7):
                value += part_in[t, at_v, :]
            return value

        if g == 0:

            @pl.loop(0, 4)
            def _(yy):
                for i in range(2):
                    plane[yy, i] = column_sum(2 * yy + i)

            y_in[g, y] = plane[y]
        else:
            for i in range(2):
                pair[i] = column_sum(8 + i)
            y_in[g, y] = pair[...]
        send_all(lambda t: send_plane(g, t), 4)

    def sum_plane(g):
        arrive(y_in.at[g, pl.ds(0, 3)], y_recv.at[g])
        value = y_in[g, 0]
        for yy in range(1, 4):
            value += y_in[g, yy]
        z_out[g] = value
        z_in[g, z] = value
        send_all(lambda t: send_across(g, t), 8)

    def spread_out(g):
        first, end = tiles(g)
        send_all(lambda t: send_out(g, t), 8)
        out_in[0, first:end] = own_all[first:end]

    def sum_across(g):
        arrive(z_in.at[g, pl.ds(0, 7)], z_recv.at[g])
        value = z_in[g, 0]
        for zz in range(1, 8):
            value += z_in[g, zz]
        if g == 0:
            own_all[pl.ds(2 * y, 2)] = value
            send_all(send_row, 4)
        else:
            own_all[8:10] = value
            spread_out(1)

    def collect_rows():
        arrive(own_all.at[pl.ds(0, 6)], row_recv)
        spread_out(0)

    def collect(g):
        first, end = tiles(g)
        arrive(out_in.at[pl.ds(1, 7), pl.ds(first, end - first)], out_recv.at[g])

        @pl.loop(0, 8)
        def _(t):
            cols = pl.ds(pl.multiple_of(lax.rem(q - t + 8, 8) * 128, 128), 128)
            for o in range(first, end):
                sums_ref[o * 8 : (o + 1) * 8, cols] = out_in[t, o]

    def last_copy(phase, t):
        if phase == 1:
            to = lax.rem(in_stack + t, 16)
            src, dst, device = last_mid, last_z.at[in_stack], stack_device(to)
        else:
            to = lax.rem(in_plane + t, 16)
            src = last.at[to] if phase == 0 else last_own
            dst = (last_in if phase == 0 else last_out).at[in_plane]
            device = plane_device(to)
        return pltpu.make_async_remote_copy(
            src_ref=src,
            dst_ref=dst,
            send_sem=last_send.at[phase],
            recv_sem=last_recv.at[phase],
            device_id=device,
            device_id_type=MESH,
        )

    def last_start(phase):
        send_all(lambda t: last_copy(phase, t), 16)

    def last_sum(phase, source):
        arrive(source.at[pl.ds(0, 15)], last_recv.at[phase])
        value = source[0]
        for t in range(1, 16):
            value += source[t]
        return value

    def last_scatter():
        last_start(0)
        last_in[in_plane] = last[in_plane]

    def last_across():
        value = last_sum(0, last_in)
        last_mid[...] = value
        last_start(1)
        last_z[in_stack] = value

    def last_gather():
        value = last_sum(1, last_z)
        last_own[...] = value
        last_start(2)
        last_out[in_plane] = value

    def last_collect():
        arrive(last_out.at[pl.ds(0, 15)], last_recv.at[2])

        @pl.loop(0, 8)
        def _(j):
            cols = pl.ds(pl.multiple_of(j * 128, 128), 128)
            for i in range(6):
                rows = slice(LAST + 4 * i, LAST + 4 * i + 4)
                sums_ref[rows, cols] = last_out[2 * j + i // 3, i % 3]

    def latent(first, end):
        @pl.loop(first, end)
        def _(b):
            points = block_points(b)
            value = lax.dot_general(
                grad[0:V, points], weight[...], (((0,), (0,)), ((), ())), preferred_element_type=F32
            )
            latent_ref[points, :] = (GRAD_SCALE * value).astype(jnp.bfloat16)

    pairs(0)
    misfits()
    pairs(1)
    pairs(2)
    gradient(0)
    send_parts(0)
    gradient(1)
    send_parts(1)
    sum_beside(0)
    gradient(2)
    extras()
    last_scatter()
    sum_plane(0)
    sum_beside(1)
    latent(0, 2)
    last_across()
    sum_across(0)
    sum_plane(1)
    latent(2, 4)
    last_gather()
    collect_rows()
    sum_across(1)
    latent(4, 8)
    last_collect()
    collect(0)
    collect(1)

    arrive(field, fwd_send)
    arrive(signs, ret_send)
    arrive(part.at[pl.ds(0, 7)], part_send)
    arrive(plane.at[pl.ds(0, 3)], y_send.at[0])
    arrive(plane.at[pl.ds(0, 3)], y_send.at[1])
    for g in range(len(GROUPS)):
        arrive(z_in.at[g, pl.ds(0, 7)], z_send.at[g])
    arrive(own_all.at[pl.ds(0, 6)], row_send)
    arrive(out_in.at[pl.ds(0, 7)], out_send)
    for phase in range(3):
        arrive(last.at[pl.ds(0, 15)], last_send.at[phase])


def finish_kernel(factor, latent, sums, latent_hbm, wgrad_hbm, bias_ref, loss_ref, wgrad, sem):
    stores = []
    for b in range(4):
        rows = pl.ds(b * CAP, CAP)
        stores.append(pltpu.make_async_copy(latent.at[rows], latent_hbm.at[rows], sem.at[b]))
        stores[-1].start()
    wgrad[...] = sums[0:V, :] * factor
    stores.append(pltpu.make_async_copy(wgrad, wgrad_hbm, sem.at[4]))
    stores[-1].start()
    extra = sums[V : V + 1, 0:128]
    lane = lax.broadcasted_iota(jnp.int32, (1, 128), 1)
    total = jnp.sum(jnp.where(lane == V, extra, 0.0), axis=1, keepdims=True)
    points = jnp.sum(jnp.where(lane == V + 1, extra, 0.0), axis=1, keepdims=True)
    bias_ref[...] = extra[:, 0:V] * factor
    loss_ref[...] = total / (V * (points * (1.0 / NB)))
    for store in stores:
        store.wait()


def per_device(hidden_state, proj_weight, offset, truth, counts, var_weight, total_rows):
    latitude = (np.arange(total_rows) + 0.5) * (LATITUDE_SPAN / total_rows) * (math.pi / 180.0)
    area = jnp.asarray(np.cos(latitude), dtype=F32)
    vmem = pl.BlockSpec(memory_space=pltpu.VMEM)
    smem = pl.BlockSpec(memory_space=pltpu.SMEM)
    hbm = pl.BlockSpec(memory_space=pltpu.HBM)
    dma = pltpu.SemaphoreType.DMA
    bf16 = jnp.bfloat16
    blocks = pltpu.VMEM((NB, NT, 8, 128), F32)
    half_tiles = (3, 4, 128)
    latent, sums = pl.pallas_call(
        exchange_kernel,
        out_shape=(
            pltpu.VMEM((POINTS, D), bf16),
            pltpu.VMEM((VP, D), F32),
        ),
        in_specs=[smem, smem, vmem, vmem, hbm, hbm, hbm],
        out_specs=(vmem, vmem),
        scratch_shapes=[
            pltpu.VMEM((V, D), bf16),
            pltpu.VMEM((POINTS, D), bf16),
            pltpu.VMEM((V, ROWS, CAP), F32),
            blocks,
            blocks,
            blocks,
            blocks,
            blocks,
            pltpu.VMEM((GP, POINTS), bf16),
            pltpu.VMEM((8, 128), F32),
            pltpu.VMEM((NT, 8, 128), F32),
            pltpu.VMEM((NT, 8, 128), F32),
            pltpu.VMEM((8, LAST, 128), F32),
            pltpu.VMEM((7, LAST, 128), F32),
            pltpu.VMEM((4, 2, 8, 128), F32),
            pltpu.VMEM((2, 8, 128), F32),
            pltpu.VMEM((2, 4, 2, 8, 128), F32),
            pltpu.VMEM((2, 2, 8, 128), F32),
            pltpu.VMEM((2, 8, 2, 8, 128), F32),
            pltpu.VMEM((LAST // 8, 8, 128), F32),
            pltpu.VMEM((8, LAST // 8, 8, 128), F32),
            pltpu.VMEM((16, *half_tiles), F32),
            pltpu.VMEM((16, *half_tiles), F32),
            pltpu.VMEM(half_tiles, F32),
            pltpu.VMEM((16, *half_tiles), F32),
            pltpu.VMEM(half_tiles, F32),
            pltpu.VMEM((16, *half_tiles), F32),
            dma((NB,)),
            dma((2,)),
            dma,
            dma((NC,)),
            dma,
            dma((NC,)),
            dma,
            dma((2,)),
            dma((2,)),
            dma((2,)),
            dma((2,)),
            dma((2,)),
            dma,
            dma,
            dma,
            dma((2,)),
            dma((3,)),
            dma((3,)),
        ],
        compiler_params=pltpu.CompilerParams(
            collective_id=0, has_side_effects=True, vmem_limit_bytes=59 * 1024 * 1024
        ),
        cost_estimate=pl.CostEstimate(
            flops=6 * V * POINTS * D, bytes_accessed=5_000_000, transcendentals=8_000_000
        ),
    )(
        counts,
        area,
        offset.reshape(1, V),
        var_weight.reshape(1, V),
        proj_weight,
        hidden_state.reshape(POINTS, D),
        truth,
    )
    factor = GRAD_SCALE / math.sqrt(NB * total_rows * CAP)
    latent, wgrad, bias, loss = pl.pallas_call(
        lambda *refs: finish_kernel(factor, *refs),
        out_shape=(
            jax.ShapeDtypeStruct((POINTS, D), bf16),
            jax.ShapeDtypeStruct((V, D), F32),
            jax.ShapeDtypeStruct((1, V), F32),
            jax.ShapeDtypeStruct((1, 1), F32),
        ),
        in_specs=[vmem, vmem],
        out_specs=(hbm, hbm, vmem, vmem),
        scratch_shapes=[pltpu.VMEM((V, D), F32), dma((5,))],
        compiler_params=pltpu.CompilerParams(vmem_limit_bytes=16 * 1024 * 1024),
        cost_estimate=pl.CostEstimate(flops=V * D, bytes_accessed=5_000_000, transcendentals=0),
    )(latent, sums)
    return latent.reshape(hidden_state.shape), wgrad, bias.reshape(V), loss.reshape(())


def solution(mesh):
    total_rows = ROWS * mesh.shape["space"]

    def step(*args):
        return per_device(*args, total_rows)

    return jax.shard_map(
        step,
        mesh=mesh,
        in_specs=(
            P("member", "space", None, None),
            P(),
            P(),
            P(None, "space", None),
            P("space"),
            P(),
        ),
        out_specs=(P("member", "space", None, None), P(), P(), P()),
        check_vma=False,
    )
```

```python
import math

import numpy as np

import jax
import jax.numpy as jnp
from jax import lax
from jax.experimental import pallas as pl
from jax.experimental.pallas import tpu as pltpu
from jax.sharding import PartitionSpec as P

SMOOTHING = 0.05
FAIRNESS = 0.95
GRAD_SCALE = 16.0
LATITUDE_SPAN = 80.0

V = 100
VP = 104
GP = 112
D = 1024
ROWS = 4
CAP = 512
POINTS = ROWS * CAP
BLOCK = 256
NB = 8
NT = 25
CHUNKS = ((0, 8), (8, 8), (16, 4), (20, 5))
NC = len(CHUNKS)
GROUPS = ((0, 64), (64, 16))
LAST = 80
MESH = pl.DeviceIdType.MESH
F32 = jnp.float32
EPS2 = SMOOTHING * SMOOTHING
COEFF = FAIRNESS / (NB * (NB - 1)) + (1.0 - FAIRNESS) / (NB * NB)


def column(row):
    n = row.shape[1]
    here = lax.broadcasted_iota(jnp.int32, (VP, n), 0) == lax.broadcasted_iota(
        jnp.int32, (VP, n), 1
    )
    return jnp.sum(jnp.where(here, jnp.broadcast_to(row, (VP, n)), 0.0), axis=1, keepdims=True)


def exchange_kernel(
    counts_ref,
    area_ref,
    offset_ref,
    scale_ref,
    weight_hbm,
    hidden_hbm,
    truth_hbm,
    latent_ref,
    sums_ref,
    weight,
    hbuf,
    truth,
    field,
    met,
    signs,
    back,
    obs,
    grad,
    loss_acc,
    bias_acc,
    scale,
    part,
    part_in,
    plane,
    pair,
    y_in,
    z_out,
    z_in,
    own_all,
    out_in,
    last,
    last_in,
    last_mid,
    last_z,
    last_own,
    last_out,
    load_sem,
    side_sem,
    fwd_send,
    fwd_recv,
    ret_send,
    ret_recv,
    part_send,
    part_recv,
    y_send,
    y_recv,
    z_send,
    z_recv,
    row_send,
    row_recv,
    out_send,
    out_recv,
    last_send,
    last_recv,
):
    member = lax.axis_index("member")
    space = lax.axis_index("space")
    y, z_hi = lax.div(member, 2), lax.rem(member, 2)
    z_lo, q = lax.div(space, 8), lax.rem(space, 8)
    x, core = lax.div(q, 2), lax.rem(q, 2)
    z = z_hi * 4 + z_lo
    in_plane = x * 4 + y
    in_stack = z * 2 + core

    def at(xx, yy, zz, cc):
        return (yy * 2 + lax.div(zz, 4), lax.rem(zz, 4) * 8 + xx * 2 + cc)

    def beside(j):
        return at(lax.div(j, 2), y, z, lax.rem(j, 2))

    def plane_device(w):
        return at(lax.div(w, 4), lax.rem(w, 4), z, core)

    def stack_device(u):
        return at(x, y, lax.div(u, 2), lax.rem(u, 2))

    def block_points(b):
        return pl.ds(pl.multiple_of(b * BLOCK, BLOCK), BLOCK)

    def turn(t):
        return lax.rem(member + core + t, NB)

    def load(t):
        rows = block_points(turn(t))
        return pltpu.make_async_copy(hidden_hbm.at[rows], hbuf.at[rows], load_sem.at[t - 1])

    load_weight = pltpu.make_async_copy(weight_hbm, weight, side_sem.at[0])
    load_weight.start()
    for t in range(1, NB + 1):
        load(t).start()
    load_truth = pltpu.make_async_copy(truth_hbm, truth, side_sem.at[1])
    load_truth.start()

    barrier = pltpu.get_barrier_semaphore()

    def greet(device):
        pl.semaphore_signal(barrier, inc=1, device_id=device, device_id_type=MESH)

    for t in range(1, 16):
        greet(plane_device(lax.rem(in_plane + t, 16)))
        greet(stack_device(lax.rem(in_stack + t, 16)))
    for t in range(1, 4):
        greet(at(x, lax.rem(y + t, 4), lax.rem(z + 2, 8), core))
        greet(at(x, lax.rem(y + t, 4), lax.rem(z + 6, 8), core))
        greet(at(lax.rem(x + t, 4), y, z, 1 - core))

    offsets = column(offset_ref[...])[0:V]
    scales = jnp.broadcast_to(column(scale_ref[...]), (VP, 128))
    for i in range(NT // 2):
        scale[2 * i] = scales[8 * i : 8 * i + 8]
        scale[2 * i + 1] = scales[8 * i : 8 * i + 8]
    scale[NT - 1] = jnp.concatenate([scales[96:V], scales[96:V]], axis=0)
    loss_acc[...] = jnp.zeros_like(loss_acc)
    bias_acc[...] = jnp.zeros_like(bias_acc)

    lane = lax.broadcasted_iota(jnp.int32, (1, 128), 1)
    sub = lax.broadcasted_iota(jnp.int32, (8, 128), 0)

    def live(b, h):
        return lane + (lax.rem(b, 2) * 2 + h) * 128 < counts_ref[lax.div(b, 2)]

    def point_weights(b, factor):
        area = area_ref[space * ROWS + lax.div(b, 2)] * factor
        halves = [jnp.where(live(b, h), area, 0.0) for h in range(2)]
        return halves, jnp.where(sub < 4, halves[0], halves[1])

    def send_forecast(c, b):
        block = pl.ds(*CHUNKS[c])
        return pltpu.make_async_remote_copy(
            src_ref=field.at[b, block],
            dst_ref=met.at[member, block],
            send_sem=fwd_send,
            recv_sem=fwd_recv.at[c],
            device_id=at(x, lax.div(b, 2), lax.rem(z_lo + 2 + 4 * lax.rem(b, 2), 8), core),
            device_id_type=MESH,
        )

    for t in range(1, NB + 1):
        load(t).wait()
        if t == 1:
            load_weight.wait()
        b = turn(t)
        product = lax.dot_general(
            weight[...],
            hbuf[block_points(b), :],
            (((1,), (1,)), ((), ())),
            preferred_element_type=F32,
        )
        forecast = product + offsets
        halves = [
            jnp.where(live(b, h), forecast[:, h * 128 : (h + 1) * 128], 0.0) for h in range(2)
        ]
        for i in range(NT // 2):
            for h in range(2):
                field[b, 2 * i + h] = halves[h][8 * i : 8 * i + 8]
        field[b, NT - 1] = jnp.concatenate([halves[0][96:V], halves[1][96:V]], axis=0)
        if t == 1:
            pl.semaphore_wait(barrier, 39)
        for c in range(2):
            send_forecast(c, b).start()
    for c in range(2, NC):
        for t in range(1, NB + 1):
            send_forecast(c, turn(t)).start()

    def misfit(b, tile, target, weight_here):
        gap = field[b, tile] - target
        square = gap * gap + EPS2
        inverse = lax.rsqrt(square)
        factor = weight_here * scale[tile]
        obs[b, tile] = factor * (gap * inverse)
        return factor * (square * inverse - SMOOTHING)

    def target(b, v, h):
        first = (b % 2) * BLOCK + h * 128
        return truth[v, b // 2, first : first + 128]

    def misfits():
        load_truth.wait()

        @pl.loop(0, NT // 2)
        def _(i):
            at_v = pl.ds(pl.multiple_of(i * 8, 8), 8)
            total = jnp.zeros((8, 128), F32)
            for b in range(NB):
                halves, _ = point_weights(b, 1.0 / NB)
                for h in range(2):
                    total += misfit(b, 2 * i + h, target(b, at_v, h), halves[h])
            loss_acc[...] += total

        total = jnp.zeros((8, 128), F32)
        for b in range(NB):
            _, both = point_weights(b, 1.0 / NB)
            tail = pl.ds(96, 4)
            goal = jnp.concatenate([target(b, tail, 0), target(b, tail, 1)], axis=0)
            total += misfit(b, NT - 1, goal, both)
        loss_acc[...] += total

    z_from = lax.rem(z + 2, 4)
    block_here = y * 2 + lax.div(lax.rem(z - z_from - 2 + 16, 8), 4)
    space_from = z_from * 8 + q
    area_here = area_ref[space_from * ROWS + y]

    def send_sign(c, m):
        block = pl.ds(*CHUNKS[c])
        return pltpu.make_async_remote_copy(
            src_ref=signs.at[m, block],
            dst_ref=back.at[block_here, block],
            send_sem=ret_send,
            recv_sem=ret_recv.at[c],
            device_id=(m, space_from),
            device_id_type=MESH,
        )

    def arrive(ref, sem):
        pltpu.make_async_copy(ref, ref, sem).wait()

    def meet(block):
        values = [met[m, block] for m in range(NB)]
        sums = [None] * NB
        roots = None
        for m in range(NB):
            for k in range(m + 1, NB):
                gap = values[m] - values[k]
                square = gap * gap + EPS2
                inverse = lax.rsqrt(square)
                sign = gap * inverse
                root = square * inverse
                roots = root if roots is None else roots + root
                sums[m] = sign if sums[m] is None else sums[m] + sign
                sums[k] = -sign if sums[k] is None else sums[k] - sign
        for m in range(NB):
            signs[m, block] = sums[m]
        spread = (roots - (NB * (NB - 1) // 2) * SMOOTHING) * scale[block]
        loss_acc[...] += (-COEFF * area_here) * jnp.sum(spread, axis=0)

    def pairs(c):
        first, n = CHUNKS[c]
        arrive(met.at[:, pl.ds(first, n)], fwd_recv.at[c])

        @pl.loop(0, n // 2)
        def _(i):
            meet(pl.ds(first + 2 * i, 2))

        if n % 2:
            meet(pl.ds(first + n - 1, 1))

        for t in range(1, NB + 1):
            send_sign(c, turn(t)).start()

    def gradient(c):
        first, n = CHUNKS[c]
        v0 = 4 * first
        arrive(back.at[:, pl.ds(first, n)], ret_recv.at[c])

        @pl.loop(0, NB)
        def _(b):
            halves, both = point_weights(b, COEFF)

            def value(tile, weight_here):
                result = obs[b, tile] - (weight_here * scale[tile]) * back[b, tile]
                bias_acc[tile] += result
                return result

            pieces = [
                [value(first + 2 * i + h, halves[h]) for i in range(n // 2)] for h in range(2)
            ]
            if n % 2:
                tail = value(NT - 1, both)
                for h in range(2):
                    pieces[h] += [tail[4 * h : 4 * h + 4], jnp.zeros((GP - V, 128), F32)]
            for h in range(2):
                stacked = jnp.concatenate(pieces[h], axis=0)
                points = pl.ds(pl.multiple_of(b * BLOCK + h * 128, 128), 128)
                grad[v0 : v0 + stacked.shape[0], points] = stacked.astype(jnp.bfloat16)

        @pl.loop(0, 4)
        def _(j):
            rows = GP - v0 if n % 2 else 4 * n
            piece = jnp.dot(
                grad[v0 : v0 + rows, :],
                hbuf[:, pl.ds(pl.multiple_of(j * 256, 256), 256)],
                preferred_element_type=F32,
            )
            for k in range(2):
                block = piece[:, k * 128 : (k + 1) * 128]
                if n % 2:
                    for i in range(6):
                        last[4 * j + 2 * k + i // 3, i % 3] = block[4 * i : 4 * i + 4]
                else:
                    part[2 * j + k, v0 : v0 + rows, :] = block

    def extras():
        rows = []
        for i in range(NT // 2):
            rows.append(bias_acc[2 * i] + bias_acc[2 * i + 1])
        tail = bias_acc[NT - 1]
        rows += [tail[0:4] + tail[4:8], jnp.zeros((VP - V, 128), F32)]
        bias = jnp.sum(jnp.concatenate(rows, axis=0), axis=1, keepdims=True)
        eye = lax.broadcasted_iota(jnp.int32, (VP, 128), 0) == lax.broadcasted_iota(
            jnp.int32, (VP, 128), 1
        )
        extra = jnp.sum(jnp.where(eye, bias, 0.0), axis=0, keepdims=True)
        loss_here = jnp.sum(jnp.sum(loss_acc[...], axis=0, keepdims=True), axis=1, keepdims=True)
        points_here = jnp.float32(0.0)
        for r in range(ROWS):
            points_here += area_ref[space * ROWS + r] * counts_ref[r].astype(F32)
        extra = jnp.where(lane == V, loss_here, extra)
        extra = jnp.where(lane == V + 1, points_here, extra)
        last[1, 2, 0:1, :] = extra

    def tiles(g):
        first, n = GROUPS[g]
        return first // 8, (first + n) // 8

    def send_part(g, t):
        rows = pl.ds(*GROUPS[g])
        j = lax.rem(q + t, 8)
        return pltpu.make_async_remote_copy(
            src_ref=part.at[j, rows],
            dst_ref=part_in.at[t - 1, rows],
            send_sem=part_send,
            recv_sem=part_recv.at[g],
            device_id=beside(j),
            device_id_type=MESH,
        )

    def send_plane(g, t):
        yy = lax.rem(y + t, 4)
        return pltpu.make_async_remote_copy(
            src_ref=plane.at[yy] if g == 0 else pair,
            dst_ref=y_in.at[g, y],
            send_sem=y_send.at[g],
            recv_sem=y_recv.at[g],
            device_id=at(x, yy, z, core),
            device_id_type=MESH,
        )

    def send_across(g, t):
        return pltpu.make_async_remote_copy(
            src_ref=z_out.at[g],
            dst_ref=z_in.at[g, z],
            send_sem=z_send.at[g],
            recv_sem=z_recv.at[g],
            device_id=at(x, y, lax.rem(z + t, 8), core),
            device_id_type=MESH,
        )

    def send_row(t):
        block = own_all.at[pl.ds(2 * y, 2)]
        return pltpu.make_async_remote_copy(
            src_ref=block,
            dst_ref=block,
            send_sem=row_send,
            recv_sem=row_recv,
            device_id=at(x, lax.rem(y + t, 4), z, core),
            device_id_type=MESH,
        )

    def send_out(g, t):
        first, end = tiles(g)
        block = pl.ds(first, end - first)
        return pltpu.make_async_remote_copy(
            src_ref=own_all.at[block],
            dst_ref=out_in.at[t, block],
            send_sem=out_send,
            recv_sem=out_recv.at[g],
            device_id=beside(lax.rem(q + t, 8)),
            device_id_type=MESH,
        )

    def send_all(send, number):
        for t in range(1, number):
            send(t).start()

    def send_parts(g):
        send_all(lambda t: send_part(g, t), 8)

    def sum_beside(g):
        arrive(part_in.at[:, pl.ds(*GROUPS[g])], part_recv.at[g])

        def column_sum(o):
            at_v = pl.ds(pl.multiple_of(o * 8, 8), 8)
            value = part[q, at_v, :]
            for t in range(7):
                value += part_in[t, at_v, :]
            return value

        if g == 0:

            @pl.loop(0, 4)
            def _(yy):
                for i in range(2):
                    plane[yy, i] = column_sum(2 * yy + i)

            y_in[g, y] = plane[y]
        else:
            for i in range(2):
                pair[i] = column_sum(8 + i)
            y_in[g, y] = pair[...]
        send_all(lambda t: send_plane(g, t), 4)

    def sum_plane(g):
        arrive(y_in.at[g, pl.ds(0, 3)], y_recv.at[g])
        value = y_in[g, 0]
        for yy in range(1, 4):
            value += y_in[g, yy]
        z_out[g] = value
        z_in[g, z] = value
        send_all(lambda t: send_across(g, t), 8)

    def spread_out(g):
        first, end = tiles(g)
        send_all(lambda t: send_out(g, t), 8)
        out_in[0, first:end] = own_all[first:end]

    def sum_across(g):
        arrive(z_in.at[g, pl.ds(0, 7)], z_recv.at[g])
        value = z_in[g, 0]
        for zz in range(1, 8):
            value += z_in[g, zz]
        if g == 0:
            own_all[pl.ds(2 * y, 2)] = value
            send_all(send_row, 4)
        else:
            own_all[8:10] = value
            spread_out(1)

    def collect_rows():
        arrive(own_all.at[pl.ds(0, 6)], row_recv)
        spread_out(0)

    def collect(g):
        first, end = tiles(g)
        arrive(out_in.at[pl.ds(1, 7), pl.ds(first, end - first)], out_recv.at[g])

        @pl.loop(0, 8)
        def _(t):
            cols = pl.ds(pl.multiple_of(lax.rem(q - t + 8, 8) * 128, 128), 128)
            for o in range(first, end):
                sums_ref[o * 8 : (o + 1) * 8, cols] = out_in[t, o]

    def last_copy(phase, t):
        if phase == 1:
            to = lax.rem(in_stack + t, 16)
            src, dst, device = last_mid, last_z.at[in_stack], stack_device(to)
        else:
            to = lax.rem(in_plane + t, 16)
            src = last.at[to] if phase == 0 else last_own
            dst = (last_in if phase == 0 else last_out).at[in_plane]
            device = plane_device(to)
        return pltpu.make_async_remote_copy(
            src_ref=src,
            dst_ref=dst,
            send_sem=last_send.at[phase],
            recv_sem=last_recv.at[phase],
            device_id=device,
            device_id_type=MESH,
        )

    def last_start(phase):
        send_all(lambda t: last_copy(phase, t), 16)

    def last_sum(phase, source):
        arrive(source.at[pl.ds(0, 15)], last_recv.at[phase])
        value = source[0]
        for t in range(1, 16):
            value += source[t]
        return value

    def last_scatter():
        last_start(0)
        last_in[in_plane] = last[in_plane]

    def last_across():
        value = last_sum(0, last_in)
        last_mid[...] = value
        last_start(1)
        last_z[in_stack] = value

    def last_gather():
        value = last_sum(1, last_z)
        last_own[...] = value
        last_start(2)
        last_out[in_plane] = value

    def last_collect():
        arrive(last_out.at[pl.ds(0, 15)], last_recv.at[2])

        @pl.loop(0, 8)
        def _(j):
            cols = pl.ds(pl.multiple_of(j * 128, 128), 128)
            for i in range(6):
                rows = slice(LAST + 4 * i, LAST + 4 * i + 4)
                sums_ref[rows, cols] = last_out[2 * j + i // 3, i % 3]

    def latent(first, end):
        @pl.loop(first, end)
        def _(b):
            points = block_points(b)
            value = lax.dot_general(
                grad[0:V, points], weight[...], (((0,), (0,)), ((), ())), preferred_element_type=F32
            )
            latent_ref[points, :] = (GRAD_SCALE * value).astype(jnp.bfloat16)

    pairs(0)
    pairs(1)
    misfits()
    pairs(2)
    pairs(3)
    gradient(0)
    gradient(1)
    send_parts(0)
    gradient(2)
    send_parts(1)
    sum_beside(0)
    gradient(3)
    extras()
    last_scatter()
    sum_plane(0)
    sum_beside(1)
    latent(0, 2)
    last_across()
    sum_across(0)
    sum_plane(1)
    latent(2, 4)
    last_gather()
    collect_rows()
    sum_across(1)
    latent(4, 8)
    last_collect()
    collect(0)
    collect(1)

    arrive(field, fwd_send)
    arrive(signs, ret_send)
    arrive(part.at[pl.ds(0, 7)], part_send)
    arrive(plane.at[pl.ds(0, 3)], y_send.at[0])
    arrive(plane.at[pl.ds(0, 3)], y_send.at[1])
    for g in range(len(GROUPS)):
        arrive(z_in.at[g, pl.ds(0, 7)], z_send.at[g])
    arrive(own_all.at[pl.ds(0, 6)], row_send)
    arrive(out_in.at[pl.ds(0, 7)], out_send)
    for phase in range(3):
        arrive(last.at[pl.ds(0, 15)], last_send.at[phase])


def finish_kernel(factor, latent, sums, latent_hbm, wgrad_hbm, bias_ref, loss_ref, wgrad, sem):
    stores = []
    for b in range(4):
        rows = pl.ds(b * CAP, CAP)
        stores.append(pltpu.make_async_copy(latent.at[rows], latent_hbm.at[rows], sem.at[b]))
        stores[-1].start()
    wgrad[...] = sums[0:V, :] * factor
    stores.append(pltpu.make_async_copy(wgrad, wgrad_hbm, sem.at[4]))
    stores[-1].start()
    extra = sums[V : V + 1, 0:128]
    lane = lax.broadcasted_iota(jnp.int32, (1, 128), 1)
    total = jnp.sum(jnp.where(lane == V, extra, 0.0), axis=1, keepdims=True)
    points = jnp.sum(jnp.where(lane == V + 1, extra, 0.0), axis=1, keepdims=True)
    bias_ref[...] = extra[:, 0:V] * factor
    loss_ref[...] = total / (V * (points * (1.0 / NB)))
    for store in stores:
        store.wait()


def per_device(hidden_state, proj_weight, offset, truth, counts, var_weight, total_rows):
    latitude = (np.arange(total_rows) + 0.5) * (LATITUDE_SPAN / total_rows) * (math.pi / 180.0)
    area = jnp.asarray(np.cos(latitude), dtype=F32)
    vmem = pl.BlockSpec(memory_space=pltpu.VMEM)
    smem = pl.BlockSpec(memory_space=pltpu.SMEM)
    hbm = pl.BlockSpec(memory_space=pltpu.HBM)
    dma = pltpu.SemaphoreType.DMA
    bf16 = jnp.bfloat16
    blocks = pltpu.VMEM((NB, NT, 8, 128), F32)
    half_tiles = (3, 4, 128)
    latent, sums = pl.pallas_call(
        exchange_kernel,
        out_shape=(
            pltpu.VMEM((POINTS, D), bf16),
            pltpu.VMEM((VP, D), F32),
        ),
        in_specs=[smem, smem, vmem, vmem, hbm, hbm, hbm],
        out_specs=(vmem, vmem),
        scratch_shapes=[
            pltpu.VMEM((V, D), bf16),
            pltpu.VMEM((POINTS, D), bf16),
            pltpu.VMEM((V, ROWS, CAP), F32),
            blocks,
            blocks,
            blocks,
            blocks,
            blocks,
            pltpu.VMEM((GP, POINTS), bf16),
            pltpu.VMEM((8, 128), F32),
            pltpu.VMEM((NT, 8, 128), F32),
            pltpu.VMEM((NT, 8, 128), F32),
            pltpu.VMEM((8, LAST, 128), F32),
            pltpu.VMEM((7, LAST, 128), F32),
            pltpu.VMEM((4, 2, 8, 128), F32),
            pltpu.VMEM((2, 8, 128), F32),
            pltpu.VMEM((2, 4, 2, 8, 128), F32),
            pltpu.VMEM((2, 2, 8, 128), F32),
            pltpu.VMEM((2, 8, 2, 8, 128), F32),
            pltpu.VMEM((LAST // 8, 8, 128), F32),
            pltpu.VMEM((8, LAST // 8, 8, 128), F32),
            pltpu.VMEM((16, *half_tiles), F32),
            pltpu.VMEM((16, *half_tiles), F32),
            pltpu.VMEM(half_tiles, F32),
            pltpu.VMEM((16, *half_tiles), F32),
            pltpu.VMEM(half_tiles, F32),
            pltpu.VMEM((16, *half_tiles), F32),
            dma((NB,)),
            dma((2,)),
            dma,
            dma((NC,)),
            dma,
            dma((NC,)),
            dma,
            dma((2,)),
            dma((2,)),
            dma((2,)),
            dma((2,)),
            dma((2,)),
            dma,
            dma,
            dma,
            dma((2,)),
            dma((3,)),
            dma((3,)),
        ],
        compiler_params=pltpu.CompilerParams(
            collective_id=0, has_side_effects=True, vmem_limit_bytes=59 * 1024 * 1024
        ),
        cost_estimate=pl.CostEstimate(
            flops=6 * V * POINTS * D, bytes_accessed=5_000_000, transcendentals=8_000_000
        ),
    )(
        counts,
        area,
        offset.reshape(1, V),
        var_weight.reshape(1, V),
        proj_weight,
        hidden_state.reshape(POINTS, D),
        truth,
    )
    factor = GRAD_SCALE / math.sqrt(NB * total_rows * CAP)
    latent, wgrad, bias, loss = pl.pallas_call(
        lambda *refs: finish_kernel(factor, *refs),
        out_shape=(
            jax.ShapeDtypeStruct((POINTS, D), bf16),
            jax.ShapeDtypeStruct((V, D), F32),
            jax.ShapeDtypeStruct((1, V), F32),
            jax.ShapeDtypeStruct((1, 1), F32),
        ),
        in_specs=[vmem, vmem],
        out_specs=(hbm, hbm, vmem, vmem),
        scratch_shapes=[pltpu.VMEM((V, D), F32), dma((5,))],
        compiler_params=pltpu.CompilerParams(vmem_limit_bytes=16 * 1024 * 1024),
        cost_estimate=pl.CostEstimate(flops=V * D, bytes_accessed=5_000_000, transcendentals=0),
    )(latent, sums)
    return latent.reshape(hidden_state.shape), wgrad, bias.reshape(V), loss.reshape(())


def solution(mesh):
    total_rows = ROWS * mesh.shape["space"]

    def step(*args):
        return per_device(*args, total_rows)

    return jax.shard_map(
        step,
        mesh=mesh,
        in_specs=(
            P("member", "space", None, None),
            P(),
            P(),
            P(None, "space", None),
            P("space"),
            P(),
        ),
        out_specs=(P("member", "space", None, None), P(), P(), P()),
        check_vma=False,
    )
```

```python
import math

import numpy as np

import jax
import jax.numpy as jnp
from jax import lax
from jax.experimental import pallas as pl
from jax.experimental.pallas import tpu as pltpu
from jax.sharding import PartitionSpec as P

SMOOTHING = 0.05
FAIRNESS = 0.95
GRAD_SCALE = 16.0
LATITUDE_SPAN = 80.0

V = 100
VP = 104
GP = 112
D = 1024
ROWS = 4
CAP = 512
POINTS = ROWS * CAP
BLOCK = 256
NB = 8
NT = 25
CHUNKS = ((0, 8), (8, 8), (16, 4), (20, 5))
NC = len(CHUNKS)
GROUPS = ((0, 64), (64, 16))
LAST = 80
MESH = pl.DeviceIdType.MESH
F32 = jnp.float32
EPS2 = SMOOTHING * SMOOTHING
COEFF = FAIRNESS / (NB * (NB - 1)) + (1.0 - FAIRNESS) / (NB * NB)


def column(row):
    n = row.shape[1]
    here = lax.broadcasted_iota(jnp.int32, (VP, n), 0) == lax.broadcasted_iota(
        jnp.int32, (VP, n), 1
    )
    return jnp.sum(jnp.where(here, jnp.broadcast_to(row, (VP, n)), 0.0), axis=1, keepdims=True)


def exchange_kernel(
    counts_ref,
    area_ref,
    offset_ref,
    scale_ref,
    weight_hbm,
    hidden_hbm,
    truth_hbm,
    latent_ref,
    sums_ref,
    weight,
    hbuf,
    truth,
    field,
    met,
    signs,
    back,
    obs,
    grad,
    loss_acc,
    bias_acc,
    scale,
    part,
    part_in,
    plane,
    pair,
    y_in,
    z_out,
    z_in,
    own_all,
    out_in,
    last,
    last_in,
    last_mid,
    last_z,
    last_own,
    last_out,
    load_sem,
    side_sem,
    fwd_send,
    fwd_recv,
    ret_send,
    ret_recv,
    part_send,
    part_recv,
    y_send,
    y_recv,
    z_send,
    z_recv,
    row_send,
    row_recv,
    out_send,
    out_recv,
    last_send,
    last_recv,
):
    member = lax.axis_index("member")
    space = lax.axis_index("space")
    y, z_hi = lax.div(member, 2), lax.rem(member, 2)
    z_lo, q = lax.div(space, 8), lax.rem(space, 8)
    x, core = lax.div(q, 2), lax.rem(q, 2)
    z = z_hi * 4 + z_lo
    in_plane = x * 4 + y
    in_stack = z * 2 + core

    def at(xx, yy, zz, cc):
        return (yy * 2 + lax.div(zz, 4), lax.rem(zz, 4) * 8 + xx * 2 + cc)

    def beside(j):
        return at(lax.div(j, 2), y, z, lax.rem(j, 2))

    def plane_device(w):
        return at(lax.div(w, 4), lax.rem(w, 4), z, core)

    def stack_device(u):
        return at(x, y, lax.div(u, 2), lax.rem(u, 2))

    def block_points(b):
        return pl.ds(pl.multiple_of(b * BLOCK, BLOCK), BLOCK)

    def load(t):
        rows = block_points(lax.rem(member + t, NB))
        return pltpu.make_async_copy(hidden_hbm.at[rows], hbuf.at[rows], load_sem.at[t - 1])

    load_weight = pltpu.make_async_copy(weight_hbm, weight, side_sem.at[0])
    load_weight.start()
    for t in range(1, NB + 1):
        load(t).start()
    load_truth = pltpu.make_async_copy(truth_hbm, truth, side_sem.at[1])
    load_truth.start()

    barrier = pltpu.get_barrier_semaphore()

    def greet(device):
        pl.semaphore_signal(barrier, inc=1, device_id=device, device_id_type=MESH)

    for t in range(1, 16):
        greet(plane_device(lax.rem(in_plane + t, 16)))
        greet(stack_device(lax.rem(in_stack + t, 16)))
    for t in range(1, 4):
        greet(at(x, lax.rem(y + t, 4), lax.rem(z + 2, 8), core))
        greet(at(x, lax.rem(y + t, 4), lax.rem(z + 6, 8), core))
        greet(at(lax.rem(x + t, 4), y, z, 1 - core))

    offsets = column(offset_ref[...])[0:V]
    scales = jnp.broadcast_to(column(scale_ref[...]), (VP, 128))
    for i in range(NT // 2):
        scale[2 * i] = scales[8 * i : 8 * i + 8]
        scale[2 * i + 1] = scales[8 * i : 8 * i + 8]
    scale[NT - 1] = jnp.concatenate([scales[96:V], scales[96:V]], axis=0)
    loss_acc[...] = jnp.zeros_like(loss_acc)
    bias_acc[...] = jnp.zeros_like(bias_acc)

    lane = lax.broadcasted_iota(jnp.int32, (1, 128), 1)
    sub = lax.broadcasted_iota(jnp.int32, (8, 128), 0)

    def live(b, h):
        return lane + (lax.rem(b, 2) * 2 + h) * 128 < counts_ref[lax.div(b, 2)]

    def point_weights(b, factor):
        area = area_ref[space * ROWS + lax.div(b, 2)] * factor
        halves = [jnp.where(live(b, h), area, 0.0) for h in range(2)]
        return halves, jnp.where(sub < 4, halves[0], halves[1])

    def send_forecast(c, b):
        block = pl.ds(*CHUNKS[c])
        return pltpu.make_async_remote_copy(
            src_ref=field.at[b, block],
            dst_ref=met.at[member, block],
            send_sem=fwd_send,
            recv_sem=fwd_recv.at[c],
            device_id=at(x, lax.div(b, 2), lax.rem(z_lo + 2 + 4 * lax.rem(b, 2), 8), core),
            device_id_type=MESH,
        )

    for t in range(1, NB + 1):
        load(t).wait()
        if t == 1:
            load_weight.wait()
        b = lax.rem(member + t, NB)
        product = lax.dot_general(
            hbuf[block_points(b), :],
            weight[...],
            (((1,), (1,)), ((), ())),
            preferred_element_type=F32,
        )
        forecast = product.T + offsets
        halves = [
            jnp.where(live(b, h), forecast[:, h * 128 : (h + 1) * 128], 0.0) for h in range(2)
        ]
        for i in range(NT // 2):
            for h in range(2):
                field[b, 2 * i + h] = halves[h][8 * i : 8 * i + 8]
        field[b, NT - 1] = jnp.concatenate([halves[0][96:V], halves[1][96:V]], axis=0)
        if t == 1:
            pl.semaphore_wait(barrier, 39)
        for c in range(2):
            send_forecast(c, b).start()
    for c in range(2, NC):
        for t in range(1, NB + 1):
            send_forecast(c, lax.rem(member + t, NB)).start()

    def misfit(b, tile, target, weight_here):
        gap = field[b, tile] - target
        square = gap * gap + EPS2
        inverse = lax.rsqrt(square)
        factor = weight_here * scale[tile]
        obs[b, tile] = factor * (gap * inverse)
        return factor * (square * inverse - SMOOTHING)

    def target(b, v, h):
        first = (b % 2) * BLOCK + h * 128
        return truth[v, b // 2, first : first + 128]

    def misfits():
        load_truth.wait()

        @pl.loop(0, NT // 2)
        def _(i):
            at_v = pl.ds(pl.multiple_of(i * 8, 8), 8)
            total = jnp.zeros((8, 128), F32)
            for b in range(NB):
                halves, _ = point_weights(b, 1.0 / NB)
                for h in range(2):
                    total += misfit(b, 2 * i + h, target(b, at_v, h), halves[h])
            loss_acc[...] += total

        total = jnp.zeros((8, 128), F32)
        for b in range(NB):
            _, both = point_weights(b, 1.0 / NB)
            tail = pl.ds(96, 4)
            goal = jnp.concatenate([target(b, tail, 0), target(b, tail, 1)], axis=0)
            total += misfit(b, NT - 1, goal, both)
        loss_acc[...] += total

    z_from = lax.rem(z + 2, 4)
    block_here = y * 2 + lax.div(lax.rem(z - z_from - 2 + 16, 8), 4)
    space_from = z_from * 8 + q
    area_here = area_ref[space_from * ROWS + y]

    def send_sign(c, m):
        block = pl.ds(*CHUNKS[c])
        return pltpu.make_async_remote_copy(
            src_ref=signs.at[m, block],
            dst_ref=back.at[block_here, block],
            send_sem=ret_send,
            recv_sem=ret_recv.at[c],
            device_id=(m, space_from),
            device_id_type=MESH,
        )

    def arrive(ref, sem):
        pltpu.make_async_copy(ref, ref, sem).wait()

    def meet(block):
        values = [met[m, block] for m in range(NB)]
        sums = [None] * NB
        roots = None
        for m in range(NB):
            for k in range(m + 1, NB):
                gap = values[m] - values[k]
                square = gap * gap + EPS2
                inverse = lax.rsqrt(square)
                sign = gap * inverse
                root = square * inverse
                roots = root if roots is None else roots + root
                sums[m] = sign if sums[m] is None else sums[m] + sign
                sums[k] = -sign if sums[k] is None else sums[k] - sign
        for m in range(NB):
            signs[m, block] = sums[m]
        spread = (roots - (NB * (NB - 1) // 2) * SMOOTHING) * scale[block]
        loss_acc[...] += (-COEFF * area_here) * jnp.sum(spread, axis=0)

    def pairs(c):
        first, n = CHUNKS[c]
        arrive(met.at[:, pl.ds(first, n)], fwd_recv.at[c])

        @pl.loop(0, n // 2)
        def _(i):
            meet(pl.ds(first + 2 * i, 2))

        if n % 2:
            meet(pl.ds(first + n - 1, 1))

        for t in range(1, NB + 1):
            send_sign(c, lax.rem(member + t, NB)).start()

    def gradient(c):
        first, n = CHUNKS[c]
        v0 = 4 * first
        arrive(back.at[:, pl.ds(first, n)], ret_recv.at[c])

        @pl.loop(0, NB)
        def _(b):
            halves, both = point_weights(b, COEFF)

            def value(tile, weight_here):
                result = obs[b, tile] - (weight_here * scale[tile]) * back[b, tile]
                bias_acc[tile] += result
                return result

            pieces = [
                [value(first + 2 * i + h, halves[h]) for i in range(n // 2)] for h in range(2)
            ]
            if n % 2:
                tail = value(NT - 1, both)
                for h in range(2):
                    pieces[h] += [tail[4 * h : 4 * h + 4], jnp.zeros((GP - V, 128), F32)]
            for h in range(2):
                stacked = jnp.concatenate(pieces[h], axis=0)
                points = pl.ds(pl.multiple_of(b * BLOCK + h * 128, 128), 128)
                grad[v0 : v0 + stacked.shape[0], points] = stacked.astype(jnp.bfloat16)

        @pl.loop(0, 4)
        def _(j):
            rows = GP - v0 if n % 2 else 4 * n
            piece = jnp.dot(
                grad[v0 : v0 + rows, :],
                hbuf[:, pl.ds(pl.multiple_of(j * 256, 256), 256)],
                preferred_element_type=F32,
            )
            for k in range(2):
                block = piece[:, k * 128 : (k + 1) * 128]
                if n % 2:
                    for i in range(6):
                        last[4 * j + 2 * k + i // 3, i % 3] = block[4 * i : 4 * i + 4]
                else:
                    part[2 * j + k, v0 : v0 + rows, :] = block

    def extras():
        rows = []
        for i in range(NT // 2):
            rows.append(bias_acc[2 * i] + bias_acc[2 * i + 1])
        tail = bias_acc[NT - 1]
        rows += [tail[0:4] + tail[4:8], jnp.zeros((VP - V, 128), F32)]
        bias = jnp.sum(jnp.concatenate(rows, axis=0), axis=1, keepdims=True)
        eye = lax.broadcasted_iota(jnp.int32, (VP, 128), 0) == lax.broadcasted_iota(
            jnp.int32, (VP, 128), 1
        )
        extra = jnp.sum(jnp.where(eye, bias, 0.0), axis=0, keepdims=True)
        loss_here = jnp.sum(jnp.sum(loss_acc[...], axis=0, keepdims=True), axis=1, keepdims=True)
        points_here = jnp.float32(0.0)
        for r in range(ROWS):
            points_here += area_ref[space * ROWS + r] * counts_ref[r].astype(F32)
        extra = jnp.where(lane == V, loss_here, extra)
        extra = jnp.where(lane == V + 1, points_here, extra)
        last[1, 2, 0:1, :] = extra

    def tiles(g):
        first, n = GROUPS[g]
        return first // 8, (first + n) // 8

    def send_part(g, t):
        rows = pl.ds(*GROUPS[g])
        j = lax.rem(q + t, 8)
        return pltpu.make_async_remote_copy(
            src_ref=part.at[j, rows],
            dst_ref=part_in.at[t - 1, rows],
            send_sem=part_send,
            recv_sem=part_recv.at[g],
            device_id=beside(j),
            device_id_type=MESH,
        )

    def send_plane(g, t):
        yy = lax.rem(y + t, 4)
        return pltpu.make_async_remote_copy(
            src_ref=plane.at[yy] if g == 0 else pair,
            dst_ref=y_in.at[g, y],
            send_sem=y_send.at[g],
            recv_sem=y_recv.at[g],
            device_id=at(x, yy, z, core),
            device_id_type=MESH,
        )

    def send_across(g, t):
        return pltpu.make_async_remote_copy(
            src_ref=z_out.at[g],
            dst_ref=z_in.at[g, z],
            send_sem=z_send.at[g],
            recv_sem=z_recv.at[g],
            device_id=at(x, y, lax.rem(z + t, 8), core),
            device_id_type=MESH,
        )

    def send_row(t):
        block = own_all.at[pl.ds(2 * y, 2)]
        return pltpu.make_async_remote_copy(
            src_ref=block,
            dst_ref=block,
            send_sem=row_send,
            recv_sem=row_recv,
            device_id=at(x, lax.rem(y + t, 4), z, core),
            device_id_type=MESH,
        )

    def send_out(g, t):
        first, end = tiles(g)
        block = pl.ds(first, end - first)
        return pltpu.make_async_remote_copy(
            src_ref=own_all.at[block],
            dst_ref=out_in.at[t, block],
            send_sem=out_send,
            recv_sem=out_recv.at[g],
            device_id=beside(lax.rem(q + t, 8)),
            device_id_type=MESH,
        )

    def send_all(send, number):
        for t in range(1, number):
            send(t).start()

    def send_parts(g):
        send_all(lambda t: send_part(g, t), 8)

    def sum_beside(g):
        arrive(part_in.at[:, pl.ds(*GROUPS[g])], part_recv.at[g])

        def column_sum(o):
            at_v = pl.ds(pl.multiple_of(o * 8, 8), 8)
            value = part[q, at_v, :]
            for t in range(7):
                value += part_in[t, at_v, :]
            return value

        if g == 0:

            @pl.loop(0, 4)
            def _(yy):
                for i in range(2):
                    plane[yy, i] = column_sum(2 * yy + i)

            y_in[g, y] = plane[y]
        else:
            for i in range(2):
                pair[i] = column_sum(8 + i)
            y_in[g, y] = pair[...]
        send_all(lambda t: send_plane(g, t), 4)

    def sum_plane(g):
        arrive(y_in.at[g, pl.ds(0, 3)], y_recv.at[g])
        value = y_in[g, 0]
        for yy in range(1, 4):
            value += y_in[g, yy]
        z_out[g] = value
        z_in[g, z] = value
        send_all(lambda t: send_across(g, t), 8)

    def spread_out(g):
        first, end = tiles(g)
        send_all(lambda t: send_out(g, t), 8)
        out_in[0, first:end] = own_all[first:end]

    def sum_across(g):
        arrive(z_in.at[g, pl.ds(0, 7)], z_recv.at[g])
        value = z_in[g, 0]
        for zz in range(1, 8):
            value += z_in[g, zz]
        if g == 0:
            own_all[pl.ds(2 * y, 2)] = value
            send_all(send_row, 4)
        else:
            own_all[8:10] = value
            spread_out(1)

    def collect_rows():
        arrive(own_all.at[pl.ds(0, 6)], row_recv)
        spread_out(0)

    def collect(g):
        first, end = tiles(g)
        arrive(out_in.at[pl.ds(1, 7), pl.ds(first, end - first)], out_recv.at[g])

        @pl.loop(0, 8)
        def _(t):
            cols = pl.ds(pl.multiple_of(lax.rem(q - t + 8, 8) * 128, 128), 128)
            for o in range(first, end):
                sums_ref[o * 8 : (o + 1) * 8, cols] = out_in[t, o]

    def last_copy(phase, t):
        if phase == 1:
            to = lax.rem(in_stack + t, 16)
            src, dst, device = last_mid, last_z.at[in_stack], stack_device(to)
        else:
            to = lax.rem(in_plane + t, 16)
            src = last.at[to] if phase == 0 else last_own
            dst = (last_in if phase == 0 else last_out).at[in_plane]
            device = plane_device(to)
        return pltpu.make_async_remote_copy(
            src_ref=src,
            dst_ref=dst,
            send_sem=last_send.at[phase],
            recv_sem=last_recv.at[phase],
            device_id=device,
            device_id_type=MESH,
        )

    def last_start(phase):
        send_all(lambda t: last_copy(phase, t), 16)

    def last_sum(phase, source):
        arrive(source.at[pl.ds(0, 15)], last_recv.at[phase])
        value = source[0]
        for t in range(1, 16):
            value += source[t]
        return value

    def last_scatter():
        last_start(0)
        last_in[in_plane] = last[in_plane]

    def last_across():
        value = last_sum(0, last_in)
        last_mid[...] = value
        last_start(1)
        last_z[in_stack] = value

    def last_gather():
        value = last_sum(1, last_z)
        last_own[...] = value
        last_start(2)
        last_out[in_plane] = value

    def last_collect():
        arrive(last_out.at[pl.ds(0, 15)], last_recv.at[2])

        @pl.loop(0, 8)
        def _(j):
            cols = pl.ds(pl.multiple_of(j * 128, 128), 128)
            for i in range(6):
                rows = slice(LAST + 4 * i, LAST + 4 * i + 4)
                sums_ref[rows, cols] = last_out[2 * j + i // 3, i % 3]

    def latent(first, end):
        @pl.loop(first, end)
        def _(b):
            points = block_points(b)
            value = lax.dot_general(
                grad[0:V, points], weight[...], (((0,), (0,)), ((), ())), preferred_element_type=F32
            )
            latent_ref[points, :] = (GRAD_SCALE * value).astype(jnp.bfloat16)

    pairs(0)
    pairs(1)
    misfits()
    pairs(2)
    pairs(3)
    gradient(0)
    gradient(1)
    send_parts(0)
    gradient(2)
    send_parts(1)
    sum_beside(0)
    gradient(3)
    extras()
    last_scatter()
    sum_plane(0)
    sum_beside(1)
    latent(0, 2)
    last_across()
    sum_across(0)
    sum_plane(1)
    latent(2, 4)
    last_gather()
    collect_rows()
    sum_across(1)
    latent(4, 8)
    last_collect()
    collect(0)
    collect(1)

    arrive(field, fwd_send)
    arrive(signs, ret_send)
    arrive(part.at[pl.ds(0, 7)], part_send)
    arrive(plane.at[pl.ds(0, 3)], y_send.at[0])
    arrive(plane.at[pl.ds(0, 3)], y_send.at[1])
    for g in range(len(GROUPS)):
        arrive(z_in.at[g, pl.ds(0, 7)], z_send.at[g])
    arrive(own_all.at[pl.ds(0, 6)], row_send)
    arrive(out_in.at[pl.ds(0, 7)], out_send)
    for phase in range(3):
        arrive(last.at[pl.ds(0, 15)], last_send.at[phase])


def finish_kernel(factor, latent, sums, latent_hbm, wgrad_hbm, bias_ref, loss_ref, wgrad, sem):
    stores = []
    for b in range(4):
        rows = pl.ds(b * CAP, CAP)
        stores.append(pltpu.make_async_copy(latent.at[rows], latent_hbm.at[rows], sem.at[b]))
        stores[-1].start()
    wgrad[...] = sums[0:V, :] * factor
    stores.append(pltpu.make_async_copy(wgrad, wgrad_hbm, sem.at[4]))
    stores[-1].start()
    extra = sums[V : V + 1, 0:128]
    lane = lax.broadcasted_iota(jnp.int32, (1, 128), 1)
    total = jnp.sum(jnp.where(lane == V, extra, 0.0), axis=1, keepdims=True)
    points = jnp.sum(jnp.where(lane == V + 1, extra, 0.0), axis=1, keepdims=True)
    bias_ref[...] = extra[:, 0:V] * factor
    loss_ref[...] = total / (V * (points * (1.0 / NB)))
    for store in stores:
        store.wait()


def per_device(hidden_state, proj_weight, offset, truth, counts, var_weight, total_rows):
    latitude = (np.arange(total_rows) + 0.5) * (LATITUDE_SPAN / total_rows) * (math.pi / 180.0)
    area = jnp.asarray(np.cos(latitude), dtype=F32)
    vmem = pl.BlockSpec(memory_space=pltpu.VMEM)
    smem = pl.BlockSpec(memory_space=pltpu.SMEM)
    hbm = pl.BlockSpec(memory_space=pltpu.HBM)
    dma = pltpu.SemaphoreType.DMA
    bf16 = jnp.bfloat16
    blocks = pltpu.VMEM((NB, NT, 8, 128), F32)
    half_tiles = (3, 4, 128)
    latent, sums = pl.pallas_call(
        exchange_kernel,
        out_shape=(
            pltpu.VMEM((POINTS, D), bf16),
            pltpu.VMEM((VP, D), F32),
        ),
        in_specs=[smem, smem, vmem, vmem, hbm, hbm, hbm],
        out_specs=(vmem, vmem),
        scratch_shapes=[
            pltpu.VMEM((V, D), bf16),
            pltpu.VMEM((POINTS, D), bf16),
            pltpu.VMEM((V, ROWS, CAP), F32),
            blocks,
            blocks,
            blocks,
            blocks,
            blocks,
            pltpu.VMEM((GP, POINTS), bf16),
            pltpu.VMEM((8, 128), F32),
            pltpu.VMEM((NT, 8, 128), F32),
            pltpu.VMEM((NT, 8, 128), F32),
            pltpu.VMEM((8, LAST, 128), F32),
            pltpu.VMEM((7, LAST, 128), F32),
            pltpu.VMEM((4, 2, 8, 128), F32),
            pltpu.VMEM((2, 8, 128), F32),
            pltpu.VMEM((2, 4, 2, 8, 128), F32),
            pltpu.VMEM((2, 2, 8, 128), F32),
            pltpu.VMEM((2, 8, 2, 8, 128), F32),
            pltpu.VMEM((LAST // 8, 8, 128), F32),
            pltpu.VMEM((8, LAST // 8, 8, 128), F32),
            pltpu.VMEM((16, *half_tiles), F32),
            pltpu.VMEM((16, *half_tiles), F32),
            pltpu.VMEM(half_tiles, F32),
            pltpu.VMEM((16, *half_tiles), F32),
            pltpu.VMEM(half_tiles, F32),
            pltpu.VMEM((16, *half_tiles), F32),
            dma((NB,)),
            dma((2,)),
            dma,
            dma((NC,)),
            dma,
            dma((NC,)),
            dma,
            dma((2,)),
            dma((2,)),
            dma((2,)),
            dma((2,)),
            dma((2,)),
            dma,
            dma,
            dma,
            dma((2,)),
            dma((3,)),
            dma((3,)),
        ],
        compiler_params=pltpu.CompilerParams(
            collective_id=0, has_side_effects=True, vmem_limit_bytes=59 * 1024 * 1024
        ),
        cost_estimate=pl.CostEstimate(
            flops=6 * V * POINTS * D, bytes_accessed=5_000_000, transcendentals=8_000_000
        ),
    )(
        counts,
        area,
        offset.reshape(1, V),
        var_weight.reshape(1, V),
        proj_weight,
        hidden_state.reshape(POINTS, D),
        truth,
    )
    factor = GRAD_SCALE / math.sqrt(NB * total_rows * CAP)
    latent, wgrad, bias, loss = pl.pallas_call(
        lambda *refs: finish_kernel(factor, *refs),
        out_shape=(
            jax.ShapeDtypeStruct((POINTS, D), bf16),
            jax.ShapeDtypeStruct((V, D), F32),
            jax.ShapeDtypeStruct((1, V), F32),
            jax.ShapeDtypeStruct((1, 1), F32),
        ),
        in_specs=[vmem, vmem],
        out_specs=(hbm, hbm, vmem, vmem),
        scratch_shapes=[pltpu.VMEM((V, D), F32), dma((5,))],
        compiler_params=pltpu.CompilerParams(vmem_limit_bytes=16 * 1024 * 1024),
        cost_estimate=pl.CostEstimate(flops=V * D, bytes_accessed=5_000_000, transcendentals=0),
    )(latent, sums)
    return latent.reshape(hidden_state.shape), wgrad, bias.reshape(V), loss.reshape(())


def solution(mesh):
    total_rows = ROWS * mesh.shape["space"]

    def step(*args):
        return per_device(*args, total_rows)

    return jax.shard_map(
        step,
        mesh=mesh,
        in_specs=(
            P("member", "space", None, None),
            P(),
            P(),
            P(None, "space", None),
            P("space"),
            P(),
        ),
        out_specs=(P("member", "space", None, None), P(), P(), P()),
        check_vma=False,
    )
```

```python
import math

import numpy as np

import jax
import jax.numpy as jnp
from jax import lax
from jax.experimental import pallas as pl
from jax.experimental.pallas import tpu as pltpu
from jax.sharding import PartitionSpec as P

SMOOTHING = 0.05
FAIRNESS = 0.95
GRAD_SCALE = 16.0
LATITUDE_SPAN = 80.0

V = 100
VP = 104
GP = 112
D = 1024
ROWS = 4
CAP = 512
POINTS = ROWS * CAP
BLOCK = 256
NB = 8
NT = 25
CHUNKS = ((0, 8), (8, 8), (16, 4), (20, 5))
NC = len(CHUNKS)
GROUPS = ((0, 64), (64, 16))
LAST = 80
MESH = pl.DeviceIdType.MESH
F32 = jnp.float32
EPS2 = SMOOTHING * SMOOTHING
COEFF = FAIRNESS / (NB * (NB - 1)) + (1.0 - FAIRNESS) / (NB * NB)


def column(row):
    n = row.shape[1]
    here = lax.broadcasted_iota(jnp.int32, (VP, n), 0) == lax.broadcasted_iota(
        jnp.int32, (VP, n), 1
    )
    return jnp.sum(jnp.where(here, jnp.broadcast_to(row, (VP, n)), 0.0), axis=1, keepdims=True)


def exchange_kernel(
    counts_ref,
    area_ref,
    offset_ref,
    scale_ref,
    weight_hbm,
    hidden_hbm,
    truth_hbm,
    latent_ref,
    sums_ref,
    weight,
    hbuf,
    truth,
    field,
    met,
    signs,
    back,
    obs,
    grad,
    loss_acc,
    bias_acc,
    scale,
    part,
    part_in,
    plane,
    pair,
    y_in,
    z_out,
    z_in,
    own_all,
    out_in,
    last,
    last_in,
    last_mid,
    last_z,
    last_own,
    last_out,
    load_sem,
    side_sem,
    fwd_send,
    fwd_recv,
    ret_send,
    ret_recv,
    part_send,
    part_recv,
    y_send,
    y_recv,
    z_send,
    z_recv,
    row_send,
    row_recv,
    out_send,
    out_recv,
    last_send,
    last_recv,
):
    member = lax.axis_index("member")
    space = lax.axis_index("space")
    y, z_hi = lax.div(member, 2), lax.rem(member, 2)
    z_lo, q = lax.div(space, 8), lax.rem(space, 8)
    x, core = lax.div(q, 2), lax.rem(q, 2)
    z = z_hi * 4 + z_lo
    in_plane = (x * 4 + y) * 2 + core

    def at(xx, yy, zz, cc):
        return (yy * 2 + lax.div(zz, 4), lax.rem(zz, 4) * 8 + xx * 2 + cc)

    def beside(j):
        return at(lax.div(j, 2), y, z, lax.rem(j, 2))

    def plane_device(w):
        return at(lax.div(w, 8), lax.rem(lax.div(w, 2), 4), z, lax.rem(w, 2))

    def stack_device(zz):
        return at(x, y, zz, core)

    def block_points(b):
        return pl.ds(pl.multiple_of(b * BLOCK, BLOCK), BLOCK)

    def load(t):
        rows = block_points(lax.rem(member + t, NB))
        return pltpu.make_async_copy(hidden_hbm.at[rows], hbuf.at[rows], load_sem.at[t - 1])

    load_weight = pltpu.make_async_copy(weight_hbm, weight, side_sem.at[0])
    load_weight.start()
    for t in range(1, NB + 1):
        load(t).start()
    load_truth = pltpu.make_async_copy(truth_hbm, truth, side_sem.at[1])
    load_truth.start()

    barrier = pltpu.get_barrier_semaphore()

    def greet(device):
        pl.semaphore_signal(barrier, inc=1, device_id=device, device_id_type=MESH)

    for t in range(1, 32):
        greet(plane_device(lax.rem(in_plane + t, 32)))
    for t in range(1, 8):
        greet(stack_device(lax.rem(z + t, 8)))
    for t in range(1, 4):
        greet(at(x, lax.rem(y + t, 4), lax.rem(z + 2, 8), core))
        greet(at(x, lax.rem(y + t, 4), lax.rem(z + 6, 8), core))

    offsets = column(offset_ref[...])[0:V]
    scales = jnp.broadcast_to(column(scale_ref[...]), (VP, 128))
    for i in range(NT // 2):
        scale[2 * i] = scales[8 * i : 8 * i + 8]
        scale[2 * i + 1] = scales[8 * i : 8 * i + 8]
    scale[NT - 1] = jnp.concatenate([scales[96:V], scales[96:V]], axis=0)
    loss_acc[...] = jnp.zeros_like(loss_acc)
    bias_acc[...] = jnp.zeros_like(bias_acc)

    lane = lax.broadcasted_iota(jnp.int32, (1, 128), 1)
    sub = lax.broadcasted_iota(jnp.int32, (8, 128), 0)

    def live(b, h):
        return lane + (lax.rem(b, 2) * 2 + h) * 128 < counts_ref[lax.div(b, 2)]

    def point_weights(b, factor):
        area = area_ref[space * ROWS + lax.div(b, 2)] * factor
        halves = [jnp.where(live(b, h), area, 0.0) for h in range(2)]
        return halves, jnp.where(sub < 4, halves[0], halves[1])

    def send_forecast(c, b):
        block = pl.ds(*CHUNKS[c])
        return pltpu.make_async_remote_copy(
            src_ref=field.at[b, block],
            dst_ref=met.at[member, block],
            send_sem=fwd_send,
            recv_sem=fwd_recv.at[c],
            device_id=at(x, lax.div(b, 2), lax.rem(z_lo + 2 + 4 * lax.rem(b, 2), 8), core),
            device_id_type=MESH,
        )

    for t in range(1, NB + 1):
        load(t).wait()
        if t == 1:
            load_weight.wait()
        b = lax.rem(member + t, NB)
        product = lax.dot_general(
            weight[...],
            hbuf[block_points(b), :],
            (((1,), (1,)), ((), ())),
            preferred_element_type=F32,
        )
        forecast = product + offsets
        halves = [
            jnp.where(live(b, h), forecast[:, h * 128 : (h + 1) * 128], 0.0) for h in range(2)
        ]
        for i in range(NT // 2):
            for h in range(2):
                field[b, 2 * i + h] = halves[h][8 * i : 8 * i + 8]
        field[b, NT - 1] = jnp.concatenate([halves[0][96:V], halves[1][96:V]], axis=0)
        if t == 1:
            pl.semaphore_wait(barrier, 44)
        for c in range(2):
            send_forecast(c, b).start()
    for c in range(2, NC):
        for t in range(1, NB + 1):
            send_forecast(c, lax.rem(member + t, NB)).start()

    def misfit(b, tile, target, weight_here):
        gap = field[b, tile] - target
        square = gap * gap + EPS2
        inverse = lax.rsqrt(square)
        factor = weight_here * scale[tile]
        obs[b, tile] = factor * (gap * inverse)
        return factor * (square * inverse - SMOOTHING)

    def target(b, v, h):
        first = (b % 2) * BLOCK + h * 128
        return truth[v, b // 2, first : first + 128]

    def misfits():
        load_truth.wait()

        @pl.loop(0, NT // 2)
        def _(i):
            at_v = pl.ds(pl.multiple_of(i * 8, 8), 8)
            total = jnp.zeros((8, 128), F32)
            for b in range(NB):
                halves, _ = point_weights(b, 1.0 / NB)
                for h in range(2):
                    total += misfit(b, 2 * i + h, target(b, at_v, h), halves[h])
            loss_acc[...] += total

        total = jnp.zeros((8, 128), F32)
        for b in range(NB):
            _, both = point_weights(b, 1.0 / NB)
            tail = pl.ds(96, 4)
            goal = jnp.concatenate([target(b, tail, 0), target(b, tail, 1)], axis=0)
            total += misfit(b, NT - 1, goal, both)
        loss_acc[...] += total

    z_from = lax.rem(z + 2, 4)
    block_here = y * 2 + lax.div(lax.rem(z - z_from - 2 + 16, 8), 4)
    space_from = z_from * 8 + q
    area_here = area_ref[space_from * ROWS + y]

    def send_sign(c, m):
        block = pl.ds(*CHUNKS[c])
        return pltpu.make_async_remote_copy(
            src_ref=signs.at[m, block],
            dst_ref=back.at[block_here, block],
            send_sem=ret_send,
            recv_sem=ret_recv.at[c],
            device_id=(m, space_from),
            device_id_type=MESH,
        )

    def arrive(ref, sem):
        pltpu.make_async_copy(ref, ref, sem).wait()

    def meet(block):
        values = [met[m, block] for m in range(NB)]
        sums = [None] * NB
        roots = None
        for m in range(NB):
            for k in range(m + 1, NB):
                gap = values[m] - values[k]
                square = gap * gap + EPS2
                inverse = lax.rsqrt(square)
                sign = gap * inverse
                root = square * inverse
                roots = root if roots is None else roots + root
                sums[m] = sign if sums[m] is None else sums[m] + sign
                sums[k] = -sign if sums[k] is None else sums[k] - sign
        for m in range(NB):
            signs[m, block] = sums[m]
        spread = (roots - (NB * (NB - 1) // 2) * SMOOTHING) * scale[block]
        loss_acc[...] += (-COEFF * area_here) * jnp.sum(spread, axis=0)

    def pairs(c):
        first, n = CHUNKS[c]
        arrive(met.at[:, pl.ds(first, n)], fwd_recv.at[c])

        @pl.loop(0, n // 2)
        def _(i):
            meet(pl.ds(first + 2 * i, 2))

        if n % 2:
            meet(pl.ds(first + n - 1, 1))

        for t in range(1, NB + 1):
            send_sign(c, lax.rem(member + t, NB)).start()

    def weight_sum(v0, rows, first):
        return jnp.dot(
            grad[v0 : v0 + rows, :], hbuf[:, pl.ds(first, 256)], preferred_element_type=F32
        )

    def gradient(c):
        first, n = CHUNKS[c]
        v0 = 4 * first
        arrive(back.at[:, pl.ds(first, n)], ret_recv.at[c])

        @pl.loop(0, NB)
        def _(b):
            halves, both = point_weights(b, COEFF)

            def value(tile, weight_here):
                result = obs[b, tile] - (weight_here * scale[tile]) * back[b, tile]
                bias_acc[tile] += result
                return result

            pieces = [
                [value(first + 2 * i + h, halves[h]) for i in range(n // 2)] for h in range(2)
            ]
            if n % 2:
                tail = value(NT - 1, both)
                for h in range(2):
                    pieces[h] += [tail[4 * h : 4 * h + 4], jnp.zeros((GP - V, 128), F32)]
            for h in range(2):
                stacked = jnp.concatenate(pieces[h], axis=0)
                points = pl.ds(pl.multiple_of(b * BLOCK + h * 128, 128), 128)
                grad[v0 : v0 + stacked.shape[0], points] = stacked.astype(jnp.bfloat16)

        if n % 2:
            return

        @pl.loop(0, 4)
        def _(j):
            piece = weight_sum(v0, 4 * n, pl.multiple_of(j * 256, 256))
            for k in range(2):
                part[2 * j + k, v0 : v0 + 4 * n, :] = piece[:, k * 128 : (k + 1) * 128]

    def extras():
        rows = []
        for i in range(NT // 2):
            rows.append(bias_acc[2 * i] + bias_acc[2 * i + 1])
        tail = bias_acc[NT - 1]
        rows += [tail[0:4] + tail[4:8], jnp.zeros((VP - V, 128), F32)]
        bias = jnp.sum(jnp.concatenate(rows, axis=0), axis=1, keepdims=True)
        eye = lax.broadcasted_iota(jnp.int32, (VP, 128), 0) == lax.broadcasted_iota(
            jnp.int32, (VP, 128), 1
        )
        extra = jnp.sum(jnp.where(eye, bias, 0.0), axis=0, keepdims=True)
        loss_here = jnp.sum(jnp.sum(loss_acc[...], axis=0, keepdims=True), axis=1, keepdims=True)
        points_here = jnp.float32(0.0)
        for r in range(ROWS):
            points_here += area_ref[space * ROWS + r] * counts_ref[r].astype(F32)
        extra = jnp.where(lane == V, loss_here, extra)
        extra = jnp.where(lane == V + 1, points_here, extra)
        return extra

    def tiles(g):
        first, n = GROUPS[g]
        return first // 8, (first + n) // 8

    def send_part(g, t):
        rows = pl.ds(*GROUPS[g])
        j = lax.rem(q + t, 8)
        return pltpu.make_async_remote_copy(
            src_ref=part.at[j, rows],
            dst_ref=part_in.at[t - 1, rows],
            send_sem=part_send,
            recv_sem=part_recv.at[g],
            device_id=beside(j),
            device_id_type=MESH,
        )

    def send_plane(g, t):
        yy = lax.rem(y + t, 4)
        return pltpu.make_async_remote_copy(
            src_ref=plane.at[yy] if g == 0 else pair,
            dst_ref=y_in.at[g, y],
            send_sem=y_send.at[g],
            recv_sem=y_recv.at[g],
            device_id=at(x, yy, z, core),
            device_id_type=MESH,
        )

    def send_across(g, t):
        return pltpu.make_async_remote_copy(
            src_ref=z_out.at[g],
            dst_ref=z_in.at[g, z],
            send_sem=z_send.at[g],
            recv_sem=z_recv.at[g],
            device_id=at(x, y, lax.rem(z + t, 8), core),
            device_id_type=MESH,
        )

    def send_row(t):
        block = own_all.at[pl.ds(2 * y, 2)]
        return pltpu.make_async_remote_copy(
            src_ref=block,
            dst_ref=block,
            send_sem=row_send,
            recv_sem=row_recv,
            device_id=at(x, lax.rem(y + t, 4), z, core),
            device_id_type=MESH,
        )

    def send_out(g, t):
        first, end = tiles(g)
        block = pl.ds(first, end - first)
        return pltpu.make_async_remote_copy(
            src_ref=own_all.at[block],
            dst_ref=out_in.at[t, block],
            send_sem=out_send,
            recv_sem=out_recv.at[g],
            device_id=beside(lax.rem(q + t, 8)),
            device_id_type=MESH,
        )

    def send_all(send, number):
        for t in range(1, number):
            send(t).start()

    def send_parts(g):
        send_all(lambda t: send_part(g, t), 8)

    def sum_beside(g):
        arrive(part_in.at[:, pl.ds(*GROUPS[g])], part_recv.at[g])

        def column_sum(o):
            at_v = pl.ds(pl.multiple_of(o * 8, 8), 8)
            value = part[q, at_v, :]
            for t in range(7):
                value += part_in[t, at_v, :]
            return value

        if g == 0:

            @pl.loop(0, 4)
            def _(yy):
                for i in range(2):
                    plane[yy, i] = column_sum(2 * yy + i)

            y_in[g, y] = plane[y]
        else:
            for i in range(2):
                pair[i] = column_sum(8 + i)
            y_in[g, y] = pair[...]
        send_all(lambda t: send_plane(g, t), 4)

    def sum_plane(g):
        arrive(y_in.at[g, pl.ds(0, 3)], y_recv.at[g])
        value = y_in[g, 0]
        for yy in range(1, 4):
            value += y_in[g, yy]
        z_out[g] = value
        z_in[g, z] = value
        send_all(lambda t: send_across(g, t), 8)

    def spread_out(g):
        first, end = tiles(g)
        send_all(lambda t: send_out(g, t), 8)
        out_in[0, first:end] = own_all[first:end]

    def sum_across(g):
        arrive(z_in.at[g, pl.ds(0, 7)], z_recv.at[g])
        value = z_in[g, 0]
        for zz in range(1, 8):
            value += z_in[g, zz]
        if g == 0:
            own_all[pl.ds(2 * y, 2)] = value
            send_all(send_row, 4)
        else:
            own_all[8:10] = value
            spread_out(1)

    def collect_rows():
        arrive(own_all.at[pl.ds(0, 6)], row_recv)
        spread_out(0)

    def collect(g):
        first, end = tiles(g)
        arrive(out_in.at[pl.ds(1, 7), pl.ds(first, end - first)], out_recv.at[g])

        @pl.loop(0, 8)
        def _(t):
            cols = pl.ds(pl.multiple_of(lax.rem(q - t + 8, 8) * 128, 128), 128)
            for o in range(first, end):
                sums_ref[o * 8 : (o + 1) * 8, cols] = out_in[t, o]

    def last_copy(phase, to):
        if phase == 1:
            src, dst, device = last_mid, last_z.at[z], stack_device(to)
        else:
            src = last.at[to] if phase == 0 else last_own
            dst = (last_in if phase == 0 else last_out).at[in_plane]
            device = plane_device(to)
        return pltpu.make_async_remote_copy(
            src_ref=src,
            dst_ref=dst,
            send_sem=last_send.at[phase],
            recv_sem=last_recv.at[phase],
            device_id=device,
            device_id_type=MESH,
        )

    def last_sum(phase, source, number):
        arrive(source.at[pl.ds(0, number - 1)], last_recv.at[phase])
        value = source[0]
        for t in range(1, number):
            value += source[t]
        return value

    def last_scatter():
        extra = extras()
        for j in (1, 2, 3, 0):
            piece = weight_sum(LAST, GP - LAST, j * 256)
            for k in range(2):
                block = piece[:, k * 128 : (k + 1) * 128]
                for i in range(12):
                    last[8 * j + 4 * k + i // 3, i % 3] = block[2 * i : 2 * i + 2]
            if j == 0:
                last[3, 1, 0:1, :] = extra
            for p in range(8 * j, 8 * j + 8):

                @pl.when(in_plane != p)
                def _():
                    last_copy(0, p).start()

        last_in[in_plane] = last[in_plane]

    def last_across():
        value = last_sum(0, last_in, 32)
        last_mid[...] = value
        for t in range(1, 8):
            last_copy(1, lax.rem(z + t, 8)).start()
        last_z[z] = value

    def last_gather():
        value = last_sum(1, last_z, 8)
        last_own[...] = value
        for t in range(1, 32):
            last_copy(2, lax.rem(in_plane + t, 32)).start()
        last_out[in_plane] = value

    def last_collect():
        arrive(last_out.at[pl.ds(0, 31)], last_recv.at[2])

        @pl.loop(0, 8)
        def _(j):
            cols = pl.ds(pl.multiple_of(j * 128, 128), 128)
            for i in range(12):
                rows = slice(LAST + 2 * i, LAST + 2 * i + 2)
                sums_ref[rows, cols] = last_out[4 * j + i // 3, i % 3]

    def latent(first, end):
        @pl.loop(first, end)
        def _(b):
            points = block_points(b)
            value = lax.dot_general(
                grad[0:V, points], weight[...], (((0,), (0,)), ((), ())), preferred_element_type=F32
            )
            latent_ref[points, :] = (GRAD_SCALE * value).astype(jnp.bfloat16)

    pairs(0)
    pairs(1)
    misfits()
    pairs(2)
    pairs(3)
    gradient(0)
    gradient(1)
    send_parts(0)
    gradient(2)
    send_parts(1)
    sum_beside(0)
    gradient(3)
    last_scatter()
    sum_plane(0)
    sum_beside(1)
    latent(0, 2)
    last_across()
    sum_across(0)
    sum_plane(1)
    latent(2, 4)
    last_gather()
    collect_rows()
    sum_across(1)
    latent(4, 8)
    last_collect()
    collect(0)
    collect(1)

    arrive(field, fwd_send)
    arrive(signs, ret_send)
    arrive(part.at[pl.ds(0, 7)], part_send)
    arrive(plane.at[pl.ds(0, 3)], y_send.at[0])
    arrive(plane.at[pl.ds(0, 3)], y_send.at[1])
    for g in range(len(GROUPS)):
        arrive(z_in.at[g, pl.ds(0, 7)], z_send.at[g])
    arrive(own_all.at[pl.ds(0, 6)], row_send)
    arrive(out_in.at[pl.ds(0, 7)], out_send)
    for phase, number in enumerate((31, 7, 31)):
        arrive(last.at[pl.ds(0, number)], last_send.at[phase])


def finish_kernel(factor, latent, sums, latent_hbm, wgrad_hbm, bias_ref, loss_ref, wgrad, sem):
    stores = []
    for b in range(4):
        rows = pl.ds(b * CAP, CAP)
        stores.append(pltpu.make_async_copy(latent.at[rows], latent_hbm.at[rows], sem.at[b]))
        stores[-1].start()
    wgrad[...] = sums[0:V, :] * factor
    stores.append(pltpu.make_async_copy(wgrad, wgrad_hbm, sem.at[4]))
    stores[-1].start()
    extra = sums[V : V + 1, 0:128]
    lane = lax.broadcasted_iota(jnp.int32, (1, 128), 1)
    total = jnp.sum(jnp.where(lane == V, extra, 0.0), axis=1, keepdims=True)
    points = jnp.sum(jnp.where(lane == V + 1, extra, 0.0), axis=1, keepdims=True)
    bias_ref[...] = extra[:, 0:V] * factor
    loss_ref[...] = total / (V * (points * (1.0 / NB)))
    for store in stores:
        store.wait()


def per_device(hidden_state, proj_weight, offset, truth, counts, var_weight, total_rows):
    latitude = (np.arange(total_rows) + 0.5) * (LATITUDE_SPAN / total_rows) * (math.pi / 180.0)
    area = jnp.asarray(np.cos(latitude), dtype=F32)
    vmem = pl.BlockSpec(memory_space=pltpu.VMEM)
    smem = pl.BlockSpec(memory_space=pltpu.SMEM)
    hbm = pl.BlockSpec(memory_space=pltpu.HBM)
    dma = pltpu.SemaphoreType.DMA
    bf16 = jnp.bfloat16
    blocks = pltpu.VMEM((NB, NT, 8, 128), F32)
    few_rows = (3, 2, 128)
    latent, sums = pl.pallas_call(
        exchange_kernel,
        out_shape=(
            pltpu.VMEM((POINTS, D), bf16),
            pltpu.VMEM((VP, D), F32),
        ),
        in_specs=[smem, smem, vmem, vmem, hbm, hbm, hbm],
        out_specs=(vmem, vmem),
        scratch_shapes=[
            pltpu.VMEM((V, D), bf16),
            pltpu.VMEM((POINTS, D), bf16),
            pltpu.VMEM((V, ROWS, CAP), F32),
            blocks,
            blocks,
            blocks,
            blocks,
            blocks,
            pltpu.VMEM((GP, POINTS), bf16),
            pltpu.VMEM((8, 128), F32),
            pltpu.VMEM((NT, 8, 128), F32),
            pltpu.VMEM((NT, 8, 128), F32),
            pltpu.VMEM((8, LAST, 128), F32),
            pltpu.VMEM((7, LAST, 128), F32),
            pltpu.VMEM((4, 2, 8, 128), F32),
            pltpu.VMEM((2, 8, 128), F32),
            pltpu.VMEM((2, 4, 2, 8, 128), F32),
            pltpu.VMEM((2, 2, 8, 128), F32),
            pltpu.VMEM((2, 8, 2, 8, 128), F32),
            pltpu.VMEM((LAST // 8, 8, 128), F32),
            pltpu.VMEM((8, LAST // 8, 8, 128), F32),
            pltpu.VMEM((32, *few_rows), F32),
            pltpu.VMEM((32, *few_rows), F32),
            pltpu.VMEM(few_rows, F32),
            pltpu.VMEM((8, *few_rows), F32),
            pltpu.VMEM(few_rows, F32),
            pltpu.VMEM((32, *few_rows), F32),
            dma((NB,)),
            dma((2,)),
            dma,
            dma((NC,)),
            dma,
            dma((NC,)),
            dma,
            dma((2,)),
            dma((2,)),
            dma((2,)),
            dma((2,)),
            dma((2,)),
            dma,
            dma,
            dma,
            dma((2,)),
            dma((3,)),
            dma((3,)),
        ],
        compiler_params=pltpu.CompilerParams(
            collective_id=0, has_side_effects=True, vmem_limit_bytes=59 * 1024 * 1024
        ),
        cost_estimate=pl.CostEstimate(
            flops=6 * V * POINTS * D, bytes_accessed=5_000_000, transcendentals=8_000_000
        ),
    )(
        counts,
        area,
        offset.reshape(1, V),
        var_weight.reshape(1, V),
        proj_weight,
        hidden_state.reshape(POINTS, D),
        truth,
    )
    factor = GRAD_SCALE / math.sqrt(NB * total_rows * CAP)
    latent, wgrad, bias, loss = pl.pallas_call(
        lambda *refs: finish_kernel(factor, *refs),
        out_shape=(
            jax.ShapeDtypeStruct((POINTS, D), bf16),
            jax.ShapeDtypeStruct((V, D), F32),
            jax.ShapeDtypeStruct((1, V), F32),
            jax.ShapeDtypeStruct((1, 1), F32),
        ),
        in_specs=[vmem, vmem],
        out_specs=(hbm, hbm, vmem, vmem),
        scratch_shapes=[pltpu.VMEM((V, D), F32), dma((5,))],
        compiler_params=pltpu.CompilerParams(vmem_limit_bytes=16 * 1024 * 1024),
        cost_estimate=pl.CostEstimate(flops=V * D, bytes_accessed=5_000_000, transcendentals=0),
    )(latent, sums)
    return latent.reshape(hidden_state.shape), wgrad, bias.reshape(V), loss.reshape(())


def solution(mesh):
    total_rows = ROWS * mesh.shape["space"]

    def step(*args):
        return per_device(*args, total_rows)

    return jax.shard_map(
        step,
        mesh=mesh,
        in_specs=(
            P("member", "space", None, None),
            P(),
            P(),
            P(None, "space", None),
            P("space"),
            P(),
        ),
        out_specs=(P("member", "space", None, None), P(), P(), P()),
        check_vma=False,
    )
```

```python
import math

import numpy as np

import jax
import jax.numpy as jnp
from jax import lax
from jax.experimental import pallas as pl
from jax.experimental.pallas import tpu as pltpu
from jax.sharding import PartitionSpec as P

SMOOTHING = 0.05
FAIRNESS = 0.95
GRAD_SCALE = 16.0
LATITUDE_SPAN = 80.0

V = 100
VP = 104
GP = 112
D = 1024
ROWS = 4
CAP = 512
POINTS = ROWS * CAP
BLOCK = 256
NB = 8
NT = 25
CHUNKS = ((0, 8), (8, 8), (16, 4), (20, 5))
NC = len(CHUNKS)
GROUPS = ((0, 64), (64, 16))
LAST = 80
MESH = pl.DeviceIdType.MESH
F32 = jnp.float32
EPS2 = SMOOTHING * SMOOTHING
COEFF = FAIRNESS / (NB * (NB - 1)) + (1.0 - FAIRNESS) / (NB * NB)


def column(row):
    n = row.shape[1]
    here = lax.broadcasted_iota(jnp.int32, (VP, n), 0) == lax.broadcasted_iota(
        jnp.int32, (VP, n), 1
    )
    return jnp.sum(jnp.where(here, jnp.broadcast_to(row, (VP, n)), 0.0), axis=1, keepdims=True)


def exchange_kernel(
    counts_ref,
    area_ref,
    offset_ref,
    scale_ref,
    weight_hbm,
    hidden_hbm,
    truth_hbm,
    latent_ref,
    sums_ref,
    weight,
    hbuf,
    truth,
    field,
    met,
    signs,
    back,
    obs,
    grad,
    loss_acc,
    bias_acc,
    scale,
    part,
    part_in,
    plane,
    pair,
    y_in,
    z_out,
    z_in,
    own_all,
    out_in,
    last,
    last_in,
    last_mid,
    last_z,
    last_own,
    last_out,
    load_sem,
    side_sem,
    fwd_send,
    fwd_recv,
    ret_send,
    ret_recv,
    part_send,
    part_recv,
    y_send,
    y_recv,
    z_send,
    z_recv,
    row_send,
    row_recv,
    out_send,
    out_recv,
    last_send,
    last_recv,
):
    member = lax.axis_index("member")
    space = lax.axis_index("space")
    y, z_hi = lax.div(member, 2), lax.rem(member, 2)
    z_lo, q = lax.div(space, 8), lax.rem(space, 8)
    x, core = lax.div(q, 2), lax.rem(q, 2)
    z = z_hi * 4 + z_lo
    in_plane = (x * 4 + y) * 2 + core

    def at(xx, yy, zz, cc):
        return (yy * 2 + lax.div(zz, 4), lax.rem(zz, 4) * 8 + xx * 2 + cc)

    def beside(j):
        return at(lax.div(j, 2), y, z, lax.rem(j, 2))

    def plane_device(w):
        return at(lax.div(w, 8), lax.rem(lax.div(w, 2), 4), z, lax.rem(w, 2))

    def stack_device(zz):
        return at(x, y, zz, core)

    def block_points(b):
        return pl.ds(pl.multiple_of(b * BLOCK, BLOCK), BLOCK)

    def load(t):
        rows = block_points(lax.rem(member + t, NB))
        return pltpu.make_async_copy(hidden_hbm.at[rows], hbuf.at[rows], load_sem.at[t - 1])

    load_weight = pltpu.make_async_copy(weight_hbm, weight, side_sem.at[0])
    load_weight.start()
    for t in range(1, NB + 1):
        load(t).start()
    load_truth = pltpu.make_async_copy(truth_hbm, truth, side_sem.at[1])
    load_truth.start()

    barrier = pltpu.get_barrier_semaphore()

    def greet(device):
        pl.semaphore_signal(barrier, inc=1, device_id=device, device_id_type=MESH)

    for t in range(1, 32):
        greet(plane_device(lax.rem(in_plane + t, 32)))
    for t in range(1, 8):
        greet(stack_device(lax.rem(z + t, 8)))
    for t in range(1, 4):
        greet(at(x, lax.rem(y + t, 4), lax.rem(z + 2, 8), core))
        greet(at(x, lax.rem(y + t, 4), lax.rem(z + 6, 8), core))

    offsets = column(offset_ref[...])[0:V]
    scales = jnp.broadcast_to(column(scale_ref[...]), (VP, 128))
    for i in range(NT // 2):
        scale[2 * i] = scales[8 * i : 8 * i + 8]
        scale[2 * i + 1] = scales[8 * i : 8 * i + 8]
    scale[NT - 1] = jnp.concatenate([scales[96:V], scales[96:V]], axis=0)
    loss_acc[...] = jnp.zeros_like(loss_acc)
    bias_acc[...] = jnp.zeros_like(bias_acc)

    lane = lax.broadcasted_iota(jnp.int32, (1, 128), 1)
    sub = lax.broadcasted_iota(jnp.int32, (8, 128), 0)

    def live(b, h):
        return lane + (lax.rem(b, 2) * 2 + h) * 128 < counts_ref[lax.div(b, 2)]

    def point_weights(b, factor):
        area = area_ref[space * ROWS + lax.div(b, 2)] * factor
        halves = [jnp.where(live(b, h), area, 0.0) for h in range(2)]
        return halves, jnp.where(sub < 4, halves[0], halves[1])

    def send_forecast(c, b):
        block = pl.ds(*CHUNKS[c])
        return pltpu.make_async_remote_copy(
            src_ref=field.at[b, block],
            dst_ref=met.at[member, block],
            send_sem=fwd_send,
            recv_sem=fwd_recv.at[c],
            device_id=at(x, lax.div(b, 2), lax.rem(z_lo + 2 + 4 * lax.rem(b, 2), 8), core),
            device_id_type=MESH,
        )

    for t in range(1, NB + 1):
        load(t).wait()
        if t == 1:
            load_weight.wait()
        b = lax.rem(member + t, NB)
        product = lax.dot_general(
            weight[...],
            hbuf[block_points(b), :],
            (((1,), (1,)), ((), ())),
            preferred_element_type=F32,
        )
        forecast = product + offsets
        halves = [
            jnp.where(live(b, h), forecast[:, h * 128 : (h + 1) * 128], 0.0) for h in range(2)
        ]
        for i in range(NT // 2):
            for h in range(2):
                field[b, 2 * i + h] = halves[h][8 * i : 8 * i + 8]
        field[b, NT - 1] = jnp.concatenate([halves[0][96:V], halves[1][96:V]], axis=0)
        if t == 1:
            pl.semaphore_wait(barrier, 44)
        for c in range(2):
            send_forecast(c, b).start()
    for c in range(2, NC):
        for t in range(1, NB + 1):
            send_forecast(c, lax.rem(member + t, NB)).start()

    def misfit(b, tile, target, weight_here):
        gap = field[b, tile] - target
        square = gap * gap + EPS2
        inverse = lax.rsqrt(square)
        factor = weight_here * scale[tile]
        obs[b, tile] = factor * (gap * inverse)
        return factor * (square * inverse - SMOOTHING)

    def target(b, v, h):
        first = (b % 2) * BLOCK + h * 128
        return truth[v, b // 2, first : first + 128]

    def misfits():
        load_truth.wait()

        @pl.loop(0, NT // 2)
        def _(i):
            at_v = pl.ds(pl.multiple_of(i * 8, 8), 8)
            total = jnp.zeros((8, 128), F32)
            for b in range(NB):
                halves, _ = point_weights(b, 1.0 / NB)
                for h in range(2):
                    total += misfit(b, 2 * i + h, target(b, at_v, h), halves[h])
            loss_acc[...] += total

        total = jnp.zeros((8, 128), F32)
        for b in range(NB):
            _, both = point_weights(b, 1.0 / NB)
            tail = pl.ds(96, 4)
            goal = jnp.concatenate([target(b, tail, 0), target(b, tail, 1)], axis=0)
            total += misfit(b, NT - 1, goal, both)
        loss_acc[...] += total

    z_from = lax.rem(z + 2, 4)
    block_here = y * 2 + lax.div(lax.rem(z - z_from - 2 + 16, 8), 4)
    space_from = z_from * 8 + q
    area_here = area_ref[space_from * ROWS + y]

    def send_sign(c, m):
        block = pl.ds(*CHUNKS[c])
        return pltpu.make_async_remote_copy(
            src_ref=signs.at[m, block],
            dst_ref=back.at[block_here, block],
            send_sem=ret_send,
            recv_sem=ret_recv.at[c],
            device_id=(m, space_from),
            device_id_type=MESH,
        )

    def arrive(ref, sem):
        pltpu.make_async_copy(ref, ref, sem).wait()

    def meet(block):
        values = [met[m, block] for m in range(NB)]
        sums = [None] * NB
        roots = None
        for m in range(NB):
            for k in range(m + 1, NB):
                gap = values[m] - values[k]
                square = gap * gap + EPS2
                inverse = lax.rsqrt(square)
                sign = gap * inverse
                root = square * inverse
                roots = root if roots is None else roots + root
                sums[m] = sign if sums[m] is None else sums[m] + sign
                sums[k] = -sign if sums[k] is None else sums[k] - sign
        for m in range(NB):
            signs[m, block] = sums[m]
        spread = (roots - (NB * (NB - 1) // 2) * SMOOTHING) * scale[block]
        loss_acc[...] += (-COEFF * area_here) * jnp.sum(spread, axis=0)

    def pairs(c):
        first, n = CHUNKS[c]
        arrive(met.at[:, pl.ds(first, n)], fwd_recv.at[c])

        @pl.loop(0, n // 2)
        def _(i):
            meet(pl.ds(first + 2 * i, 2))

        if n % 2:
            meet(pl.ds(first + n - 1, 1))

        for t in range(1, NB + 1):
            send_sign(c, lax.rem(member + t, NB)).start()

    def weight_sum(v0, rows, first):
        return jnp.dot(
            grad[v0 : v0 + rows, :], hbuf[:, pl.ds(first, 256)], preferred_element_type=F32
        )

    def gradient(c):
        first, n = CHUNKS[c]
        v0 = 4 * first
        arrive(back.at[:, pl.ds(first, n)], ret_recv.at[c])

        @pl.loop(0, NB)
        def _(b):
            halves, both = point_weights(b, COEFF)

            def value(tile, weight_here):
                result = obs[b, tile] - (weight_here * scale[tile]) * back[b, tile]
                bias_acc[tile] += result
                return result

            pieces = [
                [value(first + 2 * i + h, halves[h]) for i in range(n // 2)] for h in range(2)
            ]
            if n % 2:
                tail = value(NT - 1, both)
                for h in range(2):
                    pieces[h] += [tail[4 * h : 4 * h + 4], jnp.zeros((GP - V, 128), F32)]
            for h in range(2):
                stacked = jnp.concatenate(pieces[h], axis=0)
                points = pl.ds(pl.multiple_of(b * BLOCK + h * 128, 128), 128)
                grad[v0 : v0 + stacked.shape[0], points] = stacked.astype(jnp.bfloat16)

        if n % 2:
            return

        @pl.loop(0, 4)
        def _(j):
            piece = weight_sum(v0, 4 * n, pl.multiple_of(j * 256, 256))
            for k in range(2):
                part[2 * j + k, v0 : v0 + 4 * n, :] = piece[:, k * 128 : (k + 1) * 128]

    def extras():
        rows = []
        for i in range(NT // 2):
            rows.append(bias_acc[2 * i] + bias_acc[2 * i + 1])
        tail = bias_acc[NT - 1]
        rows += [tail[0:4] + tail[4:8], jnp.zeros((VP - V, 128), F32)]
        bias = jnp.sum(jnp.concatenate(rows, axis=0), axis=1, keepdims=True)
        eye = lax.broadcasted_iota(jnp.int32, (VP, 128), 0) == lax.broadcasted_iota(
            jnp.int32, (VP, 128), 1
        )
        extra = jnp.sum(jnp.where(eye, bias, 0.0), axis=0, keepdims=True)
        loss_here = jnp.sum(jnp.sum(loss_acc[...], axis=0, keepdims=True), axis=1, keepdims=True)
        points_here = jnp.float32(0.0)
        for r in range(ROWS):
            points_here += area_ref[space * ROWS + r] * counts_ref[r].astype(F32)
        extra = jnp.where(lane == V, loss_here, extra)
        extra = jnp.where(lane == V + 1, points_here, extra)
        return extra

    def tiles(g):
        first, n = GROUPS[g]
        return first // 8, (first + n) // 8

    def send_part(g, t):
        rows = pl.ds(*GROUPS[g])
        j = lax.rem(q + t, 8)
        return pltpu.make_async_remote_copy(
            src_ref=part.at[j, rows],
            dst_ref=part_in.at[t - 1, rows],
            send_sem=part_send,
            recv_sem=part_recv.at[g],
            device_id=beside(j),
            device_id_type=MESH,
        )

    def send_plane(g, t):
        yy = lax.rem(y + t, 4)
        return pltpu.make_async_remote_copy(
            src_ref=plane.at[yy] if g == 0 else pair,
            dst_ref=y_in.at[g, y],
            send_sem=y_send.at[g],
            recv_sem=y_recv.at[g],
            device_id=at(x, yy, z, core),
            device_id_type=MESH,
        )

    def send_across(g, t):
        return pltpu.make_async_remote_copy(
            src_ref=z_out.at[g],
            dst_ref=z_in.at[g, z],
            send_sem=z_send.at[g],
            recv_sem=z_recv.at[g],
            device_id=at(x, y, lax.rem(z + t, 8), core),
            device_id_type=MESH,
        )

    def send_row(t):
        block = own_all.at[pl.ds(2 * y, 2)]
        return pltpu.make_async_remote_copy(
            src_ref=block,
            dst_ref=block,
            send_sem=row_send,
            recv_sem=row_recv,
            device_id=at(x, lax.rem(y + t, 4), z, core),
            device_id_type=MESH,
        )

    def send_out(g, t):
        first, end = tiles(g)
        block = pl.ds(first, end - first)
        return pltpu.make_async_remote_copy(
            src_ref=own_all.at[block],
            dst_ref=out_in.at[t, block],
            send_sem=out_send,
            recv_sem=out_recv.at[g],
            device_id=beside(lax.rem(q + t, 8)),
            device_id_type=MESH,
        )

    def send_all(send, number):
        for t in range(1, number):
            send(t).start()

    def send_parts(g):
        send_all(lambda t: send_part(g, t), 8)

    def sum_beside(g):
        arrive(part_in.at[:, pl.ds(*GROUPS[g])], part_recv.at[g])

        def column_sum(o):
            at_v = pl.ds(pl.multiple_of(o * 8, 8), 8)
            value = part[q, at_v, :]
            for t in range(7):
                value += part_in[t, at_v, :]
            return value

        if g == 0:

            @pl.loop(0, 4)
            def _(yy):
                for i in range(2):
                    plane[yy, i] = column_sum(2 * yy + i)

            y_in[g, y] = plane[y]
        else:
            for i in range(2):
                pair[i] = column_sum(8 + i)
            y_in[g, y] = pair[...]
        send_all(lambda t: send_plane(g, t), 4)

    def sum_plane(g):
        arrive(y_in.at[g, pl.ds(0, 3)], y_recv.at[g])
        value = y_in[g, 0]
        for yy in range(1, 4):
            value += y_in[g, yy]
        z_out[g] = value
        z_in[g, z] = value
        send_all(lambda t: send_across(g, t), 8)

    def spread_out(g):
        first, end = tiles(g)
        send_all(lambda t: send_out(g, t), 8)
        out_in[0, first:end] = own_all[first:end]

    def sum_across(g):
        arrive(z_in.at[g, pl.ds(0, 7)], z_recv.at[g])
        value = z_in[g, 0]
        for zz in range(1, 8):
            value += z_in[g, zz]
        if g == 0:
            own_all[pl.ds(2 * y, 2)] = value
            send_all(send_row, 4)
        else:
            own_all[8:10] = value
            spread_out(1)

    def collect_rows():
        arrive(own_all.at[pl.ds(0, 6)], row_recv)
        spread_out(0)

    def collect(g):
        first, end = tiles(g)
        arrive(out_in.at[pl.ds(1, 7), pl.ds(first, end - first)], out_recv.at[g])

        @pl.loop(0, 8)
        def _(t):
            cols = pl.ds(pl.multiple_of(lax.rem(q - t + 8, 8) * 128, 128), 128)
            for o in range(first, end):
                sums_ref[o * 8 : (o + 1) * 8, cols] = out_in[t, o]

    def last_copy(phase, to):
        if phase == 1:
            src, dst, device = last_mid, last_z.at[z], stack_device(to)
        else:
            src = last.at[to] if phase == 0 else last_own
            dst = (last_in if phase == 0 else last_out).at[in_plane]
            device = plane_device(to)
        return pltpu.make_async_remote_copy(
            src_ref=src,
            dst_ref=dst,
            send_sem=last_send.at[phase],
            recv_sem=last_recv.at[phase],
            device_id=device,
            device_id_type=MESH,
        )

    def last_sum(phase, source, number):
        arrive(source.at[pl.ds(0, number - 1)], last_recv.at[phase])
        value = source[0]
        for t in range(1, number):
            value += source[t]
        return value

    def last_scatter():
        extra = extras()
        for j in (1, 2, 3, 0):
            piece = weight_sum(LAST, GP - LAST, j * 256)
            for k in range(2):
                block = piece[:, k * 128 : (k + 1) * 128]
                for i in range(12):
                    last[8 * j + 4 * k + i // 3, i % 3] = block[2 * i : 2 * i + 2]
            if j == 0:
                last[3, 1, 0:1, :] = extra
            for p in range(8 * j, 8 * j + 8):

                @pl.when(in_plane != p)
                def _():
                    last_copy(0, p).start()

        last_in[in_plane] = last[in_plane]

    def last_across():
        value = last_sum(0, last_in, 32)
        last_mid[...] = value
        for t in range(1, 8):
            last_copy(1, lax.rem(z + t, 8)).start()
        last_z[z] = value

    def last_gather():
        value = last_sum(1, last_z, 8)
        last_own[...] = value
        for t in range(1, 32):
            last_copy(2, lax.rem(in_plane + t, 32)).start()
        last_out[in_plane] = value

    def last_collect():
        arrive(last_out.at[pl.ds(0, 31)], last_recv.at[2])

        @pl.loop(0, 8)
        def _(j):
            cols = pl.ds(pl.multiple_of(j * 128, 128), 128)
            for i in range(12):
                rows = slice(LAST + 2 * i, LAST + 2 * i + 2)
                sums_ref[rows, cols] = last_out[4 * j + i // 3, i % 3]

    def latent(first, end):
        @pl.loop(first, end)
        def _(b):
            points = block_points(b)
            value = lax.dot_general(
                grad[0:V, points], weight[...], (((0,), (0,)), ((), ())), preferred_element_type=F32
            )
            latent_ref[points, :] = (GRAD_SCALE * value).astype(jnp.bfloat16)

    pairs(0)
    pairs(1)
    misfits()
    pairs(2)
    pairs(3)
    gradient(0)
    gradient(1)
    send_parts(0)
    gradient(2)
    send_parts(1)
    sum_beside(0)
    gradient(3)
    sum_plane(0)
    sum_beside(1)
    last_scatter()
    sum_across(0)
    sum_plane(1)
    latent(0, 2)
    last_across()
    collect_rows()
    sum_across(1)
    latent(2, 4)
    last_gather()
    latent(4, 8)
    collect(0)
    collect(1)
    last_collect()

    arrive(field, fwd_send)
    arrive(signs, ret_send)
    arrive(part.at[pl.ds(0, 7)], part_send)
    arrive(plane.at[pl.ds(0, 3)], y_send.at[0])
    arrive(plane.at[pl.ds(0, 3)], y_send.at[1])
    for g in range(len(GROUPS)):
        arrive(z_in.at[g, pl.ds(0, 7)], z_send.at[g])
    arrive(own_all.at[pl.ds(0, 6)], row_send)
    arrive(out_in.at[pl.ds(0, 7)], out_send)
    for phase, number in enumerate((31, 7, 31)):
        arrive(last.at[pl.ds(0, number)], last_send.at[phase])


def finish_kernel(factor, latent, sums, latent_hbm, wgrad_hbm, bias_ref, loss_ref, wgrad, sem):
    stores = []
    for b in range(4):
        rows = pl.ds(b * CAP, CAP)
        stores.append(pltpu.make_async_copy(latent.at[rows], latent_hbm.at[rows], sem.at[b]))
        stores[-1].start()
    wgrad[...] = sums[0:V, :] * factor
    stores.append(pltpu.make_async_copy(wgrad, wgrad_hbm, sem.at[4]))
    stores[-1].start()
    extra = sums[V : V + 1, 0:128]
    lane = lax.broadcasted_iota(jnp.int32, (1, 128), 1)
    total = jnp.sum(jnp.where(lane == V, extra, 0.0), axis=1, keepdims=True)
    points = jnp.sum(jnp.where(lane == V + 1, extra, 0.0), axis=1, keepdims=True)
    bias_ref[...] = extra[:, 0:V] * factor
    loss_ref[...] = total / (V * (points * (1.0 / NB)))
    for store in stores:
        store.wait()


def per_device(hidden_state, proj_weight, offset, truth, counts, var_weight, total_rows):
    latitude = (np.arange(total_rows) + 0.5) * (LATITUDE_SPAN / total_rows) * (math.pi / 180.0)
    area = jnp.asarray(np.cos(latitude), dtype=F32)
    vmem = pl.BlockSpec(memory_space=pltpu.VMEM)
    smem = pl.BlockSpec(memory_space=pltpu.SMEM)
    hbm = pl.BlockSpec(memory_space=pltpu.HBM)
    dma = pltpu.SemaphoreType.DMA
    bf16 = jnp.bfloat16
    blocks = pltpu.VMEM((NB, NT, 8, 128), F32)
    few_rows = (3, 2, 128)
    latent, sums = pl.pallas_call(
        exchange_kernel,
        out_shape=(
            pltpu.VMEM((POINTS, D), bf16),
            pltpu.VMEM((VP, D), F32),
        ),
        in_specs=[smem, smem, vmem, vmem, hbm, hbm, hbm],
        out_specs=(vmem, vmem),
        scratch_shapes=[
            pltpu.VMEM((V, D), bf16),
            pltpu.VMEM((POINTS, D), bf16),
            pltpu.VMEM((V, ROWS, CAP), F32),
            blocks,
            blocks,
            blocks,
            blocks,
            blocks,
            pltpu.VMEM((GP, POINTS), bf16),
            pltpu.VMEM((8, 128), F32),
            pltpu.VMEM((NT, 8, 128), F32),
            pltpu.VMEM((NT, 8, 128), F32),
            pltpu.VMEM((8, LAST, 128), F32),
            pltpu.VMEM((7, LAST, 128), F32),
            pltpu.VMEM((4, 2, 8, 128), F32),
            pltpu.VMEM((2, 8, 128), F32),
            pltpu.VMEM((2, 4, 2, 8, 128), F32),
            pltpu.VMEM((2, 2, 8, 128), F32),
            pltpu.VMEM((2, 8, 2, 8, 128), F32),
            pltpu.VMEM((LAST // 8, 8, 128), F32),
            pltpu.VMEM((8, LAST // 8, 8, 128), F32),
            pltpu.VMEM((32, *few_rows), F32),
            pltpu.VMEM((32, *few_rows), F32),
            pltpu.VMEM(few_rows, F32),
            pltpu.VMEM((8, *few_rows), F32),
            pltpu.VMEM(few_rows, F32),
            pltpu.VMEM((32, *few_rows), F32),
            dma((NB,)),
            dma((2,)),
            dma,
            dma((NC,)),
            dma,
            dma((NC,)),
            dma,
            dma((2,)),
            dma((2,)),
            dma((2,)),
            dma((2,)),
            dma((2,)),
            dma,
            dma,
            dma,
            dma((2,)),
            dma((3,)),
            dma((3,)),
        ],
        compiler_params=pltpu.CompilerParams(
            collective_id=0, has_side_effects=True, vmem_limit_bytes=59 * 1024 * 1024
        ),
        cost_estimate=pl.CostEstimate(
            flops=6 * V * POINTS * D, bytes_accessed=5_000_000, transcendentals=8_000_000
        ),
    )(
        counts,
        area,
        offset.reshape(1, V),
        var_weight.reshape(1, V),
        proj_weight,
        hidden_state.reshape(POINTS, D),
        truth,
    )
    factor = GRAD_SCALE / math.sqrt(NB * total_rows * CAP)
    latent, wgrad, bias, loss = pl.pallas_call(
        lambda *refs: finish_kernel(factor, *refs),
        out_shape=(
            jax.ShapeDtypeStruct((POINTS, D), bf16),
            jax.ShapeDtypeStruct((V, D), F32),
            jax.ShapeDtypeStruct((1, V), F32),
            jax.ShapeDtypeStruct((1, 1), F32),
        ),
        in_specs=[vmem, vmem],
        out_specs=(hbm, hbm, vmem, vmem),
        scratch_shapes=[pltpu.VMEM((V, D), F32), dma((5,))],
        compiler_params=pltpu.CompilerParams(vmem_limit_bytes=16 * 1024 * 1024),
        cost_estimate=pl.CostEstimate(flops=V * D, bytes_accessed=5_000_000, transcendentals=0),
    )(latent, sums)
    return latent.reshape(hidden_state.shape), wgrad, bias.reshape(V), loss.reshape(())


def solution(mesh):
    total_rows = ROWS * mesh.shape["space"]

    def step(*args):
        return per_device(*args, total_rows)

    return jax.shard_map(
        step,
        mesh=mesh,
        in_specs=(
            P("member", "space", None, None),
            P(),
            P(),
            P(None, "space", None),
            P("space"),
            P(),
        ),
        out_specs=(P("member", "space", None, None), P(), P(), P()),
        check_vma=False,
    )
```

```python
import math

import numpy as np

import jax
import jax.numpy as jnp
from jax import lax
from jax.experimental import pallas as pl
from jax.experimental.pallas import tpu as pltpu
from jax.sharding import PartitionSpec as P

SMOOTHING = 0.05
FAIRNESS = 0.95
GRAD_SCALE = 16.0
LATITUDE_SPAN = 80.0

V = 100
VP = 104
GP = 112
D = 1024
ROWS = 4
CAP = 512
POINTS = ROWS * CAP
BLOCK = 256
NB = 8
NT = 25
CHUNKS = ((0, 8), (8, 8), (16, 4), (20, 5))
NC = len(CHUNKS)
GROUPS = ((0, 64), (64, 16))
LAST = 80
MESH = pl.DeviceIdType.MESH
F32 = jnp.float32
EPS2 = SMOOTHING * SMOOTHING
COEFF = FAIRNESS / (NB * (NB - 1)) + (1.0 - FAIRNESS) / (NB * NB)


def column(row):
    n = row.shape[1]
    here = lax.broadcasted_iota(jnp.int32, (VP, n), 0) == lax.broadcasted_iota(
        jnp.int32, (VP, n), 1
    )
    return jnp.sum(jnp.where(here, jnp.broadcast_to(row, (VP, n)), 0.0), axis=1, keepdims=True)


def exchange_kernel(
    counts_ref,
    area_ref,
    offset_ref,
    scale_ref,
    weight_hbm,
    hidden_hbm,
    truth_hbm,
    latent_ref,
    sums_ref,
    weight,
    hbuf,
    truth,
    field,
    met,
    signs,
    back,
    obs,
    grad,
    loss_acc,
    bias_acc,
    scale,
    part,
    part_in,
    plane,
    pair,
    y_in,
    z_out,
    z_in,
    own_all,
    out_in,
    last,
    last_in,
    last_mid,
    last_z,
    last_own,
    last_out,
    load_sem,
    side_sem,
    fwd_send,
    fwd_recv,
    ret_send,
    ret_recv,
    part_send,
    part_recv,
    y_send,
    y_recv,
    z_send,
    z_recv,
    row_send,
    row_recv,
    out_send,
    out_recv,
    last_send,
    last_recv,
):
    member = lax.axis_index("member")
    space = lax.axis_index("space")
    y, z_hi = lax.div(member, 2), lax.rem(member, 2)
    z_lo, q = lax.div(space, 8), lax.rem(space, 8)
    x, core = lax.div(q, 2), lax.rem(q, 2)
    z = z_hi * 4 + z_lo
    in_plane = (x * 4 + y) * 2 + core

    def at(xx, yy, zz, cc):
        return (yy * 2 + lax.div(zz, 4), lax.rem(zz, 4) * 8 + xx * 2 + cc)

    def beside(j):
        return at(lax.div(j, 2), y, z, lax.rem(j, 2))

    def plane_device(w):
        return at(lax.div(w, 8), lax.rem(lax.div(w, 2), 4), z, lax.rem(w, 2))

    def stack_device(zz):
        return at(x, y, zz, core)

    def block_points(b):
        return pl.ds(pl.multiple_of(b * BLOCK, BLOCK), BLOCK)

    def load(t):
        rows = block_points(lax.rem(member + t, NB))
        return pltpu.make_async_copy(hidden_hbm.at[rows], hbuf.at[rows], load_sem.at[t - 1])

    load_weight = pltpu.make_async_copy(weight_hbm, weight, side_sem.at[0])
    load_weight.start()
    for t in range(1, NB + 1):
        load(t).start()
    load_truth = pltpu.make_async_copy(truth_hbm, truth, side_sem.at[1])
    load_truth.start()

    barrier = pltpu.get_barrier_semaphore()

    def greet(device):
        pl.semaphore_signal(barrier, inc=1, device_id=device, device_id_type=MESH)

    for t in range(1, 32):
        greet(plane_device(lax.rem(in_plane + t, 32)))
    for t in range(1, 8):
        greet(stack_device(lax.rem(z + t, 8)))
    for t in range(1, 4):
        greet(at(x, lax.rem(y + t, 4), lax.rem(z + 2, 8), core))
        greet(at(x, lax.rem(y + t, 4), lax.rem(z + 6, 8), core))

    offsets = column(offset_ref[...])[0:V]
    scales = jnp.broadcast_to(column(scale_ref[...]), (VP, 128))
    for i in range(NT // 2):
        scale[2 * i] = scales[8 * i : 8 * i + 8]
        scale[2 * i + 1] = scales[8 * i : 8 * i + 8]
    scale[NT - 1] = jnp.concatenate([scales[96:V], scales[96:V]], axis=0)
    loss_acc[...] = jnp.zeros_like(loss_acc)
    bias_acc[...] = jnp.zeros_like(bias_acc)

    lane = lax.broadcasted_iota(jnp.int32, (1, 128), 1)
    sub = lax.broadcasted_iota(jnp.int32, (8, 128), 0)

    def live(b, h):
        return lane + (lax.rem(b, 2) * 2 + h) * 128 < counts_ref[lax.div(b, 2)]

    def point_weights(b, factor):
        area = area_ref[space * ROWS + lax.div(b, 2)] * factor
        halves = [jnp.where(live(b, h), area, 0.0) for h in range(2)]
        return halves, jnp.where(sub < 4, halves[0], halves[1])

    def send_forecast(c, b):
        block = pl.ds(*CHUNKS[c])
        return pltpu.make_async_remote_copy(
            src_ref=field.at[b, block],
            dst_ref=met.at[member, block],
            send_sem=fwd_send,
            recv_sem=fwd_recv.at[c],
            device_id=at(x, lax.div(b, 2), lax.rem(z_lo + 2 + 4 * lax.rem(b, 2), 8), core),
            device_id_type=MESH,
        )

    for t in range(1, NB + 1):
        load(t).wait()
        if t == 1:
            load_weight.wait()
        b = lax.rem(member + t, NB)
        product = lax.dot_general(
            weight[...],
            hbuf[block_points(b), :],
            (((1,), (1,)), ((), ())),
            preferred_element_type=F32,
        )
        forecast = product + offsets
        halves = [
            jnp.where(live(b, h), forecast[:, h * 128 : (h + 1) * 128], 0.0) for h in range(2)
        ]
        for i in range(NT // 2):
            for h in range(2):
                field[b, 2 * i + h] = halves[h][8 * i : 8 * i + 8]
        field[b, NT - 1] = jnp.concatenate([halves[0][96:V], halves[1][96:V]], axis=0)
        if t == 1:
            pl.semaphore_wait(barrier, 44)
        for c in range(2):
            send_forecast(c, b).start()
    for c in range(2, NC):
        for t in range(1, NB + 1):
            send_forecast(c, lax.rem(member + t, NB)).start()

    def misfit(b, tile, target, weight_here):
        gap = field[b, tile] - target
        square = gap * gap + EPS2
        inverse = lax.rsqrt(square)
        factor = weight_here * scale[tile]
        obs[b, tile] = factor * (gap * inverse)
        return factor * (square * inverse - SMOOTHING)

    def target(b, v, h):
        first = (b % 2) * BLOCK + h * 128
        return truth[v, b // 2, first : first + 128]

    def misfits():
        load_truth.wait()

        @pl.loop(0, NT // 2)
        def _(i):
            at_v = pl.ds(pl.multiple_of(i * 8, 8), 8)
            total = jnp.zeros((8, 128), F32)
            for b in range(NB):
                halves, _ = point_weights(b, 1.0 / NB)
                for h in range(2):
                    total += misfit(b, 2 * i + h, target(b, at_v, h), halves[h])
            loss_acc[...] += total

        total = jnp.zeros((8, 128), F32)
        for b in range(NB):
            _, both = point_weights(b, 1.0 / NB)
            tail = pl.ds(96, 4)
            goal = jnp.concatenate([target(b, tail, 0), target(b, tail, 1)], axis=0)
            total += misfit(b, NT - 1, goal, both)
        loss_acc[...] += total

    z_from = lax.rem(z + 2, 4)
    block_here = y * 2 + lax.div(lax.rem(z - z_from - 2 + 16, 8), 4)
    space_from = z_from * 8 + q
    area_here = area_ref[space_from * ROWS + y]

    def send_sign(c, m):
        block = pl.ds(*CHUNKS[c])
        return pltpu.make_async_remote_copy(
            src_ref=signs.at[m, block],
            dst_ref=back.at[block_here, block],
            send_sem=ret_send,
            recv_sem=ret_recv.at[c],
            device_id=(m, space_from),
            device_id_type=MESH,
        )

    def arrive(ref, sem):
        pltpu.make_async_copy(ref, ref, sem).wait()

    def meet(block):
        values = [met[m, block] for m in range(NB)]
        sums = [None] * NB
        roots = None
        for m in range(NB):
            for k in range(m + 1, NB):
                gap = values[m] - values[k]
                square = gap * gap + EPS2
                inverse = lax.rsqrt(square)
                sign = gap * inverse
                root = square * inverse
                roots = root if roots is None else roots + root
                sums[m] = sign if sums[m] is None else sums[m] + sign
                sums[k] = -sign if sums[k] is None else sums[k] - sign
        for m in range(NB):
            signs[m, block] = sums[m]
        spread = (roots - (NB * (NB - 1) // 2) * SMOOTHING) * scale[block]
        loss_acc[...] += (-COEFF * area_here) * jnp.sum(spread, axis=0)

    def pairs(c):
        first, n = CHUNKS[c]
        arrive(met.at[:, pl.ds(first, n)], fwd_recv.at[c])

        @pl.loop(0, n // 2)
        def _(i):
            meet(pl.ds(first + 2 * i, 2))

        if n % 2:
            meet(pl.ds(first + n - 1, 1))

        for t in range(1, NB + 1):
            send_sign(c, lax.rem(member + t, NB)).start()

    def weight_sum(v0, rows, first):
        return jnp.dot(
            grad[v0 : v0 + rows, :], hbuf[:, pl.ds(first, 256)], preferred_element_type=F32
        )

    def gradient(c):
        first, n = CHUNKS[c]
        v0 = 4 * first
        arrive(back.at[:, pl.ds(first, n)], ret_recv.at[c])

        @pl.loop(0, NB)
        def _(b):
            halves, both = point_weights(b, COEFF)

            def value(tile, weight_here):
                result = obs[b, tile] - (weight_here * scale[tile]) * back[b, tile]
                bias_acc[tile] += result
                return result

            pieces = [
                [value(first + 2 * i + h, halves[h]) for i in range(n // 2)] for h in range(2)
            ]
            if n % 2:
                tail = value(NT - 1, both)
                for h in range(2):
                    pieces[h] += [tail[4 * h : 4 * h + 4], jnp.zeros((GP - V, 128), F32)]
            for h in range(2):
                stacked = jnp.concatenate(pieces[h], axis=0)
                points = pl.ds(pl.multiple_of(b * BLOCK + h * 128, 128), 128)
                grad[v0 : v0 + stacked.shape[0], points] = stacked.astype(jnp.bfloat16)

        if n % 2:
            return

        @pl.loop(0, 4)
        def _(j):
            piece = weight_sum(v0, 4 * n, pl.multiple_of(j * 256, 256))
            for k in range(2):
                part[2 * j + k, v0 : v0 + 4 * n, :] = piece[:, k * 128 : (k + 1) * 128]

    def extras():
        rows = []
        for i in range(NT // 2):
            rows.append(bias_acc[2 * i] + bias_acc[2 * i + 1])
        tail = bias_acc[NT - 1]
        rows += [tail[0:4] + tail[4:8], jnp.zeros((VP - V, 128), F32)]
        bias = jnp.sum(jnp.concatenate(rows, axis=0), axis=1, keepdims=True)
        eye = lax.broadcasted_iota(jnp.int32, (VP, 128), 0) == lax.broadcasted_iota(
            jnp.int32, (VP, 128), 1
        )
        extra = jnp.sum(jnp.where(eye, bias, 0.0), axis=0, keepdims=True)
        loss_here = jnp.sum(jnp.sum(loss_acc[...], axis=0, keepdims=True), axis=1, keepdims=True)
        points_here = jnp.float32(0.0)
        for r in range(ROWS):
            points_here += area_ref[space * ROWS + r] * counts_ref[r].astype(F32)
        extra = jnp.where(lane == V, loss_here, extra)
        extra = jnp.where(lane == V + 1, points_here, extra)
        return extra

    def tiles(g):
        first, n = GROUPS[g]
        return first // 8, (first + n) // 8

    def send_part(g, t):
        rows = pl.ds(*GROUPS[g])
        j = lax.rem(q + t, 8)
        return pltpu.make_async_remote_copy(
            src_ref=part.at[j, rows],
            dst_ref=part_in.at[t - 1, rows],
            send_sem=part_send,
            recv_sem=part_recv.at[g],
            device_id=beside(j),
            device_id_type=MESH,
        )

    def send_plane(g, t):
        yy = lax.rem(y + t, 4)
        return pltpu.make_async_remote_copy(
            src_ref=plane.at[yy] if g == 0 else pair,
            dst_ref=y_in.at[g, y],
            send_sem=y_send.at[g],
            recv_sem=y_recv.at[g],
            device_id=at(x, yy, z, core),
            device_id_type=MESH,
        )

    def send_across(g, t):
        return pltpu.make_async_remote_copy(
            src_ref=z_out.at[g],
            dst_ref=z_in.at[g, z],
            send_sem=z_send.at[g],
            recv_sem=z_recv.at[g],
            device_id=at(x, y, lax.rem(z + t, 8), core),
            device_id_type=MESH,
        )

    def send_row(t):
        block = own_all.at[pl.ds(2 * y, 2)]
        return pltpu.make_async_remote_copy(
            src_ref=block,
            dst_ref=block,
            send_sem=row_send,
            recv_sem=row_recv,
            device_id=at(x, lax.rem(y + t, 4), z, core),
            device_id_type=MESH,
        )

    def send_out(g, t):
        first, end = tiles(g)
        block = pl.ds(first, end - first)
        return pltpu.make_async_remote_copy(
            src_ref=own_all.at[block],
            dst_ref=out_in.at[t, block],
            send_sem=out_send,
            recv_sem=out_recv.at[g],
            device_id=beside(lax.rem(q + t, 8)),
            device_id_type=MESH,
        )

    def send_all(send, number):
        for t in range(1, number):
            send(t).start()

    def send_parts(g):
        send_all(lambda t: send_part(g, t), 8)

    def sum_beside(g):
        arrive(part_in.at[:, pl.ds(*GROUPS[g])], part_recv.at[g])

        def column_sum(o):
            at_v = pl.ds(pl.multiple_of(o * 8, 8), 8)
            value = part[q, at_v, :]
            for t in range(7):
                value += part_in[t, at_v, :]
            return value

        if g == 0:

            @pl.loop(0, 4)
            def _(yy):
                for i in range(2):
                    plane[yy, i] = column_sum(2 * yy + i)

            y_in[g, y] = plane[y]
        else:
            for i in range(2):
                pair[i] = column_sum(8 + i)
            y_in[g, y] = pair[...]
        send_all(lambda t: send_plane(g, t), 4)

    def sum_plane(g):
        arrive(y_in.at[g, pl.ds(0, 3)], y_recv.at[g])
        value = y_in[g, 0]
        for yy in range(1, 4):
            value += y_in[g, yy]
        z_out[g] = value
        z_in[g, z] = value
        send_all(lambda t: send_across(g, t), 8)

    def spread_out(g):
        first, end = tiles(g)
        send_all(lambda t: send_out(g, t), 8)
        out_in[0, first:end] = own_all[first:end]

    def sum_across(g):
        arrive(z_in.at[g, pl.ds(0, 7)], z_recv.at[g])
        value = z_in[g, 0]
        for zz in range(1, 8):
            value += z_in[g, zz]
        if g == 0:
            own_all[pl.ds(2 * y, 2)] = value
            send_all(send_row, 4)
        else:
            own_all[8:10] = value
            spread_out(1)

    def collect_rows():
        arrive(own_all.at[pl.ds(0, 6)], row_recv)
        spread_out(0)

    def collect(g):
        first, end = tiles(g)
        arrive(out_in.at[pl.ds(1, 7), pl.ds(first, end - first)], out_recv.at[g])

        @pl.loop(0, 8)
        def _(t):
            cols = pl.ds(pl.multiple_of(lax.rem(q - t + 8, 8) * 128, 128), 128)
            for o in range(first, end):
                sums_ref[o * 8 : (o + 1) * 8, cols] = out_in[t, o]

    def last_copy(phase, to):
        if phase == 1:
            src, dst, device = last_mid, last_z.at[z], stack_device(to)
        else:
            src = last.at[to] if phase == 0 else last_own
            dst = (last_in if phase == 0 else last_out).at[in_plane]
            device = plane_device(to)
        return pltpu.make_async_remote_copy(
            src_ref=src,
            dst_ref=dst,
            send_sem=last_send.at[phase],
            recv_sem=last_recv.at[phase],
            device_id=device,
            device_id_type=MESH,
        )

    def last_sum(phase, source, number):
        arrive(source.at[pl.ds(0, number - 1)], last_recv.at[phase])
        value = source[0]
        for t in range(1, number):
            value += source[t]
        return value

    def last_scatter():
        extra = extras()
        for j in (1, 2, 3, 0):
            piece = weight_sum(LAST, GP - LAST, j * 256)
            for k in range(2):
                block = piece[:, k * 128 : (k + 1) * 128]
                for i in range(12):
                    last[8 * j + 4 * k + i // 3, i % 3] = block[2 * i : 2 * i + 2]
            if j == 0:
                last[3, 1, 0:1, :] = extra
            for p in range(8 * j, 8 * j + 8):

                @pl.when(in_plane != p)
                def _():
                    last_copy(0, p).start()

        last_in[in_plane] = last[in_plane]

    def last_across():
        value = last_sum(0, last_in, 32)
        last_mid[...] = value
        for t in range(1, 8):
            last_copy(1, lax.rem(z + t, 8)).start()
        last_z[z] = value

    def last_gather():
        value = last_sum(1, last_z, 8)
        last_own[...] = value
        for t in range(1, 32):
            last_copy(2, lax.rem(in_plane + t, 32)).start()
        last_out[in_plane] = value

    def last_collect():
        arrive(last_out.at[pl.ds(0, 31)], last_recv.at[2])

        @pl.loop(0, 8)
        def _(j):
            cols = pl.ds(pl.multiple_of(j * 128, 128), 128)
            for i in range(12):
                rows = slice(LAST + 2 * i, LAST + 2 * i + 2)
                sums_ref[rows, cols] = last_out[4 * j + i // 3, i % 3]

    def latent(first, end):
        @pl.loop(first, end)
        def _(b):
            points = block_points(b)
            value = lax.dot_general(
                grad[0:V, points], weight[...], (((0,), (0,)), ((), ())), preferred_element_type=F32
            )
            latent_ref[points, :] = (GRAD_SCALE * value).astype(jnp.bfloat16)

    pairs(0)
    pairs(1)
    misfits()
    pairs(2)
    pairs(3)
    gradient(0)
    gradient(1)
    send_parts(0)
    gradient(2)
    send_parts(1)
    gradient(3)
    sum_beside(0)
    last_scatter()
    sum_plane(0)
    sum_beside(1)
    latent(0, 2)
    last_across()
    sum_across(0)
    sum_plane(1)
    latent(2, 4)
    last_gather()
    collect_rows()
    sum_across(1)
    latent(4, 8)
    last_collect()
    collect(0)
    collect(1)

    arrive(field, fwd_send)
    arrive(signs, ret_send)
    arrive(part.at[pl.ds(0, 7)], part_send)
    arrive(plane.at[pl.ds(0, 3)], y_send.at[0])
    arrive(plane.at[pl.ds(0, 3)], y_send.at[1])
    for g in range(len(GROUPS)):
        arrive(z_in.at[g, pl.ds(0, 7)], z_send.at[g])
    arrive(own_all.at[pl.ds(0, 6)], row_send)
    arrive(out_in.at[pl.ds(0, 7)], out_send)
    for phase, number in enumerate((31, 7, 31)):
        arrive(last.at[pl.ds(0, number)], last_send.at[phase])


def finish_kernel(factor, latent, sums, latent_hbm, wgrad_hbm, bias_ref, loss_ref, wgrad, sem):
    stores = []
    for b in range(4):
        rows = pl.ds(b * CAP, CAP)
        stores.append(pltpu.make_async_copy(latent.at[rows], latent_hbm.at[rows], sem.at[b]))
        stores[-1].start()
    wgrad[...] = sums[0:V, :] * factor
    stores.append(pltpu.make_async_copy(wgrad, wgrad_hbm, sem.at[4]))
    stores[-1].start()
    extra = sums[V : V + 1, 0:128]
    lane = lax.broadcasted_iota(jnp.int32, (1, 128), 1)
    total = jnp.sum(jnp.where(lane == V, extra, 0.0), axis=1, keepdims=True)
    points = jnp.sum(jnp.where(lane == V + 1, extra, 0.0), axis=1, keepdims=True)
    bias_ref[...] = extra[:, 0:V] * factor
    loss_ref[...] = total / (V * (points * (1.0 / NB)))
    for store in stores:
        store.wait()


def per_device(hidden_state, proj_weight, offset, truth, counts, var_weight, total_rows):
    latitude = (np.arange(total_rows) + 0.5) * (LATITUDE_SPAN / total_rows) * (math.pi / 180.0)
    area = jnp.asarray(np.cos(latitude), dtype=F32)
    vmem = pl.BlockSpec(memory_space=pltpu.VMEM)
    smem = pl.BlockSpec(memory_space=pltpu.SMEM)
    hbm = pl.BlockSpec(memory_space=pltpu.HBM)
    dma = pltpu.SemaphoreType.DMA
    bf16 = jnp.bfloat16
    blocks = pltpu.VMEM((NB, NT, 8, 128), F32)
    few_rows = (3, 2, 128)
    latent, sums = pl.pallas_call(
        exchange_kernel,
        out_shape=(
            pltpu.VMEM((POINTS, D), bf16),
            pltpu.VMEM((VP, D), F32),
        ),
        in_specs=[smem, smem, vmem, vmem, hbm, hbm, hbm],
        out_specs=(vmem, vmem),
        scratch_shapes=[
            pltpu.VMEM((V, D), bf16),
            pltpu.VMEM((POINTS, D), bf16),
            pltpu.VMEM((V, ROWS, CAP), F32),
            blocks,
            blocks,
            blocks,
            blocks,
            blocks,
            pltpu.VMEM((GP, POINTS), bf16),
            pltpu.VMEM((8, 128), F32),
            pltpu.VMEM((NT, 8, 128), F32),
            pltpu.VMEM((NT, 8, 128), F32),
            pltpu.VMEM((8, LAST, 128), F32),
            pltpu.VMEM((7, LAST, 128), F32),
            pltpu.VMEM((4, 2, 8, 128), F32),
            pltpu.VMEM((2, 8, 128), F32),
            pltpu.VMEM((2, 4, 2, 8, 128), F32),
            pltpu.VMEM((2, 2, 8, 128), F32),
            pltpu.VMEM((2, 8, 2, 8, 128), F32),
            pltpu.VMEM((LAST // 8, 8, 128), F32),
            pltpu.VMEM((8, LAST // 8, 8, 128), F32),
            pltpu.VMEM((32, *few_rows), F32),
            pltpu.VMEM((32, *few_rows), F32),
            pltpu.VMEM(few_rows, F32),
            pltpu.VMEM((8, *few_rows), F32),
            pltpu.VMEM(few_rows, F32),
            pltpu.VMEM((32, *few_rows), F32),
            dma((NB,)),
            dma((2,)),
            dma,
            dma((NC,)),
            dma,
            dma((NC,)),
            dma,
            dma((2,)),
            dma((2,)),
            dma((2,)),
            dma((2,)),
            dma((2,)),
            dma,
            dma,
            dma,
            dma((2,)),
            dma((3,)),
            dma((3,)),
        ],
        compiler_params=pltpu.CompilerParams(
            collective_id=0, has_side_effects=True, vmem_limit_bytes=59 * 1024 * 1024
        ),
        cost_estimate=pl.CostEstimate(
            flops=6 * V * POINTS * D, bytes_accessed=5_000_000, transcendentals=8_000_000
        ),
    )(
        counts,
        area,
        offset.reshape(1, V),
        var_weight.reshape(1, V),
        proj_weight,
        hidden_state.reshape(POINTS, D),
        truth,
    )
    factor = GRAD_SCALE / math.sqrt(NB * total_rows * CAP)
    latent, wgrad, bias, loss = pl.pallas_call(
        lambda *refs: finish_kernel(factor, *refs),
        out_shape=(
            jax.ShapeDtypeStruct((POINTS, D), bf16),
            jax.ShapeDtypeStruct((V, D), F32),
            jax.ShapeDtypeStruct((1, V), F32),
            jax.ShapeDtypeStruct((1, 1), F32),
        ),
        in_specs=[vmem, vmem],
        out_specs=(hbm, hbm, vmem, vmem),
        scratch_shapes=[pltpu.VMEM((V, D), F32), dma((5,))],
        compiler_params=pltpu.CompilerParams(vmem_limit_bytes=16 * 1024 * 1024),
        cost_estimate=pl.CostEstimate(flops=V * D, bytes_accessed=5_000_000, transcendentals=0),
    )(latent, sums)
    return latent.reshape(hidden_state.shape), wgrad, bias.reshape(V), loss.reshape(())


def solution(mesh):
    total_rows = ROWS * mesh.shape["space"]

    def step(*args):
        return per_device(*args, total_rows)

    return jax.shard_map(
        step,
        mesh=mesh,
        in_specs=(
            P("member", "space", None, None),
            P(),
            P(),
            P(None, "space", None),
            P("space"),
            P(),
        ),
        out_specs=(P("member", "space", None, None), P(), P(), P()),
        check_vma=False,
    )
```
